256 devices in a mesh: stripe: 32 (over x_hi, z, core), tile: 8 (over x_lo, y).
Axes of the slice: x: 4 (x_hi: 2, x_lo: 2; x = x_hi * 2 + x_lo), y: 4, z: 8, core: 2. Of those that a mesh axis runs over, the one named last changes fastest.
Arguments:
- shot_blocks: bfloat16 [16384, 128, 128], P(('stripe', 'tile')), may hold values from 0.049804688 to 1
- shot_dose: float32 [16384], P(('stripe', 'tile')), may hold values from 0.5 to 1.5
- shot_tile: int32 [16384], P(('stripe', 'tile')), may hold values from 0 to 31
- shot_count: int32 [2048], P(('stripe', 'tile')), may hold values from 1 to 8, as said below
Outputs:
- energy: float32 [8192, 16384], P('tile', 'stripe')
- backscatter: float32 [64, 128], P('tile', 'stripe')
- new_dose: float32 [16384], P(('stripe', 'tile'))
The draws below stay inside these ranges and needn't reach their ends.
Inputs may be any that keep to these rules, and one draw needn't show every extreme that they name: `shot_count`: entry (a * 8 + b) * 8 + d counts the live blocks in bucket d of device (a, b); they fill the first slots of the bucket.
All inputs are finite; a program needn't handle non-finite values.
Results may differ from the reference program's by a relative error of at most 0.007.
Values may be sent and summed in bfloat16 or wider, within the bound.
No kernel may reach another device: no remote copies, remote signals or barrier semaphores. Data moves between devices by JAX's collectives and lax.ppermute only.
A program may use at most 64 MiB of HBM per device.

```python
import jax
import jax.numpy as jnp
from jax import lax

TILE = 128
TR = 8
TC = 4
HALO = 16
SLOTS_DEV = 64
CAP = 8
SLOTS = 16384
NY = 8192
NX = 16384
NYC = 64
NXC = 128
N_STRIPE = 32
N_TILE = 8


def draw_shot_count(key, part):
    key = jax.random.fold_in(key, 11)
    hot_key, base_key = jax.random.split(key)
    hottest = jax.random.randint(hot_key, (N_STRIPE, 1, 1), 0, N_TILE)
    lowest = max(1, CAP // 4)
    highest = max(lowest + 1, CAP // 2 + 1)
    base = jax.random.randint(base_key, (N_STRIPE, N_TILE, N_TILE), lowest, highest)
    target_dev = lax.broadcasted_iota(jnp.int32, (N_STRIPE, N_TILE, N_TILE), 2)
    return jnp.where(target_dev == hottest, CAP, base).reshape(-1).astype(jnp.int32)


def place_ends(drawn, stream_key, low, top_value):
    longest = drawn.shape.index(max(drawn.shape))
    spots = []
    for shift in (0, 1):
        where = [jax.random.randint(jax.random.fold_in(stream_key, axis), (), 0, length) for axis, length in enumerate(drawn.shape)]
        where[longest] = (where[longest] + shift) % drawn.shape[longest]
        spots.append(tuple(where))
    return drawn.at[spots[0]].set(low).at[spots[1]].set(top_value)


def block_levels(stream_key, shape, cuts, low, top_value):
    level = 1.0
    for axis_at, parts in cuts:
        heights = jax.random.uniform(jax.random.fold_in(jax.random.fold_in(stream_key, 6), axis_at), (parts,), jnp.float32, low / len(cuts), top_value / len(cuts))
        level = level * jnp.repeat(jnp.exp(heights), shape[axis_at] // parts).reshape((-1,) + (1,) * (len(shape) - 1 - axis_at))
    return level


def setup_inputs(seed: int = 0) -> dict:
    streams_of = jax.random.split(jax.random.key(seed), 5)
    shot_blocks = jnp.clip(0.049804688 + 0.9501953 * jax.random.uniform(streams_of[0], (SLOTS, TILE, TILE), jnp.float32) ** block_levels(streams_of[0], (SLOTS, TILE, TILE), ((0, 256),), -0.2, 0.2), 0.049804688, 1.0).astype(jnp.bfloat16)
    shot_dose = jnp.clip(0.5 + 1.0 * jax.random.uniform(streams_of[1], (SLOTS,), jnp.float32) ** block_levels(streams_of[1], (SLOTS,), ((0, 256),), -0.2, 0.2), 0.5, 1.5)
    shot_tile = place_ends(jax.random.randint(streams_of[2], (SLOTS,), 0, TR * TC), jax.random.fold_in(streams_of[2], 1), 0, (TR * TC) - 1).astype(jnp.int32)
    shot_count = draw_shot_count(jax.random.fold_in(streams_of[4], 71), 0)
    return dict(shot_blocks=shot_blocks, shot_dose=shot_dose, shot_tile=shot_tile, shot_count=shot_count)


ETA_BACK = 0.7
DILATED_WEIGHT = 0.5
TARGET_DOSE = 1.0
NARROW_SIGMA = 2.0
DILATED_SIGMA = 4.0
SPREAD_DIVISOR = 5.0
LOOP_DIVISOR = 2.0


def kernel_taps(offset):
    offset = offset.astype(jnp.int32)
    inside = jnp.abs(offset) <= HALO
    offset_f = offset.astype(jnp.float32)
    narrow = jnp.where(inside, jnp.exp(-offset_f * offset_f / (2.0 * NARROW_SIGMA * NARROW_SIGMA)), jnp.float32(0.0))
    even_tap = inside & (offset % 2 == 0)
    dilated = jnp.where(even_tap, jnp.exp(-offset_f * offset_f / (8.0 * DILATED_SIGMA * DILATED_SIGMA)), jnp.float32(0.0))
    return narrow, dilated


def loop_weight(source_idx, target_idx, loop_len, spread):
    distance_raw = jnp.abs(source_idx - target_idx)
    distance = jnp.minimum(distance_raw, loop_len - distance_raw).astype(jnp.float32)
    return jnp.exp(-distance * distance / (2.0 * spread * spread))


def gauss_weight(source_idx, target_idx, spread):
    distance = (source_idx - target_idx).astype(jnp.float32)
    return jnp.exp(-distance * distance / (2.0 * spread * spread))


def tap_tables():
    offsets = jnp.arange(-HALO, HALO + 1, dtype=jnp.int32)
    narrow, dilated = kernel_taps(offsets)
    narrow_low = (narrow / jnp.sum(narrow)).astype(jnp.bfloat16)
    dilated_low = (dilated / jnp.sum(dilated)).astype(jnp.bfloat16)
    narrow_low, dilated_low = lax.optimization_barrier((narrow_low, dilated_low))
    return narrow_low.astype(jnp.float32), dilated_low.astype(jnp.float32)


def rows_pass(field, taps):
    height = field.shape[0]
    padded = jnp.pad(field.astype(jnp.float32), ((HALO, HALO), (0, 0)))
    running = jnp.zeros(field.shape, jnp.float32)
    for shift_at in range(2 * HALO + 1):
        running = running + taps[shift_at] * padded[shift_at:shift_at + height]
    return running


def cols_pass(field, taps):
    width = field.shape[1]
    wide = field.astype(jnp.float32)
    padded = jnp.concatenate([wide[:, width - HALO:], wide, wide[:, :HALO]], axis=1)
    running = jnp.zeros(field.shape, jnp.float32)
    for shift_at in range(2 * HALO + 1):
        running = running + taps[shift_at] * padded[:, shift_at:shift_at + width]
    return running


def reference(shot_blocks, shot_dose, shot_tile, shot_count):
    tile_count = TR * TC
    blocks = shot_blocks.reshape(N_STRIPE, N_TILE, N_TILE, CAP, TILE * TILE)
    position = lax.broadcasted_iota(jnp.int32, (N_STRIPE, N_TILE, N_TILE, CAP), 3)
    is_live = position < shot_count.reshape(N_STRIPE, N_TILE, N_TILE, 1)
    dose_live = jnp.where(is_live, shot_dose.reshape(N_STRIPE, N_TILE, N_TILE, CAP), jnp.float32(0.0))
    tile_ids = shot_tile.reshape(N_STRIPE, N_TILE, N_TILE, CAP)
    devices = jnp.arange(N_STRIPE * N_TILE, dtype=jnp.int32)

    def arrived(device):
        segment = device // N_TILE
        target_dev = device % N_TILE
        got_blocks = blocks[segment, :, target_dev].reshape(SLOTS_DEV, TILE * TILE)
        got_dose = dose_live[segment, :, target_dev].reshape(SLOTS_DEV)
        got_tiles = tile_ids[segment, :, target_dev].reshape(SLOTS_DEV)
        return got_blocks, got_dose, got_tiles

    def deposit(device):
        got_blocks, got_dose, got_tiles = arrived(device)
        owners = lax.broadcasted_iota(jnp.int32, (tile_count, SLOTS_DEV), 0)
        weights = jnp.where(owners == got_tiles[None, :], got_dose[None, :], jnp.float32(0.0)).astype(jnp.bfloat16)
        return jnp.dot(weights, got_blocks, preferred_element_type=jnp.float32)

    deposits = lax.map(deposit, devices)
    pattern = deposits.reshape(N_STRIPE, N_TILE, TR, TC, TILE, TILE).transpose(1, 2, 4, 0, 3, 5).reshape(NY, NX)

    narrow_taps, dilated_taps = tap_tables()
    pattern_low = pattern.astype(jnp.bfloat16)
    narrow_rows = rows_pass(pattern_low, narrow_taps).astype(jnp.bfloat16)
    dilated_rows = rows_pass(pattern_low, dilated_taps).astype(jnp.bfloat16)
    forward = cols_pass(narrow_rows, narrow_taps) + DILATED_WEIGHT * cols_pass(dilated_rows, dilated_taps)

    coarse = pattern.reshape(NYC, TILE, NXC, TILE).mean(axis=(1, 3))
    loop_spread = NXC / LOOP_DIVISOR
    band_spread = NYC / SPREAD_DIVISOR
    loop_axis = jnp.arange(NXC, dtype=jnp.int32)
    loop_matrix = loop_weight(loop_axis[:, None], loop_axis[None, :], NXC, loop_spread)
    loop_total = jnp.sum(loop_weight(loop_axis, jnp.zeros_like(loop_axis), NXC, loop_spread))
    band_axis = jnp.arange(NYC, dtype=jnp.int32)
    band_matrix = gauss_weight(band_axis[:, None], band_axis[None, :], band_spread)
    band_offsets = jnp.arange(-(NYC - 1), NYC, dtype=jnp.int32)
    band_total = jnp.sum(gauss_weight(band_offsets, jnp.zeros_like(band_offsets), band_spread))
    along_band = jnp.dot(band_matrix, coarse, precision=lax.Precision.HIGHEST, preferred_element_type=jnp.float32)
    beside_all = jnp.dot(along_band, loop_matrix, precision=lax.Precision.HIGHEST, preferred_element_type=jnp.float32)
    backscatter = (beside_all / (loop_total * band_total)).astype(jnp.float32)

    energy = forward + ETA_BACK * jnp.repeat(jnp.repeat(backscatter, TILE, axis=0), TILE, axis=1)
    energy_grid = energy.reshape(N_TILE, TR, TILE, N_STRIPE, TC, TILE)

    def corrected(device):
        got_blocks, got_dose, got_tiles = arrived(device)
        segment = device // N_TILE
        target_dev = device % N_TILE
        local_grid = energy_grid[target_dev, :, :, segment]
        energy_tiles = local_grid.transpose(0, 2, 1, 3).reshape(tile_count, TILE * TILE)
        energy_seen = jnp.take(energy_tiles, got_tiles, axis=0)
        blocks_wide = got_blocks.astype(jnp.float32)
        exposure = jnp.sum(blocks_wide * energy_seen, axis=1) / jnp.sum(blocks_wide, axis=1)
        return jnp.where(got_dose > 0.0, got_dose * TARGET_DOSE / exposure, jnp.float32(0.0))

    new_dose = lax.map(corrected, devices).reshape(SLOTS)
    return energy, backscatter, new_dose
```

```python
import functools

import jax
import jax.numpy as jnp
import numpy as np
import ml_dtypes
from jax import lax
from jax.experimental import pallas as pl
from jax.experimental.pallas import tpu as pltpu
from jax.sharding import PartitionSpec as P

TILE = 128
TR = 8
TC = 4
HALO = 16
CAP = 8
N_STRIPE = 32
N_TILE = 8
SLOTS = N_TILE * CAP
ROWS = TR * TILE
COLS = TC * TILE
ROW_BLOCK = 256
N_ROW_BLOCKS = ROWS // ROW_BLOCK

ETA_BACK = 0.7
DILATED_WEIGHT = 0.5
TARGET_DOSE = 1.0
NARROW_SIGMA = 2.0
DILATED_SIGMA = 4.0
NXC = N_STRIPE * TC
NYC = N_TILE * TR
LOOP_SPREAD = NXC / 2.0
BAND_SPREAD = NYC / 5.0

F32 = jnp.float32
BF16 = jnp.bfloat16


def taps():
    offset = np.arange(-HALO, HALO + 1).astype(np.float32)
    narrow = np.exp(-offset * offset / np.float32(2.0 * NARROW_SIGMA**2))
    dilated = np.exp(-offset * offset / np.float32(8.0 * DILATED_SIGMA**2))
    dilated = np.where(np.arange(-HALO, HALO + 1) % 2 == 0, dilated, np.float32(0))
    narrow = (narrow / narrow.sum(dtype=np.float32)).astype(ml_dtypes.bfloat16)
    dilated = (dilated / dilated.sum(dtype=np.float32)).astype(ml_dtypes.bfloat16)
    return narrow.astype(np.float32), dilated.astype(np.float32)


def by_offset(table, offset):
    inside = np.abs(offset) <= HALO
    return np.where(inside, table[np.clip(offset + HALO, 0, 2 * HALO)], np.float32(0))


def tables():
    narrow, dilated = taps()
    y = np.arange(ROW_BLOCK)[:, None]
    j = np.arange(ROW_BLOCK + 2 * HALO)[None, :]
    rows = np.concatenate([by_offset(narrow, j - HALO - y), by_offset(dilated, j - HALO - y)], 0)
    j = np.arange(3 * TILE)[:, None]
    y = np.arange(TILE)[None, :]
    strip = np.concatenate([by_offset(narrow, j - TILE - y), by_offset(dilated, j - TILE - y)], 1)
    q = np.arange(COLS)[None, :]
    own = np.arange(COLS)[:, None]
    left = np.arange(HALO)[:, None] - HALO
    right = np.arange(HALO)[:, None] + COLS
    half = np.float32(DILATED_WEIGHT)
    cols = np.concatenate(
        [
            by_offset(narrow, own - q),
            half * by_offset(dilated, own - q),
            by_offset(narrow, left - q),
            by_offset(narrow, right - q),
            half * by_offset(dilated, left - q),
            half * by_offset(dilated, right - q),
            np.zeros((TILE - 4 * HALO, COLS), np.float32),
        ],
        0,
    )
    low = ml_dtypes.bfloat16
    return rows.astype(low), strip.astype(low), cols.astype(low)


def back_norm():
    m = np.arange(NXC)
    m = np.minimum(m, NXC - m).astype(np.float64)
    sx = np.exp(-m * m / (2.0 * LOOP_SPREAD**2)).sum()
    o = np.arange(-(NYC - 1), NYC).astype(np.float64)
    sy = np.exp(-o * o / (2.0 * BAND_SPREAD**2)).sum()
    return float(sx * sy)


def iota(shape, dim):
    return lax.broadcasted_iota(jnp.int32, shape, dim)


def fetch_groups(blocks, buf, sems):
    copies = []
    for g in range(N_TILE):
        at = pl.ds(g * CAP, CAP)
        copies.append(pltpu.make_async_copy(blocks.at[at], buf.at[at], sems.at[g]))
    return copies


def source_kernel(me_ref, dose_ref, tile_ref, count_ref, blocks, out, buf, part, total, corner, sems):
    me = me_ref[0]
    copies = fetch_groups(blocks, buf, sems)
    for c in copies:
        c.start()
    corner[...] = jnp.zeros_like(corner)
    lane16 = iota((HALO, TILE), 1)
    for d in range(N_TILE):
        copies[d].wait()

        def sum_slot(k, carry, d=d):
            s = d * CAP + k
            x = buf[s].astype(F32)
            part[s] = jnp.sum(x.reshape(TILE // 8, 8, TILE), axis=0)
            t = tile_ref[s]
            live = k < count_ref[d]
            top = (t == 0) | (t == TC - 1)
            bottom = (t == TC * (TR - 1)) | (t == TC * TR - 1)
            on_left = (t == 0) | (t == TC * (TR - 1))

            @pl.when(live & (top | bottom))
            def _():
                w = jnp.full((HALO, TILE), dose_ref[s], F32).astype(BF16).astype(F32)
                first = jnp.where(on_left, 0, TILE - HALO)
                side = (lane16 >= first) & (lane16 < first + HALO)
                w = jnp.where(side, w, 0.0)

                @pl.when(top)
                def _():
                    corner[d, 0:HALO] += w * buf[s, 0:HALO].astype(F32)

                @pl.when(bottom)
                def _():
                    corner[d, HALO : 2 * HALO] += w * buf[s, TILE - HALO : TILE].astype(F32)

            return carry

        lax.fori_loop(0, CAP, sum_slot, 0, unroll=True)
    sums = jnp.sum(jnp.sum(part[...], axis=1), axis=1, keepdims=True)
    total[...] = jnp.broadcast_to(sums, (SLOTS, TILE))
    row = iota((8, TILE), 0)
    lane = iota((8, TILE), 1)
    target = row ^ me
    target_row = target * TR + ((lane - 32) >> 2)
    in_coarse = (lane >= 32) & (lane < 32 + TR * TC)

    def add_slot(s, acc):
        d = s >> 3
        k = s & (CAP - 1)
        t = tile_ref[s]
        dose = jnp.where(k < count_ref[d], dose_ref[s], 0.0)
        dose = jnp.full((8, TILE), dose, F32)
        value = jnp.broadcast_to(total[pl.ds(s, 1), :], (8, TILE))
        weight = dose.astype(BF16).astype(F32)
        gap = (target_row - (d * TR + (t >> 2))).astype(F32)
        across = jnp.exp(gap * gap * (-1.0 / (2.0 * BAND_SPREAD**2)))
        mine = in_coarse & ((lane & (TC - 1)) == (t & (TC - 1)))
        acc = acc + jnp.where(mine, across * (weight * value * (1.0 / (TILE * TILE))), 0.0)
        own = target == d
        tile = jnp.full((8, TILE), t, jnp.int32).astype(F32)
        sent = jnp.where(lane < CAP, dose, jnp.where(lane < 2 * CAP, tile, value))
        here = own & ((lane & (CAP - 1)) == k) & (lane < 3 * CAP)
        return acc + jnp.where(here, sent, 0.0)

    info = lax.fori_loop(0, SLOTS, add_slot, jnp.zeros((8, TILE), F32), unroll=8)
    side = (lane < HALO) | (lane >= TILE - HALO)
    for r in range(N_TILE):
        out[r, 0:8] = jnp.broadcast_to(info[r : r + 1, :], (8, TILE))
        target_dev = me ^ r
        before = jnp.maximum(target_dev - 1, 0)
        after = jnp.minimum(target_dev + 1, N_TILE - 1)
        has_before = jnp.where(target_dev > 0, 1.0, 0.0)
        has_after = jnp.where(target_dev < N_TILE - 1, 1.0, 0.0)
        packed = jnp.zeros((8, TILE), F32)
        for g in range(4):
            if g < 2:
                x = corner[before, HALO + 8 * g : HALO + 8 * g + 8] * has_before
            else:
                x = corner[after, 8 * g - HALO : 8 * g - HALO + 8] * has_after
            packed = packed + pltpu.roll(jnp.where(side, x, 0.0), (HALO + 32 * g) % TILE, 1)
        out[r, 8:16] = packed


def back_kernel(me_ref, gathered, out):
    me = me_ref[0]
    row = iota((N_STRIPE, TILE), 0)
    lane = iota((N_STRIPE, TILE), 1)
    source = (row ^ me) * TC + (lane & (TC - 1))
    out_row = iota((8, TILE), 0)
    out_lane = iota((8, TILE), 1)
    mine = (out_lane >= 32) & (((out_lane - 32) >> 2) == out_row)
    result = jnp.zeros((8, TILE), F32)
    values = gathered[...]
    for q in range(TC):
        gap = jnp.abs(source - (me * TC + q))
        gap = jnp.minimum(gap, NXC - gap).astype(F32)
        loop = jnp.exp(gap * gap * (-1.0 / (2.0 * LOOP_SPREAD**2)))
        summed = jnp.sum(values * loop, axis=0, keepdims=True)
        spread = jnp.where(mine, jnp.broadcast_to(summed, (8, TILE)), 0.0)
        column = jnp.sum(spread, axis=1, keepdims=True)
        result = result + jnp.where(out_lane == q, column, 0.0)
    out[...] = (result * (1.0 / back_norm()))[:, 0:TC]


def select_rows(first):
    r = iota((HALO, TILE), 0)
    c = iota((HALO, TILE), 1)
    return jnp.where(c == r + first, 1.0, 0.0).astype(BF16)


def dot_nt(a, b):
    return lax.dot_general(a, b, (((1,), (1,)), ((), ())), preferred_element_type=F32)


def deposit_kernel(me_ref, info, tiles, blocks, pattern, top, bottom, left, right, buf, acc, sems):
    me = me_ref[0]
    copies = fetch_groups(blocks, buf, sems)
    for c in copies:
        c.start()
    acc[...] = jnp.zeros_like(acc)
    for b in range(N_TILE):
        copies[b].wait()
        source = me ^ b

        def add_slot(k, carry, b=b, source=source):
            dose = info[source, k]

            @pl.when(dose > 0.0)
            def _():
                t = tiles[source, k]
                at_row = pl.ds(pl.multiple_of((t >> 2) * TILE, TILE), TILE)
                at_col = pl.ds(pl.multiple_of((t & (TC - 1)) * TILE, TILE), TILE)
                w = jnp.full((TILE, TILE), dose, F32).astype(BF16).astype(F32)
                acc[at_row, at_col] += w * buf[b * CAP + k].astype(F32)

            return carry

        lax.fori_loop(0, CAP, add_slot, 0)

    def low(i, carry):
        at = pl.ds(pl.multiple_of(i * TILE, TILE), TILE)
        pattern[at, :] = acc[at, :].astype(BF16)
        return carry

    lax.fori_loop(0, TR, low, 0)
    top[...] = pattern[0:HALO, :]
    bottom[...] = pattern[ROWS - HALO : ROWS, :]
    left[...] = dot_nt(select_rows(0), pattern[:, 0:TILE]).astype(BF16)
    right[...] = dot_nt(select_rows(TILE - HALO), pattern[:, COLS - TILE : COLS]).astype(BF16)


def forward_kernel(
    me_ref, info, tiles, back, pattern, above, below, before, after, corner_before, corner_after,
    rows_table, strip_table, cols_table, blocks,
    energy, new_dose,
    buf, ext, windows, halo_cols, local, nums, sems, out_sems,
):
    me = me_ref[0]
    copies = fetch_groups(blocks, buf, sems)
    for c in copies:
        c.start()
    zeros = jnp.zeros((TILE - HALO, TILE), F32)
    for n, (strip, packed, first) in enumerate(
        ((before, corner_before, TILE - HALO), (after, corner_after, 0))
    ):
        at = pl.ds(n * HALO, HALO)
        ext[at, TILE : TILE + ROWS] = strip[...]
        rolled = [pltpu.roll(packed[...], (TILE - HALO - 32 * g) % TILE, 1) for g in range(4)]
        up = jnp.concatenate([zeros, rolled[0], rolled[1]], 0).astype(BF16)
        down = jnp.concatenate([rolled[2], rolled[3], zeros], 0).astype(BF16)
        pick = select_rows(first)
        ext[at, 0:TILE] = dot_nt(pick, up).astype(BF16)
        ext[at, TILE + ROWS : 2 * TILE + ROWS] = dot_nt(pick, down).astype(BF16)
    for i in range(TR):
        windows[2 * HALO * i : 2 * HALO * (i + 1), :] = ext[:, TILE * i : TILE * (i + 3)]
    passed = jnp.dot(windows[...], strip_table[...], preferred_element_type=F32)
    blank = jnp.zeros((TILE - 4 * HALO, TILE), F32)
    for i in range(TR):
        both = passed[2 * HALO * i : 2 * HALO * (i + 1), :]
        stacked = jnp.concatenate([both[:, 0:TILE], both[:, TILE:], blank], 0)
        halo_cols[TILE * i : TILE * (i + 1), :] = stacked.T.astype(BF16)
    out_copies = []
    for j in range(N_ROW_BLOCKS):
        lo, hi = ROW_BLOCK * j, ROW_BLOCK * (j + 1)
        if j == 0:
            window = jnp.concatenate([above[...], pattern[0 : hi + HALO, :]], 0)
        elif j == N_ROW_BLOCKS - 1:
            window = jnp.concatenate([pattern[lo - HALO : hi, :], below[...]], 0)
        else:
            window = pattern[lo - HALO : hi + HALO, :]
        passed = jnp.dot(rows_table[...], window, preferred_element_type=F32)
        narrow = passed[0:ROW_BLOCK].astype(BF16)
        dilated = passed[ROW_BLOCK:].astype(BF16)
        result = jnp.dot(narrow, cols_table[0:COLS, :], preferred_element_type=F32)
        result += jnp.dot(dilated, cols_table[COLS : 2 * COLS, :], preferred_element_type=F32)
        result += jnp.dot(halo_cols[lo:hi, :], cols_table[2 * COLS :, :], preferred_element_type=F32)
        for h in range(ROW_BLOCK // TILE):
            for c in range(TC):
                term = ETA_BACK * back[j * (ROW_BLOCK // TILE) + h, c]
                local[lo + h * TILE : lo + (h + 1) * TILE, c * TILE : (c + 1) * TILE] = (
                    result[h * TILE : (h + 1) * TILE, c * TILE : (c + 1) * TILE] + term
                )
        copy = pltpu.make_async_copy(local.at[pl.ds(lo, ROW_BLOCK)], energy.at[pl.ds(lo, ROW_BLOCK)], out_sems.at[j])
        copy.start()
        out_copies.append(copy)
    lane = iota((8, TILE), 1)
    row = iota((8, TILE), 0)
    dose_row = jnp.zeros((8, TILE), F32)
    sum_row = jnp.ones((8, TILE), F32)
    for b in range(N_TILE):
        copies[b].wait()
        source = me ^ b

        def see_slot(k, carry, b=b, source=source):
            dose_row, sum_row = carry
            s = b * CAP + k
            t = tiles[source, k]
            dose = info[source, k]

            @pl.when(dose > 0.0)
            def _():
                at_row = pl.ds(pl.multiple_of((t >> 2) * TILE, TILE), TILE)
                at_col = pl.ds(pl.multiple_of((t & (TC - 1)) * TILE, TILE), TILE)
                x = local[at_row, at_col] * buf[s].astype(F32)
                nums[s] = jnp.sum(x.reshape(TILE // 8, 8, TILE), axis=0)

            @pl.when(dose <= 0.0)
            def _():
                nums[s] = jnp.ones((8, TILE), F32)

            here = lane == s
            dose_row = jnp.where(here, dose, dose_row)
            sum_row = jnp.where(here, info[source, 2 * CAP + k], sum_row)
            return dose_row, sum_row

        dose_row, sum_row = lax.fori_loop(0, CAP, see_slot, (dose_row, sum_row))
    num = jnp.sum(jnp.sum(nums[...], axis=1), axis=1, keepdims=True)
    at_slot = iota((SLOTS, TILE), 0) == iota((SLOTS, TILE), 1)
    num_row = jnp.sum(jnp.where(at_slot, jnp.broadcast_to(num, (SLOTS, TILE)), 0.0), axis=0, keepdims=True)
    num_row = jnp.where(lane[0:1] < SLOTS, num_row, 1.0)
    dose = dose_row[0:1]
    corrected = dose * TARGET_DOSE / (num_row / sum_row[0:1])
    new_dose[...] = jnp.where(dose > 0.0, corrected, 0.0)[:, 0:SLOTS]
    for copy in out_copies:
        copy.wait()


def spec(space):
    return pl.BlockSpec(memory_space=space)


VMEM, SMEM, ANY = pltpu.VMEM, pltpu.SMEM, pl.ANY
PARAMS = pltpu.CompilerParams(vmem_limit_bytes=24 * 2**20)


def on_device(shot_blocks, shot_dose, shot_tile, shot_count):
    me_tile = lax.axis_index("tile").astype(jnp.int32).reshape(1)
    me_stripe = lax.axis_index("stripe").astype(jnp.int32).reshape(1)
    rows_table, strip_table, cols_table = (jnp.asarray(t) for t in tables())

    blocks = lax.all_to_all(
        shot_blocks.reshape(N_TILE, CAP, TILE, TILE), "tile", split_axis=0, concat_axis=0, tiled=True
    ).reshape(SLOTS, TILE, TILE)

    message = pl.pallas_call(
        source_kernel,
        out_shape=jax.ShapeDtypeStruct((N_TILE, 16, TILE), F32),
        in_specs=[spec(SMEM)] * 4 + [spec(ANY)],
        out_specs=spec(VMEM),
        scratch_shapes=[
            pltpu.VMEM((SLOTS, TILE, TILE), BF16),
            pltpu.VMEM((SLOTS, 8, TILE), F32),
            pltpu.VMEM((SLOTS, TILE), F32),
            pltpu.VMEM((N_TILE, 2 * HALO, TILE), F32),
            pltpu.SemaphoreType.DMA((N_TILE,)),
        ],
        compiler_params=PARAMS,
        name="source",
    )(me_tile, shot_dose, shot_tile, shot_count, shot_blocks)

    order = lax.broadcasted_iota(jnp.int32, (N_TILE, 1, 1), 0)
    for bit in (4, 2, 1):
        got = lax.ppermute(message, "tile", [(i, i ^ bit) for i in range(N_TILE)])
        message = jnp.where((order & bit) != 0, got, message)
    info = message[:, 0, :]
    tiles = info[:, CAP : 2 * CAP].astype(jnp.int32)
    summed = jnp.sum(message, axis=0)
    corners = summed[8:16]
    ring_up = [(i, (i + 1) % N_STRIPE) for i in range(N_STRIPE)]
    ring_down = [(j, i) for i, j in ring_up]
    corner_before = lax.ppermute(corners, "stripe", ring_up)
    corner_after = lax.ppermute(corners, "stripe", ring_down)
    gathered = summed[0:1]
    for bit in (1, 2, 4, 8, 16):
        got = lax.ppermute(gathered, "stripe", [(i, i ^ bit) for i in range(N_STRIPE)])
        gathered = jnp.concatenate([gathered, got], axis=0)
    backscatter = pl.pallas_call(
        back_kernel,
        out_shape=jax.ShapeDtypeStruct((TR, TC), F32),
        in_specs=[spec(SMEM), spec(VMEM)],
        out_specs=spec(VMEM),
        compiler_params=PARAMS,
        name="back",
    )(me_stripe, gathered)

    low = lambda *shape: jax.ShapeDtypeStruct(shape, BF16)
    pattern, top, bottom, left, right = pl.pallas_call(
        deposit_kernel,
        out_shape=(low(ROWS, COLS), low(HALO, COLS), low(HALO, COLS), low(HALO, ROWS), low(HALO, ROWS)),
        in_specs=[spec(SMEM)] * 3 + [spec(ANY)],
        out_specs=(spec(VMEM),) * 5,
        scratch_shapes=[
            pltpu.VMEM((SLOTS, TILE, TILE), BF16),
            pltpu.VMEM((ROWS, COLS), F32),
            pltpu.SemaphoreType.DMA((N_TILE,)),
        ],
        compiler_params=PARAMS,
        name="deposit",
    )(me_tile, info, tiles, blocks)

    band_up = [(i, i + 1) for i in range(N_TILE - 1)]
    band_down = [(j, i) for i, j in band_up]
    above = lax.ppermute(bottom, "tile", band_up)
    below = lax.ppermute(top, "tile", band_down)
    before = lax.ppermute(right, "stripe", ring_up)
    after = lax.ppermute(left, "stripe", ring_down)

    energy, new_dose = pl.pallas_call(
        forward_kernel,
        out_shape=(
            jax.ShapeDtypeStruct((ROWS, COLS), F32),
            jax.ShapeDtypeStruct((1, SLOTS), F32),
        ),
        in_specs=[spec(SMEM)] * 4 + [spec(VMEM)] * 10 + [spec(ANY)],
        out_specs=(spec(ANY), spec(VMEM)),
        scratch_shapes=[
            pltpu.VMEM((SLOTS, TILE, TILE), BF16),
            pltpu.VMEM((2 * HALO, ROWS + 2 * TILE), BF16),
            pltpu.VMEM((TR * 2 * HALO, 3 * TILE), BF16),
            pltpu.VMEM((ROWS, TILE), BF16),
            pltpu.VMEM((ROWS, COLS), F32),
            pltpu.VMEM((SLOTS, 8, TILE), F32),
            pltpu.SemaphoreType.DMA((N_TILE,)),
            pltpu.SemaphoreType.DMA((N_ROW_BLOCKS,)),
        ],
        compiler_params=PARAMS,
        name="forward",
    )(
        me_tile, info, tiles, backscatter, pattern, above, below, before, after, corner_before, corner_after,
        rows_table, strip_table, cols_table, blocks,
    )
    return energy, backscatter, new_dose.reshape(SLOTS)


def solution(mesh):
    in_specs = (
        P(("stripe", "tile"), None, None),
        P(("stripe", "tile")),
        P(("stripe", "tile")),
        P(("stripe", "tile")),
    )
    out_specs = (P("tile", "stripe"), P("tile", "stripe"), P(("stripe", "tile")))
    return jax.shard_map(
        on_device, mesh=mesh, in_specs=in_specs, out_specs=out_specs, check_vma=False
    )
```

```python
import jax
import jax.numpy as jnp
import numpy as np
import ml_dtypes
from jax import lax
from jax.experimental import pallas as pl
from jax.experimental.pallas import tpu as pltpu
from jax.sharding import PartitionSpec as P

TILE = 128
TR = 8
TC = 4
HALO = 16
CAP = 8
N_STRIPE = 32
N_TILE = 8
SLOTS = N_TILE * CAP
ROWS = TR * TILE
COLS = TC * TILE
ROW_BLOCK = 256
EXT_ROWS = ROWS + 2 * HALO
STRIP = ROWS + TILE
BODY = CAP * TILE
EDGE = 2 * TC * HALO
INFO = BODY + EDGE
MESSAGE = INFO + HALO
N_ROW_BLOCKS = ROWS // ROW_BLOCK

ETA_BACK = 0.7
DILATED_WEIGHT = 0.5
TARGET_DOSE = 1.0
NARROW_SIGMA = 2.0
DILATED_SIGMA = 4.0
NXC = N_STRIPE * TC
NYC = N_TILE * TR
LOOP_SPREAD = NXC / 2.0
BAND_SPREAD = NYC / 5.0

F32 = jnp.float32
BF16 = jnp.bfloat16


def taps():
    offset = np.arange(-HALO, HALO + 1).astype(np.float32)
    narrow = np.exp(-offset * offset / np.float32(2.0 * NARROW_SIGMA**2))
    dilated = np.exp(-offset * offset / np.float32(8.0 * DILATED_SIGMA**2))
    dilated = np.where(np.arange(-HALO, HALO + 1) % 2 == 0, dilated, np.float32(0))
    narrow = (narrow / narrow.sum(dtype=np.float32)).astype(ml_dtypes.bfloat16)
    dilated = (dilated / dilated.sum(dtype=np.float32)).astype(ml_dtypes.bfloat16)
    return narrow.astype(np.float32), dilated.astype(np.float32)


def by_offset(table, offset):
    inside = np.abs(offset) <= HALO
    return np.where(inside, table[np.clip(offset + HALO, 0, 2 * HALO)], np.float32(0))


def tables():
    narrow, dilated = taps()
    y = np.arange(ROW_BLOCK)[:, None]
    j = np.arange(ROW_BLOCK + 2 * HALO)[None, :]
    rows = np.concatenate([by_offset(narrow, j - HALO - y), by_offset(dilated, j - HALO - y)], 0)
    j = np.arange(2 * TILE)[:, None]
    y = np.arange(TILE)[None, :]
    strip = np.concatenate([by_offset(narrow, j - HALO - y), by_offset(dilated, j - HALO - y)], 1)
    q = np.arange(COLS)[None, :]
    own = np.arange(COLS)[:, None]
    left = np.arange(HALO)[:, None] - HALO
    right = np.arange(HALO)[:, None] + COLS
    half = np.float32(DILATED_WEIGHT)
    cols = np.concatenate(
        [
            by_offset(narrow, own - q),
            half * by_offset(dilated, own - q),
            by_offset(narrow, left - q),
            by_offset(narrow, right - q),
            half * by_offset(dilated, left - q),
            half * by_offset(dilated, right - q),
            np.zeros((TILE - 4 * HALO, COLS), np.float32),
        ],
        0,
    )
    low = ml_dtypes.bfloat16
    return rows.astype(low), strip.astype(low), cols.astype(low)


def back_norm():
    m = np.arange(NXC)
    m = np.minimum(m, NXC - m).astype(np.float64)
    sx = np.exp(-m * m / (2.0 * LOOP_SPREAD**2)).sum()
    o = np.arange(-(NYC - 1), NYC).astype(np.float64)
    sy = np.exp(-o * o / (2.0 * BAND_SPREAD**2)).sum()
    return float(sx * sy)


def iota(shape, dim):
    return lax.broadcasted_iota(jnp.int32, shape, dim)


def splat_low(value, shape):
    return jnp.full(shape, value, F32).astype(BF16).astype(F32)


def pack_kernel(dose_ref, tile_ref, count_ref, groups, blocks, out, tops, bottoms, edge, tail, sems, strip_sems):
    body = [
        pltpu.make_async_copy(groups.at[d], out.at[d, pl.ds(0, BODY)], sems.at[d])
        for d in range(N_TILE)
    ]
    strips = [
        pltpu.make_async_copy(blocks.at[:, pl.ds(0, HALO)], tops, strip_sems.at[0]),
        pltpu.make_async_copy(blocks.at[:, pl.ds(TILE - HALO, HALO)], bottoms, strip_sems.at[1]),
    ]
    for c in strips + body:
        c.start()
    edge[...] = jnp.zeros_like(edge)
    row = iota((8, TILE), 0)
    lane = iota((8, TILE), 1)

    def add_info(s, acc):
        d = s >> 3
        k = s & (CAP - 1)
        dose = jnp.where(k < count_ref[d], dose_ref[s], 0.0)
        tile = jnp.full((8, TILE), tile_ref[s], jnp.int32).astype(F32)
        acc = jnp.where((row == d) & (lane == k), dose, acc)
        return jnp.where((row == d) & (lane == k + CAP), tile, acc)

    info = lax.fori_loop(0, SLOTS, add_info, jnp.zeros((8, TILE), F32), unroll=8)
    high = info.astype(BF16).astype(F32)
    middle = (info - high).astype(BF16).astype(F32)
    lowest = info - high - middle
    row = iota((HALO, TILE), 0)
    for d in range(N_TILE):
        at = slice(d, d + 1)
        rows = jnp.where(row == 0, high[at], jnp.where(row == 1, middle[at], jnp.where(row == 2, lowest[at], 0.0)))
        tail[d, EDGE:] = rows.astype(BF16)
    for c in strips:
        c.wait()

    def add_edges(s, carry):
        d = s >> 3
        t = tile_ref[s]
        live = (s & (CAP - 1)) < count_ref[d]
        c = t & (TC - 1)

        @pl.when(live & (t < TC))
        def _():
            edge[d, 0, c] += splat_low(dose_ref[s], (HALO, TILE)) * tops[s].astype(F32)

        @pl.when(live & (t >= TC * (TR - 1)))
        def _():
            edge[d, 1, c] += splat_low(dose_ref[s], (HALO, TILE)) * bottoms[s].astype(F32)

        return carry

    lax.fori_loop(0, SLOTS, add_edges, 0)
    blank = jnp.zeros((EDGE // 2, TILE), BF16)
    for d in range(N_TILE):
        if d > 0:
            tail[d, 0 : EDGE // 2] = edge[d - 1, 1].reshape(EDGE // 2, TILE).astype(BF16)
        else:
            tail[d, 0 : EDGE // 2] = blank
        if d < N_TILE - 1:
            tail[d, EDGE // 2 : EDGE] = edge[d + 1, 0].reshape(EDGE // 2, TILE).astype(BF16)
        else:
            tail[d, EDGE // 2 : EDGE] = blank
    last = pltpu.make_async_copy(tail, out.at[:, pl.ds(BODY, MESSAGE - BODY)], strip_sems.at[2])
    last.start()
    for c in body:
        c.wait()
    last.wait()


def source_kernel(me_ref, dose_ref, tile_ref, count_ref, groups, out, buf, part, total, sems):
    me = me_ref[0]
    copies = [pltpu.make_async_copy(groups.at[d], buf.at[d], sems.at[d]) for d in range(N_TILE)]
    for c in copies:
        c.start()
    for d in range(N_TILE):
        copies[d].wait()
        for k in range(CAP):
            x = buf[d, k * TILE : (k + 1) * TILE].astype(F32)
            part[d * CAP + k] = jnp.sum(x.reshape(TILE // 8, 8, TILE), axis=0)
    sums = jnp.sum(jnp.sum(part[...], axis=1), axis=1, keepdims=True) * (1.0 / (TILE * TILE))
    total[...] = jnp.broadcast_to(sums, (SLOTS, TILE))
    row = iota((8, TILE), 0)
    lane = iota((8, TILE), 1)
    target_row = row * TR + ((lane & 31) >> 2)
    column = lane >> 5

    def add_slot(s, acc):
        d = s >> 3
        t = tile_ref[s]
        dose = jnp.where((s & (CAP - 1)) < count_ref[d], dose_ref[s], 0.0)
        value = jnp.broadcast_to(total[pl.ds(s, 1), :], (8, TILE))
        gap = (target_row - (d * TR + (t >> 2))).astype(F32)
        across = jnp.exp(gap * gap * (-1.0 / (2.0 * BAND_SPREAD**2)))
        return acc + jnp.where(column == (t & (TC - 1)), across * (splat_low(dose, (8, TILE)) * value), 0.0)

    acc = lax.fori_loop(0, SLOTS, add_slot, jnp.zeros((8, TILE), F32), unroll=8)
    for i in range(8):
        low_bits = ((i >> 2) & 1) + (i & 2) + 4 * (i & 1)
        result = jnp.zeros((8, TILE), F32)
        for g in range(4):
            r = low_bits + 8 * (g >> 1) + 16 * (g & 1)
            gap = jnp.abs(me * TC + column - ((me ^ r) * TC + (lane & (TC - 1))))
            gap = jnp.minimum(gap, NXC - gap).astype(F32)
            x = acc * jnp.exp(gap * gap * (-1.0 / (2.0 * LOOP_SPREAD**2)))
            x = x + pltpu.roll(x, 64, 1)
            x = x + pltpu.roll(x, 32, 1)
            result = jnp.where(column == g, x, result)
        out[i] = result


def select_rows(first):
    r = iota((HALO, TILE), 0)
    c = iota((HALO, TILE), 1)
    return jnp.where(c == r + first, 1.0, 0.0).astype(BF16)


def dot_nt(a, b):
    return lax.dot_general(a, b, (((1,), (1,)), ((), ())), preferred_element_type=F32)


def tile_at(t):
    at_row = pl.ds(pl.multiple_of((t >> 2) * TILE, TILE), TILE)
    at_col = pl.ds(pl.multiple_of((t & (TC - 1)) * TILE, TILE), TILE)
    return at_row, at_col


def deposit_kernel(got, pattern, left, right, info, tiles, acc, ext, dose_s, tile_s, sems, out_sems):
    rows = []
    for b in range(N_TILE):
        x = got[b, INFO:MESSAGE].astype(F32)
        rows.append(x[0:1] + x[1:2] + x[2:3])
    values = jnp.concatenate(rows, 0)
    info[...] = values
    tiles[...] = values.astype(jnp.int32)
    to_dose = pltpu.make_async_copy(info, dose_s, sems.at[0])
    to_tile = pltpu.make_async_copy(tiles, tile_s, sems.at[1])
    to_dose.start()
    to_tile.start()
    acc[...] = jnp.zeros_like(acc)
    for side in range(2):
        at = slice(0, HALO) if side == 0 else slice(EXT_ROWS - HALO, EXT_ROWS)
        for c in range(TC):
            first = BODY + (side * TC + c) * HALO
            x = got[0, first : first + HALO].astype(F32)
            for b in range(1, N_TILE):
                x = x + got[b, first : first + HALO].astype(F32)
            ext[at, c * TILE : (c + 1) * TILE] = x.astype(BF16)
    to_dose.wait()
    to_tile.wait()

    def add_group(b, carry):
        for k in range(CAP):
            dose = dose_s[b, k]

            @pl.when(dose > 0.0)
            def _(k=k, dose=dose):
                x = got[b, k * TILE : (k + 1) * TILE].astype(F32)
                acc[tile_at(tile_s[b, CAP + k])] += splat_low(dose, (TILE, TILE)) * x

        return carry

    lax.fori_loop(0, N_TILE, add_group, 0)
    copies = []
    for j in range(N_ROW_BLOCKS):
        lo, hi = j * ROW_BLOCK, (j + 1) * ROW_BLOCK
        ext[HALO + lo : HALO + hi, :] = acc[lo:hi, :].astype(BF16)
        first = 0 if j == 0 else HALO + lo
        end = EXT_ROWS if j == N_ROW_BLOCKS - 1 else HALO + hi
        at = pl.ds(first, end - first)
        copies.append(pltpu.make_async_copy(ext.at[at], pattern.at[at], out_sems.at[j]))
        copies[-1].start()
    blank = jnp.zeros((HALO, STRIP - EXT_ROWS), BF16)
    for out, first, lane in ((left, 0, 0), (right, TILE - HALO, COLS - TILE)):
        strip = dot_nt(select_rows(first), ext[:, lane : lane + TILE]).astype(BF16)
        out[...] = jnp.concatenate([strip, blank], 1)
    for c in copies:
        c.wait()


def forward_kernel(
    me_ref, info, tiles, back_own, back_got, before, after, got, pattern, rows_hbm, strip_hbm, cols_hbm,
    energy, new_dose, backscatter,
    ext, rows_table, strip_table, cols_table, windows, halo_cols, local, nums, dens, sems, in_sems, out_sems,
):
    me = me_ref[0]
    to_strip = pltpu.make_async_copy(strip_hbm, strip_table, sems.at[0])
    to_rows = pltpu.make_async_copy(rows_hbm, rows_table, sems.at[1])
    to_cols = pltpu.make_async_copy(cols_hbm, cols_table, sems.at[2])
    parts = []
    for j in range(N_ROW_BLOCKS):
        first = 0 if j == 0 else j * ROW_BLOCK + 2 * HALO
        at = pl.ds(first, (j + 1) * ROW_BLOCK + 2 * HALO - first)
        parts.append(pltpu.make_async_copy(pattern.at[at], ext.at[at], in_sems.at[j]))
    for c in [to_strip, to_rows, parts[0], to_cols] + parts[1:]:
        c.start()
    lane = iota((8, TILE), 1)
    row = iota((8, TILE), 0)
    own = (back_own[...] + back_got[...]) * (1.0 / back_norm())
    own = jnp.sum(jnp.where(iota((8, 32), 0) == me, own, 0.0), axis=0, keepdims=True)
    own = jnp.broadcast_to(own, (8, 32))
    small_row, small_lane = iota((8, 32), 0), iota((8, 32), 1)
    terms = []
    for c in range(TC):
        at = small_lane == small_row * TC + c
        term = jnp.sum(jnp.where(at, own, 0.0), axis=1, keepdims=True)
        terms.append(jnp.broadcast_to(term, (8, TILE)))
        backscatter[c : c + 1, :] = jnp.sum(jnp.where(lane == row, terms[c], 0.0), axis=0, keepdims=True)[:, 0:TR]
    to_strip.wait()
    for i in range(TR):
        at = slice(TILE * i, TILE * (i + 2))
        windows[2 * HALO * i : 2 * HALO * i + HALO, :] = before[:, at]
        windows[2 * HALO * i + HALO : 2 * HALO * (i + 1), :] = after[:, at]
    passed = jnp.dot(windows[...], strip_table[...], preferred_element_type=F32)
    blank = jnp.zeros((TILE - 4 * HALO, TILE), F32)
    for i in range(TR):
        both = passed[2 * HALO * i : 2 * HALO * (i + 1), :]
        stacked = jnp.concatenate([both[:, 0:TILE], both[:, TILE:], blank], 0)
        halo_cols[TILE * i : TILE * (i + 1), :] = stacked.T.astype(BF16)
    to_rows.wait()
    out_copies = []
    for j in range(N_ROW_BLOCKS):
        lo, hi = ROW_BLOCK * j, ROW_BLOCK * (j + 1)
        parts[j].wait()
        passed = jnp.dot(rows_table[...], ext[lo : hi + 2 * HALO, :], preferred_element_type=F32)
        narrow = passed[0:ROW_BLOCK].astype(BF16)
        dilated = passed[ROW_BLOCK:].astype(BF16)
        if j == 0:
            to_cols.wait()
        result = jnp.dot(narrow, cols_table[0:COLS, :], preferred_element_type=F32)
        result += jnp.dot(dilated, cols_table[COLS : 2 * COLS, :], preferred_element_type=F32)
        result += jnp.dot(halo_cols[lo:hi, :], cols_table[2 * COLS :, :], preferred_element_type=F32)
        for h in range(ROW_BLOCK // TILE):
            p = j * (ROW_BLOCK // TILE) + h
            for c in range(TC):
                at = slice(c * TILE, (c + 1) * TILE)
                term = ETA_BACK * terms[c][p : p + 1]
                local[lo + h * TILE : lo + (h + 1) * TILE, at] = result[h * TILE : (h + 1) * TILE, at] + term
        rows = pl.ds(lo, ROW_BLOCK)
        out_copies.append(pltpu.make_async_copy(local.at[rows], energy.at[rows], out_sems.at[j]))
        out_copies[-1].start()

    def see_group(b, dose_row):
        for k in range(CAP):
            s = b * CAP + k
            dose = info[b, k]

            @pl.when(dose > 0.0)
            def _(k=k, s=s):
                x = got[b, k * TILE : (k + 1) * TILE].astype(F32)
                seen = local[tile_at(tiles[b, CAP + k])] * x
                nums[s] = jnp.sum(seen.reshape(TILE // 8, 8, TILE), axis=0)
                dens[s] = jnp.sum(x.reshape(TILE // 8, 8, TILE), axis=0)

            @pl.when(dose <= 0.0)
            def _(s=s):
                nums[s] = jnp.ones((8, TILE), F32)
                dens[s] = jnp.ones((8, TILE), F32)

            dose_row = jnp.where(lane == s, dose, dose_row)
        return dose_row

    dose_row = lax.fori_loop(0, N_TILE, see_group, jnp.zeros((8, TILE), F32))
    num = jnp.sum(jnp.sum(nums[...], axis=1), axis=1, keepdims=True)
    den = jnp.sum(jnp.sum(dens[...], axis=1), axis=1, keepdims=True)
    exposure = jnp.broadcast_to(num / den, (SLOTS, TILE))
    at_slot = iota((SLOTS, TILE), 0) == iota((SLOTS, TILE), 1)
    exposure = jnp.sum(jnp.where(at_slot, exposure, 0.0), axis=0, keepdims=True)[:, 0:SLOTS]
    dose = dose_row[0:1, 0:SLOTS]
    new_dose[...] = jnp.where(dose > 0.0, dose * TARGET_DOSE / exposure, 0.0)
    for copy in out_copies:
        copy.wait()


def spec(space):
    return pl.BlockSpec(memory_space=space)


VMEM, SMEM, HBM = pltpu.VMEM, pltpu.SMEM, pltpu.HBM
PARAMS = pltpu.CompilerParams(vmem_limit_bytes=24 * 2**20)


def array(shape, dtype):
    return jax.ShapeDtypeStruct(shape, dtype)


def on_device(shot_blocks, shot_dose, shot_tile, shot_count):
    me_tile = lax.axis_index("tile").astype(jnp.int32).reshape(1)
    me_stripe = lax.axis_index("stripe").astype(jnp.int32).reshape(1)
    rows_table, strip_table, cols_table = (jnp.asarray(t) for t in tables())
    groups = shot_blocks.reshape(N_TILE, BODY, TILE)

    message = pl.pallas_call(
        pack_kernel,
        out_shape=array((N_TILE, MESSAGE, TILE), BF16),
        in_specs=[spec(SMEM)] * 3 + [spec(HBM)] * 2,
        out_specs=spec(HBM),
        scratch_shapes=[
            pltpu.VMEM((SLOTS, HALO, TILE), BF16),
            pltpu.VMEM((SLOTS, HALO, TILE), BF16),
            pltpu.VMEM((N_TILE, 2, TC, HALO, TILE), F32),
            pltpu.VMEM((N_TILE, MESSAGE - BODY, TILE), BF16),
            pltpu.SemaphoreType.DMA((N_TILE,)),
            pltpu.SemaphoreType.DMA((3,)),
        ],
        compiler_params=PARAMS,
        name="pack",
    )(shot_dose, shot_tile, shot_count, groups, shot_blocks)
    got = lax.all_to_all(message, "tile", split_axis=0, concat_axis=0, tiled=True)

    back = pl.pallas_call(
        source_kernel,
        out_shape=array((8, 8, TILE), F32),
        in_specs=[spec(SMEM)] * 4 + [spec(HBM)],
        out_specs=spec(VMEM),
        scratch_shapes=[
            pltpu.VMEM((N_TILE, BODY, TILE), BF16),
            pltpu.VMEM((SLOTS, 8, TILE), F32),
            pltpu.VMEM((SLOTS, TILE), F32),
            pltpu.SemaphoreType.DMA((N_TILE,)),
        ],
        compiler_params=PARAMS,
        name="source",
    )(me_stripe, shot_dose, shot_tile, shot_count, groups)

    for bit in (1, 2, 4):
        half = back.shape[0] // 2
        sent = lax.ppermute(back[half:], "stripe", [(i, i ^ bit) for i in range(N_STRIPE)])
        back = back[:half] + sent
    back = back.reshape(8, TILE)
    sent = lax.ppermute(back, "stripe", [(i, i ^ 8) for i in range(N_STRIPE)])
    back = back[:, 0:64] + sent[:, 64:128]

    def swapped(x, stripe_bit, tile_bit):
        pairs = [
            (a * N_TILE + b, (a ^ stripe_bit) * N_TILE + (b ^ tile_bit))
            for a in range(N_STRIPE)
            for b in range(N_TILE)
        ]
        return lax.ppermute(x, ("stripe", "tile"), pairs)

    back = back[:, 0:32] + swapped(back, 16, 0)[:, 32:64] + swapped(back, 0, 4)[:, 0:32] + swapped(back, 16, 4)[:, 32:64]
    back = back + swapped(back, 0, 1)
    back_got = swapped(back, 0, 2)

    pattern, left, right, info, tiles = pl.pallas_call(
        deposit_kernel,
        out_shape=(
            array((EXT_ROWS, COLS), BF16),
            array((HALO, STRIP), BF16),
            array((HALO, STRIP), BF16),
            array((N_TILE, TILE), F32),
            array((N_TILE, TILE), jnp.int32),
        ),
        in_specs=[spec(VMEM)],
        out_specs=(spec(HBM),) + (spec(VMEM),) * 4,
        scratch_shapes=[
            pltpu.VMEM((ROWS, COLS), F32),
            pltpu.VMEM((EXT_ROWS, COLS), BF16),
            pltpu.SMEM((N_TILE, TILE), F32),
            pltpu.SMEM((N_TILE, TILE), jnp.int32),
            pltpu.SemaphoreType.DMA((2,)),
            pltpu.SemaphoreType.DMA((N_ROW_BLOCKS,)),
        ],
        compiler_params=PARAMS,
        name="deposit",
    )(got)

    ring_up = [(i, (i + 1) % N_STRIPE) for i in range(N_STRIPE)]
    ring_down = [(j, i) for i, j in ring_up]
    before = lax.ppermute(right, "stripe", ring_up)
    after = lax.ppermute(left, "stripe", ring_down)

    energy, new_dose, backscatter = pl.pallas_call(
        forward_kernel,
        out_shape=(
            array((ROWS, COLS), F32),
            array((1, SLOTS), F32),
            array((TC, TR), F32),
        ),
        in_specs=[spec(SMEM)] * 3 + [spec(VMEM)] * 5 + [spec(HBM)] * 4,
        out_specs=(spec(HBM), spec(VMEM), spec(VMEM)),
        scratch_shapes=[
            pltpu.VMEM((EXT_ROWS, COLS), BF16),
            pltpu.VMEM(rows_table.shape, BF16),
            pltpu.VMEM(strip_table.shape, BF16),
            pltpu.VMEM(cols_table.shape, BF16),
            pltpu.VMEM((TR * 2 * HALO, 2 * TILE), BF16),
            pltpu.VMEM((ROWS, TILE), BF16),
            pltpu.VMEM((ROWS, COLS), F32),
            pltpu.VMEM((SLOTS, 8, TILE), F32),
            pltpu.VMEM((SLOTS, 8, TILE), F32),
            pltpu.SemaphoreType.DMA((3,)),
            pltpu.SemaphoreType.DMA((N_ROW_BLOCKS,)),
            pltpu.SemaphoreType.DMA((N_ROW_BLOCKS,)),
        ],
        compiler_params=PARAMS,
        name="forward",
    )(me_tile, info, tiles, back, back_got, before, after, got, pattern, rows_table, strip_table, cols_table)
    return energy, backscatter.T, new_dose.reshape(SLOTS)


def solution(mesh):
    in_specs = (
        P(("stripe", "tile"), None, None),
        P(("stripe", "tile")),
        P(("stripe", "tile")),
        P(("stripe", "tile")),
    )
    out_specs = (P("tile", "stripe"), P("tile", "stripe"), P(("stripe", "tile")))
    return jax.shard_map(
        on_device, mesh=mesh, in_specs=in_specs, out_specs=out_specs, check_vma=False
    )
```

```python
import jax
import jax.numpy as jnp
import numpy as np
import ml_dtypes
from jax import lax
from jax.experimental import pallas as pl
from jax.experimental.pallas import tpu as pltpu
from jax.sharding import PartitionSpec as P

TILE = 128
TR = 8
TC = 4
HALO = 16
CAP = 8
N_STRIPE = 32
N_TILE = 8
SLOTS = N_TILE * CAP
ROWS = TR * TILE
COLS = TC * TILE
ROW_BLOCK = 256
COL_BLOCK = 256
EXT_ROWS = ROWS + 2 * HALO
STRIP = ROWS + TILE
BODY = CAP * TILE
EDGE = 2 * TC * HALO
INFO = BODY + EDGE
MESSAGE = INFO + HALO
N_ROW_BLOCKS = ROWS // ROW_BLOCK

ETA_BACK = 0.7
DILATED_WEIGHT = 0.5
TARGET_DOSE = 1.0
NARROW_SIGMA = 2.0
DILATED_SIGMA = 4.0
NXC = N_STRIPE * TC
NYC = N_TILE * TR
LOOP_SPREAD = NXC / 2.0
BAND_SPREAD = NYC / 5.0

F32 = jnp.float32
BF16 = jnp.bfloat16


def taps():
    offset = np.arange(-HALO, HALO + 1).astype(np.float32)
    narrow = np.exp(-offset * offset / np.float32(2.0 * NARROW_SIGMA**2))
    dilated = np.exp(-offset * offset / np.float32(8.0 * DILATED_SIGMA**2))
    dilated = np.where(np.arange(-HALO, HALO + 1) % 2 == 0, dilated, np.float32(0))
    narrow = (narrow / narrow.sum(dtype=np.float32)).astype(ml_dtypes.bfloat16)
    dilated = (dilated / dilated.sum(dtype=np.float32)).astype(ml_dtypes.bfloat16)
    return narrow.astype(np.float32), dilated.astype(np.float32)


def by_offset(table, offset):
    inside = np.abs(offset) <= HALO
    return np.where(inside, table[np.clip(offset + HALO, 0, 2 * HALO)], np.float32(0))


OWN_NARROW, OWN_DILATED, SIDE_LEFT, SIDE_RIGHT, STRIPS, ROWS_PASS = 0, 256, 512, 640, 768, 1024
TABLE_END = 1280
TABLE_ROWS = 5120
ROWS_WINDOW = TILE + 2 * HALO


def tables():
    narrow, dilated = taps()
    half = np.float32(DILATED_WEIGHT)
    table = np.zeros((TABLE_ROWS, COL_BLOCK), np.float32)
    q = np.arange(COL_BLOCK)[None, :]
    own = np.arange(COL_BLOCK)[:, None] - q
    table[OWN_NARROW : OWN_NARROW + COL_BLOCK] = by_offset(narrow, own)
    table[OWN_DILATED : OWN_DILATED + COL_BLOCK] = half * by_offset(dilated, own)
    n = np.arange(HALO)[:, None]
    before, after = n - HALO - q, n + COL_BLOCK - q
    left, right = table[SIDE_LEFT : SIDE_LEFT + TILE], table[SIDE_RIGHT : SIDE_RIGHT + TILE]
    left[0:HALO] = by_offset(narrow, after)
    left[HALO : 2 * HALO] = half * by_offset(dilated, after)
    left[2 * HALO : 3 * HALO] = by_offset(narrow, before)
    left[3 * HALO : 4 * HALO] = half * by_offset(dilated, before)
    right[TILE - HALO : TILE] = by_offset(narrow, before)
    right[0:HALO] = half * by_offset(dilated, before)
    right[2 * HALO : 3 * HALO] = by_offset(narrow, after)
    right[3 * HALO : 4 * HALO] = half * by_offset(dilated, after)
    j = np.arange(2 * TILE)[:, None]
    y = np.arange(TILE)[None, :]
    table[STRIPS : STRIPS + 2 * TILE, 0:TILE] = by_offset(narrow, j - HALO - y)
    table[STRIPS : STRIPS + 2 * TILE, TILE:] = by_offset(dilated, j - HALO - y)
    y = np.arange(TILE)[:, None]
    j = np.arange(ROWS_WINDOW)[None, :]
    table[ROWS_PASS : ROWS_PASS + TILE, 0:ROWS_WINDOW] = by_offset(narrow, j - HALO - y)
    table[ROWS_PASS + TILE : ROWS_PASS + 2 * TILE, 0:ROWS_WINDOW] = by_offset(dilated, j - HALO - y)
    return table.astype(ml_dtypes.bfloat16)


def back_norm():
    m = np.arange(NXC)
    m = np.minimum(m, NXC - m).astype(np.float64)
    sx = np.exp(-m * m / (2.0 * LOOP_SPREAD**2)).sum()
    o = np.arange(-(NYC - 1), NYC).astype(np.float64)
    sy = np.exp(-o * o / (2.0 * BAND_SPREAD**2)).sum()
    return float(sx * sy)


def iota(shape, dim):
    return lax.broadcasted_iota(jnp.int32, shape, dim)


def splat_low(value, shape):
    return jnp.full(shape, value, F32).astype(BF16).astype(F32)


def pack_kernel(dose_ref, tile_ref, count_ref, groups, out, buf, edge, tail, in_sems, out_sems):
    reads, writes = [], []
    for d in range(N_TILE):
        reads.append(pltpu.make_async_copy(groups.at[d], buf.at[d], in_sems.at[d]))
        writes.append(pltpu.make_async_copy(buf.at[d], out.at[d, pl.ds(0, BODY)], out_sems.at[d]))
    for c in reads:
        c.start()
    edge[...] = jnp.zeros_like(edge)
    row = iota((8, TILE), 0)
    lane = iota((8, TILE), 1)

    def add_info(s, acc):
        d = s >> 3
        k = s & (CAP - 1)
        dose = jnp.where(k < count_ref[d], dose_ref[s], 0.0)
        tile = jnp.full((8, TILE), tile_ref[s], jnp.int32).astype(F32)
        acc = jnp.where((row == d) & (lane == k), dose, acc)
        return jnp.where((row == d) & (lane == k + CAP), tile, acc)

    info = lax.fori_loop(0, SLOTS, add_info, jnp.zeros((8, TILE), F32), unroll=8)
    high = info.astype(BF16).astype(F32)
    middle = (info - high).astype(BF16).astype(F32)
    lowest = info - high - middle
    row = iota((HALO, TILE), 0)
    for d in range(N_TILE):
        at = slice(d, d + 1)
        rows = jnp.where(row == 0, high[at], jnp.where(row == 1, middle[at], jnp.where(row == 2, lowest[at], 0.0)))
        tail[d, EDGE:] = rows.astype(BF16)
    half = EDGE // 2
    blank = jnp.zeros((half, TILE), BF16)

    def send_tail(d):
        above = edge[d - 1, 1].reshape(half, TILE).astype(BF16) if d > 0 else blank
        below = edge[d + 1, 0].reshape(half, TILE).astype(BF16) if d < N_TILE - 1 else blank
        tail[d, 0:half] = above
        tail[d, half:EDGE] = below
        writes.append(
            pltpu.make_async_copy(tail.at[d], out.at[d, pl.ds(BODY, MESSAGE - BODY)], out_sems.at[N_TILE + d])
        )
        writes[-1].start()

    for d in range(N_TILE):
        reads[d].wait()
        writes[d].start()

        def add_edges(k, carry, d=d):
            s = d * CAP + k
            t = tile_ref[s]
            live = k < count_ref[d]
            c = t & (TC - 1)
            first = pl.multiple_of(k * TILE, TILE)

            @pl.when(live & (t < TC))
            def _():
                x = buf[d, pl.ds(first, HALO), :].astype(F32)
                edge[d, 0, c] += splat_low(dose_ref[s], (HALO, TILE)) * x

            @pl.when(live & (t >= TC * (TR - 1)))
            def _():
                x = buf[d, pl.ds(first + TILE - HALO, HALO), :].astype(F32)
                edge[d, 1, c] += splat_low(dose_ref[s], (HALO, TILE)) * x

            return carry

        lax.fori_loop(0, CAP, add_edges, 0)
        if d > 0:
            send_tail(d - 1)
    send_tail(N_TILE - 1)
    for c in writes:
        c.wait()


def source_kernel(me_ref, dose_ref, tile_ref, count_ref, groups, out, buf, part, total, sems):
    me = me_ref[0]
    copies = [pltpu.make_async_copy(groups.at[d], buf.at[d], sems.at[d]) for d in range(N_TILE)]
    for c in copies:
        c.start()
    for d in range(N_TILE):
        copies[d].wait()
        for k in range(CAP):
            x = buf[d, k * TILE : (k + 1) * TILE].astype(F32)
            part[d * CAP + k] = jnp.sum(x.reshape(TILE // 8, 8, TILE), axis=0)
    sums = jnp.sum(jnp.sum(part[...], axis=1), axis=1, keepdims=True) * (1.0 / (TILE * TILE))
    total[...] = jnp.broadcast_to(sums, (SLOTS, TILE))
    row = iota((8, TILE), 0)
    lane = iota((8, TILE), 1)
    target_row = row * TR + ((lane & 31) >> 2)
    column = lane >> 5

    def add_slot(s, acc):
        d = s >> 3
        t = tile_ref[s]
        dose = jnp.where((s & (CAP - 1)) < count_ref[d], dose_ref[s], 0.0)
        value = jnp.broadcast_to(total[pl.ds(s, 1), :], (8, TILE))
        gap = (target_row - (d * TR + (t >> 2))).astype(F32)
        across = jnp.exp(gap * gap * (-1.0 / (2.0 * BAND_SPREAD**2)))
        return acc + jnp.where(column == (t & (TC - 1)), across * (splat_low(dose, (8, TILE)) * value), 0.0)

    acc = lax.fori_loop(0, SLOTS, add_slot, jnp.zeros((8, TILE), F32), unroll=8)
    for i in range(8):
        low_bits = ((i >> 2) & 1) + (i & 2) + 4 * (i & 1)
        result = jnp.zeros((8, TILE), F32)
        for g in range(4):
            r = low_bits + 8 * (g >> 1) + 16 * (g & 1)
            gap = jnp.abs(me * TC + column - ((me ^ r) * TC + (lane & (TC - 1))))
            gap = jnp.minimum(gap, NXC - gap).astype(F32)
            x = acc * jnp.exp(gap * gap * (-1.0 / (2.0 * LOOP_SPREAD**2)))
            x = x + pltpu.roll(x, 64, 1)
            x = x + pltpu.roll(x, 32, 1)
            result = jnp.where(column == g, x, result)
        out[i] = result


def select_rows(first):
    r = iota((HALO, TILE), 0)
    c = iota((HALO, TILE), 1)
    return jnp.where(c == r + first, 1.0, 0.0).astype(BF16)


def dot_nt(a, b):
    return lax.dot_general(a, b, (((1,), (1,)), ((), ())), preferred_element_type=F32)


def tile_at(t):
    at_row = pl.ds(pl.multiple_of((t >> 2) * TILE, TILE), TILE)
    at_col = pl.ds(pl.multiple_of((t & (TC - 1)) * TILE, TILE), TILE)
    return at_row, at_col


def decode(got):
    rows = []
    for b in range(N_TILE):
        x = got[b, INFO:MESSAGE].astype(F32)
        rows.append(x[0:1] + x[1:2] + x[2:3])
    return jnp.concatenate(rows, 0)


def slot_copies(info, tiles, dose_s, tile_s, sems):
    return (
        pltpu.make_async_copy(info, dose_s, sems.at[0]),
        pltpu.make_async_copy(tiles, tile_s, sems.at[1]),
    )


def deposit_kernel(got, ext, left, right, info, tiles, acc, dose_s, tile_s, sems):
    values = decode(got)
    info[...] = values
    tiles[...] = values.astype(jnp.int32)
    to_slots = slot_copies(info, tiles, dose_s, tile_s, sems)
    for c in to_slots:
        c.start()
    acc[...] = jnp.zeros_like(acc)
    for side in range(2):
        at = slice(0, HALO) if side == 0 else slice(EXT_ROWS - HALO, EXT_ROWS)
        for c in range(TC):
            first = BODY + (side * TC + c) * HALO
            x = got[0, first : first + HALO].astype(F32)
            for b in range(1, N_TILE):
                x = x + got[b, first : first + HALO].astype(F32)
            ext[at, c * TILE : (c + 1) * TILE] = x.astype(BF16)
    for c in to_slots:
        c.wait()

    def add_group(b, carry):
        for k in range(CAP):
            dose = dose_s[b, k]

            @pl.when(dose > 0.0)
            def _(k=k, dose=dose):
                x = got[b, k * TILE : (k + 1) * TILE].astype(F32)
                acc[tile_at(tile_s[b, CAP + k])] += splat_low(dose, (TILE, TILE)) * x

        return carry

    lax.fori_loop(0, N_TILE, add_group, 0)
    for j in range(N_ROW_BLOCKS):
        lo, hi = j * ROW_BLOCK, (j + 1) * ROW_BLOCK
        ext[HALO + lo : HALO + hi, :] = acc[lo:hi, :].astype(BF16)
    blank = jnp.zeros((HALO, STRIP - EXT_ROWS), BF16)
    for out, first, lane in ((left, 0, 0), (right, TILE - HALO, COLS - TILE)):
        strip = dot_nt(select_rows(first), ext[:, lane : lane + TILE]).astype(BF16)
        out[...] = jnp.concatenate([strip, blank], 1)


def middle_kernel(
    got, ext, info, tiles, table_hbm,
    local, own_num, sums, slot_dose, slot_tile, small,
    table, passed, nums, part, dose_s, tile_s, slot_sems, sems,
):
    to_rows = pltpu.make_async_copy(table_hbm.at[pl.ds(ROWS_PASS, 2 * TILE)], table.at[pl.ds(ROWS_PASS, 2 * TILE)], sems.at[0])
    to_cols = pltpu.make_async_copy(table_hbm.at[pl.ds(0, STRIPS)], table.at[pl.ds(0, STRIPS)], sems.at[1])
    to_small = pltpu.make_async_copy(table_hbm.at[pl.ds(SIDE_LEFT, 4 * TILE)], small, sems.at[2])
    to_slots = slot_copies(info, tiles, dose_s, tile_s, slot_sems)
    for c in (to_rows, to_cols, to_small) + to_slots:
        c.start()
    for s in range(SLOTS):
        x = got[s // CAP, (s % CAP) * TILE : (s % CAP + 1) * TILE].astype(F32)
        part[s] = jnp.sum(x.reshape(TILE // 8, 8, TILE), axis=0)
    to_rows.wait()
    for i in range(TR):
        lo, hi = i * TILE, (i + 1) * TILE
        both = jnp.dot(
            table[ROWS_PASS : ROWS_PASS + 2 * TILE, 0:ROWS_WINDOW],
            ext[lo : lo + ROWS_WINDOW, :],
            preferred_element_type=F32,
        )
        passed[0, lo:hi] = both[0:TILE].astype(BF16)
        passed[1, lo:hi] = both[TILE:].astype(BF16)
    to_cols.wait()
    lanes = iota((ROW_BLOCK, TILE), 1)
    for j in range(N_ROW_BLOCKS):
        lo, hi = ROW_BLOCK * j, ROW_BLOCK * (j + 1)
        for half in range(COLS // COL_BLOCK):
            own = slice(half * COL_BLOCK, (half + 1) * COL_BLOCK)
            if half == 0:
                beside, keep, first = slice(COL_BLOCK, COL_BLOCK + TILE), lanes < HALO, SIDE_LEFT
            else:
                beside, keep, first = slice(COL_BLOCK - TILE, COL_BLOCK), lanes >= TILE - HALO, SIDE_RIGHT
            narrow = jnp.where(keep, passed[0, lo:hi, beside].astype(F32), 0.0)
            dilated = jnp.where(keep, passed[1, lo:hi, beside].astype(F32), 0.0)
            side = (narrow + pltpu.roll(dilated, HALO, 1)).astype(BF16)
            result = jnp.dot(passed[0, lo:hi, own], table[OWN_NARROW : OWN_NARROW + COL_BLOCK, :], preferred_element_type=F32)
            result += jnp.dot(passed[1, lo:hi, own], table[OWN_DILATED : OWN_DILATED + COL_BLOCK, :], preferred_element_type=F32)
            result += jnp.dot(side, table[first : first + TILE, :], preferred_element_type=F32)
            local[lo:hi, own] = result
    for c in to_slots:
        c.wait()

    def see_group(b, carry):
        for k in range(CAP):
            s = b * CAP + k
            dose = dose_s[b, k]
            slot_dose[pl.ds(s, 1), :] = jnp.full((1, TILE), dose, F32)
            slot_tile[pl.ds(s, 1), :] = jnp.full((1, TILE), tile_s[b, CAP + k], jnp.int32)

            @pl.when(dose > 0.0)
            def _(k=k, s=s):
                x = got[b, k * TILE : (k + 1) * TILE].astype(F32)
                seen = local[tile_at(tile_s[b, CAP + k])] * x
                nums[s] = jnp.sum(seen.reshape(TILE // 8, 8, TILE), axis=0)

            @pl.when(dose <= 0.0)
            def _(s=s):
                nums[s] = jnp.ones((8, TILE), F32)

        return carry

    lax.fori_loop(0, N_TILE, see_group, 0)
    for out, parts in ((own_num, nums), (sums, part)):
        total = jnp.sum(jnp.sum(parts[...], axis=1), axis=1, keepdims=True)
        out[...] = jnp.broadcast_to(total, (SLOTS, TILE))
    to_small.wait()


def forward_kernel(
    back_got, before, after, back_own, local, own_num, sums, slot_dose, slot_tile, small, info, tiles, got,
    energy, new_dose, backscatter,
    windows, halo_left, halo_right, edge_left, edge_right, final, nums, dose_s, tile_s, slot_sems, out_sems,
):
    me = lax.axis_index("tile")
    to_slots = slot_copies(info, tiles, dose_s, tile_s, slot_sems)
    for c in to_slots:
        c.start()
    lane = iota((8, TILE), 1)
    row = iota((8, TILE), 0)
    own = (back_own[...] + back_got[...]) * (1.0 / back_norm())
    own = jnp.sum(jnp.where(iota((8, 32), 0) == me, own, 0.0), axis=0, keepdims=True)
    own = jnp.broadcast_to(own, (8, 32))
    small_row, small_lane = iota((8, 32), 0), iota((8, 32), 1)
    terms = []
    for c in range(TC):
        at = small_lane == small_row * TC + c
        term = jnp.sum(jnp.where(at, own, 0.0), axis=1, keepdims=True)
        terms.append(jnp.broadcast_to(term, (8, TILE)))
        backscatter[c : c + 1, :] = jnp.sum(jnp.where(lane == row, terms[c], 0.0), axis=0, keepdims=True)[:, 0:TR]
    for i in range(TR):
        at = slice(TILE * i, TILE * (i + 2))
        windows[HALO * i : HALO * (i + 1), :] = before[:, at]
        windows[HALO * (TR + i) : HALO * (TR + i + 1), :] = after[:, at]
    strips = jnp.dot(windows[...], small[STRIPS - SIDE_LEFT :, :], preferred_element_type=F32)
    blank = jnp.zeros((2 * HALO, TILE), F32)
    for side, (halo, edge) in enumerate(((halo_left, edge_left), (halo_right, edge_right))):
        for i in range(TR):
            both = strips[HALO * (side * TR + i) : HALO * (side * TR + i + 1), :]
            stacked = jnp.concatenate([blank, both[:, 0:TILE], both[:, TILE:], blank, blank], 0)
            halo[TILE * i : TILE * (i + 1), :] = stacked.T.astype(BF16)
        weights = small[side * TILE : (side + 1) * TILE, side * TILE : (side + 1) * TILE]
        edge[...] = jnp.dot(halo[...], weights, preferred_element_type=F32)
    out_copies = []
    for p in range(TR):
        rows = slice(p * TILE, (p + 1) * TILE)
        for c in range(TC):
            at = slice(c * TILE, (c + 1) * TILE)
            x = local[rows, at] + ETA_BACK * terms[c][p : p + 1]
            if c == 0:
                x = x + edge_left[rows, :]
            if c == TC - 1:
                x = x + edge_right[rows, :]
            final[rows, at] = x
        if p % 2 == 1:
            at = pl.ds((p - 1) * TILE, ROW_BLOCK)
            out_copies.append(pltpu.make_async_copy(final.at[at], energy.at[at], out_sems.at[p // 2]))
            out_copies[-1].start()
    for c in to_slots:
        c.wait()

    def see_group(b, carry):
        for k in range(CAP):
            s = b * CAP + k
            t = tile_s[b, CAP + k]
            live = dose_s[b, k] > 0.0
            column = t & (TC - 1)
            rows = pl.ds(pl.multiple_of((t >> 2) * TILE, TILE), TILE)
            nums[s] = jnp.zeros((8, TILE), F32)

            @pl.when(live & (column == 0))
            def _(k=k, s=s, rows=rows):
                x = got[b, k * TILE : (k + 1) * TILE].astype(F32) * edge_left[rows, :]
                nums[s] = jnp.sum(x.reshape(TILE // 8, 8, TILE), axis=0)

            @pl.when(live & (column == TC - 1))
            def _(k=k, s=s, rows=rows):
                x = got[b, k * TILE : (k + 1) * TILE].astype(F32) * edge_right[rows, :]
                nums[s] = jnp.sum(x.reshape(TILE // 8, 8, TILE), axis=0)

        return carry

    lax.fori_loop(0, N_TILE, see_group, 0)
    at_tile = slot_tile[:, 0:32] == iota((SLOTS, 32), 1)
    back = jnp.sum(jnp.where(at_tile, jnp.broadcast_to(own[0:1], (SLOTS, 32)), 0.0), axis=1, keepdims=True)
    num = jnp.sum(jnp.sum(nums[...], axis=1), axis=1, keepdims=True)
    total = sums[...]
    exposure = (own_num[...] + (num + (ETA_BACK * back) * total)) / total
    dose = slot_dose[...]
    corrected = jnp.where(dose > 0.0, dose * TARGET_DOSE / exposure, 0.0)
    at_slot = iota((SLOTS, TILE), 0) == iota((SLOTS, TILE), 1)
    new_dose[...] = jnp.sum(jnp.where(at_slot, corrected, 0.0), axis=0, keepdims=True)[:, 0:SLOTS]
    for copy in out_copies:
        copy.wait()


def spec(space):
    return pl.BlockSpec(memory_space=space)


VMEM, SMEM, HBM = pltpu.VMEM, pltpu.SMEM, pltpu.HBM
PACK_PARAMS = pltpu.CompilerParams(vmem_limit_bytes=64 * 2**20)
PARAMS = pltpu.CompilerParams(vmem_limit_bytes=24 * 2**20)


def cost(us):
    return pl.CostEstimate(flops=int(us * 1e9), bytes_accessed=int(us * 3e6), transcendentals=0)


def array(shape, dtype):
    return jax.ShapeDtypeStruct(shape, dtype)


def on_device(shot_blocks, shot_dose, shot_tile, shot_count):
    me_stripe = lax.axis_index("stripe").astype(jnp.int32).reshape(1)
    table = jnp.asarray(tables())
    groups = shot_blocks.reshape(N_TILE, BODY, TILE)

    message = pl.pallas_call(
        pack_kernel,
        out_shape=array((N_TILE, MESSAGE, TILE), BF16),
        in_specs=[spec(SMEM)] * 3 + [spec(HBM)],
        out_specs=spec(HBM),
        scratch_shapes=[
            pltpu.VMEM((N_TILE, BODY, TILE), BF16),
            pltpu.VMEM((N_TILE, 2, TC, HALO, TILE), F32),
            pltpu.VMEM((N_TILE, MESSAGE - BODY, TILE), BF16),
            pltpu.SemaphoreType.DMA((N_TILE,)),
            pltpu.SemaphoreType.DMA((2 * N_TILE,)),
        ],
        compiler_params=PACK_PARAMS,
        cost_estimate=cost(3.5),
        name="pack",
    )(shot_dose, shot_tile, shot_count, groups)
    got = lax.all_to_all(message, "tile", split_axis=0, concat_axis=0, tiled=True)

    back = pl.pallas_call(
        source_kernel,
        out_shape=array((8, 8, TILE), F32),
        in_specs=[spec(SMEM)] * 4 + [spec(HBM)],
        out_specs=spec(VMEM),
        scratch_shapes=[
            pltpu.VMEM((N_TILE, BODY, TILE), BF16),
            pltpu.VMEM((SLOTS, 8, TILE), F32),
            pltpu.VMEM((SLOTS, TILE), F32),
            pltpu.SemaphoreType.DMA((N_TILE,)),
        ],
        compiler_params=PARAMS,
        cost_estimate=cost(3),
        name="source",
    )(me_stripe, shot_dose, shot_tile, shot_count, groups)

    for bit in (1, 2, 4):
        half = back.shape[0] // 2
        sent = lax.ppermute(back[half:], "stripe", [(i, i ^ bit) for i in range(N_STRIPE)])
        back = back[:half] + sent
    back = back.reshape(8, TILE)
    sent = lax.ppermute(back, "stripe", [(i, i ^ 8) for i in range(N_STRIPE)])
    back = back[:, 0:64] + sent[:, 64:128]

    def swapped(x, stripe_bit, tile_bit):
        pairs = [
            (a * N_TILE + b, (a ^ stripe_bit) * N_TILE + (b ^ tile_bit))
            for a in range(N_STRIPE)
            for b in range(N_TILE)
        ]
        return lax.ppermute(x, ("stripe", "tile"), pairs)

    back = back[:, 0:32] + swapped(back, 16, 0)[:, 32:64] + swapped(back, 0, 4)[:, 0:32] + swapped(back, 16, 4)[:, 32:64]
    back, got = lax.optimization_barrier((back, got))
    back = back + swapped(back, 0, 1)
    back_got = swapped(back, 0, 3)

    pattern, left, right, info, tiles = pl.pallas_call(
        deposit_kernel,
        out_shape=(
            array((EXT_ROWS, COLS), BF16),
            array((HALO, STRIP), BF16),
            array((HALO, STRIP), BF16),
            array((N_TILE, TILE), F32),
            array((N_TILE, TILE), jnp.int32),
        ),
        in_specs=[spec(VMEM)],
        out_specs=(spec(VMEM),) * 5,
        scratch_shapes=[
            pltpu.VMEM((ROWS, COLS), F32),
            pltpu.SMEM((N_TILE, TILE), F32),
            pltpu.SMEM((N_TILE, TILE), jnp.int32),
            pltpu.SemaphoreType.DMA((2,)),
        ],
        compiler_params=PARAMS,
        cost_estimate=cost(2.5),
        name="deposit",
    )(got)

    ring_up = [(i, (i + 1) % N_STRIPE) for i in range(N_STRIPE)]
    before = lax.ppermute(right, "stripe", ring_up)
    after = lax.ppermute(left, "stripe", [(j, i) for i, j in ring_up])

    slots = array((SLOTS, TILE), F32)
    small_rows = ROWS_PASS - SIDE_LEFT
    local, own_num, sums, slot_dose, slot_tile, small = pl.pallas_call(
        middle_kernel,
        out_shape=(
            array((ROWS, COLS), F32),
            slots,
            slots,
            slots,
            array((SLOTS, TILE), jnp.int32),
            array((small_rows, COL_BLOCK), BF16),
        ),
        in_specs=[spec(VMEM)] * 4 + [spec(HBM)],
        out_specs=(spec(VMEM),) * 6,
        scratch_shapes=[
            pltpu.VMEM((TABLE_END, COL_BLOCK), BF16),
            pltpu.VMEM((2, ROWS, COLS), BF16),
            pltpu.VMEM((SLOTS, 8, TILE), F32),
            pltpu.VMEM((SLOTS, 8, TILE), F32),
            pltpu.SMEM((N_TILE, TILE), F32),
            pltpu.SMEM((N_TILE, TILE), jnp.int32),
            pltpu.SemaphoreType.DMA((2,)),
            pltpu.SemaphoreType.DMA((3,)),
        ],
        compiler_params=PARAMS,
        cost_estimate=cost(4),
        name="middle",
    )(got, pattern, info, tiles, table)

    energy, new_dose, backscatter = pl.pallas_call(
        forward_kernel,
        out_shape=(
            array((ROWS, COLS), F32),
            array((1, SLOTS), F32),
            array((TC, TR), F32),
        ),
        in_specs=[spec(VMEM)] * 13,
        out_specs=(spec(HBM), spec(VMEM), spec(VMEM)),
        scratch_shapes=[
            pltpu.VMEM((TR * 2 * HALO, 2 * TILE), BF16),
            pltpu.VMEM((ROWS, TILE), BF16),
            pltpu.VMEM((ROWS, TILE), BF16),
            pltpu.VMEM((ROWS, TILE), F32),
            pltpu.VMEM((ROWS, TILE), F32),
            pltpu.VMEM((ROWS, COLS), F32),
            pltpu.VMEM((SLOTS, 8, TILE), F32),
            pltpu.SMEM((N_TILE, TILE), F32),
            pltpu.SMEM((N_TILE, TILE), jnp.int32),
            pltpu.SemaphoreType.DMA((2,)),
            pltpu.SemaphoreType.DMA((N_ROW_BLOCKS,)),
        ],
        compiler_params=PARAMS,
        cost_estimate=cost(3),
        name="forward",
    )(back_got, before, after, back, local, own_num, sums, slot_dose, slot_tile, small, info, tiles, got)
    return energy, backscatter.T, new_dose.reshape(SLOTS)


def solution(mesh):
    in_specs = (
        P(("stripe", "tile"), None, None),
        P(("stripe", "tile")),
        P(("stripe", "tile")),
        P(("stripe", "tile")),
    )
    out_specs = (P("tile", "stripe"), P("tile", "stripe"), P(("stripe", "tile")))
    return jax.shard_map(
        on_device, mesh=mesh, in_specs=in_specs, out_specs=out_specs, check_vma=False
    )
```

```python
import jax
import jax.numpy as jnp
import numpy as np
import ml_dtypes
from jax import lax
from jax.experimental import pallas as pl
from jax.experimental.pallas import tpu as pltpu
from jax.sharding import PartitionSpec as P

TILE = 128
TR = 8
TC = 4
HALO = 16
CAP = 8
N_STRIPE = 32
RUN = 16
N_TILE = 8
SLOTS = N_TILE * CAP
ROWS = TR * TILE
COLS = TC * TILE
ROW_BLOCK = 256
COL_BLOCK = 256
EXT_ROWS = ROWS + 2 * HALO
STRIP = ROWS + TILE
BODY = CAP * TILE
EDGE = 2 * TC * HALO
INFO = BODY + EDGE
MESSAGE = INFO + HALO
N_ROW_BLOCKS = ROWS // ROW_BLOCK

ETA_BACK = 0.7
DILATED_WEIGHT = 0.5
TARGET_DOSE = 1.0
NARROW_SIGMA = 2.0
DILATED_SIGMA = 4.0
NXC = N_STRIPE * TC
NYC = N_TILE * TR
LOOP_SPREAD = NXC / 2.0
BAND_SPREAD = NYC / 5.0

F32 = jnp.float32
BF16 = jnp.bfloat16


def taps():
    offset = np.arange(-HALO, HALO + 1).astype(np.float32)
    narrow = np.exp(-offset * offset / np.float32(2.0 * NARROW_SIGMA**2))
    dilated = np.exp(-offset * offset / np.float32(8.0 * DILATED_SIGMA**2))
    dilated = np.where(np.arange(-HALO, HALO + 1) % 2 == 0, dilated, np.float32(0))
    narrow = (narrow / narrow.sum(dtype=np.float32)).astype(ml_dtypes.bfloat16)
    dilated = (dilated / dilated.sum(dtype=np.float32)).astype(ml_dtypes.bfloat16)
    return narrow.astype(np.float32), dilated.astype(np.float32)


def by_offset(table, offset):
    inside = np.abs(offset) <= HALO
    return np.where(inside, table[np.clip(offset + HALO, 0, 2 * HALO)], np.float32(0))


OWN_NARROW, OWN_DILATED, SIDE_LEFT, SIDE_RIGHT, STRIPS, ROWS_PASS = 0, 256, 512, 640, 768, 1024
TABLE_END = 1280
N_MIDDLE = 6
TABLE_ROWS = 5120
ROWS_WINDOW = TILE + 2 * HALO


def tables():
    narrow, dilated = taps()
    half = np.float32(DILATED_WEIGHT)
    table = np.zeros((TABLE_ROWS, COL_BLOCK), np.float32)
    q = np.arange(COL_BLOCK)[None, :]
    own = np.arange(COL_BLOCK)[:, None] - q
    table[OWN_NARROW : OWN_NARROW + COL_BLOCK] = by_offset(narrow, own)
    table[OWN_DILATED : OWN_DILATED + COL_BLOCK] = half * by_offset(dilated, own)
    n = np.arange(HALO)[:, None]
    before, after = n - HALO - q, n + COL_BLOCK - q
    left, right = table[SIDE_LEFT : SIDE_LEFT + TILE], table[SIDE_RIGHT : SIDE_RIGHT + TILE]
    left[0:HALO] = by_offset(narrow, after)
    left[HALO : 2 * HALO] = half * by_offset(dilated, after)
    left[2 * HALO : 3 * HALO] = by_offset(narrow, before)
    left[3 * HALO : 4 * HALO] = half * by_offset(dilated, before)
    right[TILE - HALO : TILE] = by_offset(narrow, before)
    right[0:HALO] = half * by_offset(dilated, before)
    right[2 * HALO : 3 * HALO] = by_offset(narrow, after)
    right[3 * HALO : 4 * HALO] = half * by_offset(dilated, after)
    j = np.arange(2 * TILE)[:, None]
    y = np.arange(TILE)[None, :]
    table[STRIPS : STRIPS + 2 * TILE, 0:TILE] = by_offset(narrow, j - HALO - y)
    table[STRIPS : STRIPS + 2 * TILE, TILE:] = by_offset(dilated, j - HALO - y)
    y = np.arange(TILE)[:, None]
    j = np.arange(ROWS_WINDOW)[None, :]
    table[ROWS_PASS : ROWS_PASS + TILE, 0:ROWS_WINDOW] = by_offset(narrow, j - HALO - y)
    table[ROWS_PASS + TILE : ROWS_PASS + 2 * TILE, 0:ROWS_WINDOW] = by_offset(dilated, j - HALO - y)
    return table.astype(ml_dtypes.bfloat16)


def back_norm():
    m = np.arange(NXC)
    m = np.minimum(m, NXC - m).astype(np.float64)
    sx = np.exp(-m * m / (2.0 * LOOP_SPREAD**2)).sum()
    o = np.arange(-(NYC - 1), NYC).astype(np.float64)
    sy = np.exp(-o * o / (2.0 * BAND_SPREAD**2)).sum()
    return float(sx * sy)


def iota(shape, dim):
    return lax.broadcasted_iota(jnp.int32, shape, dim)


def splat_low(value, shape):
    return jnp.full(shape, value, F32).astype(BF16).astype(F32)


def pack_kernel(dose_hbm, tile_hbm, count_hbm, groups, out, buf, edge, tail, dose_ref, tile_ref, count_ref, in_sems, out_sems, slot_sems):
    reads, writes = [], []
    for d in range(N_TILE):
        reads.append(pltpu.make_async_copy(groups.at[d], buf.at[d], in_sems.at[d]))
        writes.append(pltpu.make_async_copy(buf.at[d], out.at[d, pl.ds(0, BODY)], out_sems.at[d]))
    scalars = []
    for n, (source, target) in enumerate(((dose_hbm, dose_ref), (tile_hbm, tile_ref), (count_hbm, count_ref))):
        scalars.append(pltpu.make_async_copy(source, target, slot_sems.at[n]))
    for c in reads[:1] + scalars + reads[1:]:
        c.start()
    edge[...] = jnp.zeros_like(edge)
    row = iota((8, TILE), 0)
    lane = iota((8, TILE), 1)
    for c in scalars:
        c.wait()

    def add_info(s, acc):
        d = s >> 3
        k = s & (CAP - 1)
        dose = jnp.where(k < count_ref[d], dose_ref[s], 0.0)
        tile = jnp.full((8, TILE), tile_ref[s], jnp.int32).astype(F32)
        acc = jnp.where((row == d) & (lane == k), dose, acc)
        return jnp.where((row == d) & (lane == k + CAP), tile, acc)

    info = lax.fori_loop(0, SLOTS, add_info, jnp.zeros((8, TILE), F32), unroll=8)
    high = info.astype(BF16).astype(F32)
    middle = (info - high).astype(BF16).astype(F32)
    lowest = info - high - middle
    row = iota((HALO, TILE), 0)
    for d in range(N_TILE):
        at = slice(d, d + 1)
        rows = jnp.where(row == 0, high[at], jnp.where(row == 1, middle[at], jnp.where(row == 2, lowest[at], 0.0)))
        tail[d, EDGE:] = rows.astype(BF16)
    half = EDGE // 2
    blank = jnp.zeros((half, TILE), BF16)

    def send_tail(d):
        above = edge[d - 1, 1].reshape(half, TILE).astype(BF16) if d > 0 else blank
        below = edge[d + 1, 0].reshape(half, TILE).astype(BF16) if d < N_TILE - 1 else blank
        tail[d, 0:half] = above
        tail[d, half:EDGE] = below
        writes.append(
            pltpu.make_async_copy(tail.at[d], out.at[d, pl.ds(BODY, MESSAGE - BODY)], out_sems.at[N_TILE + d])
        )
        writes[-1].start()

    for d in range(N_TILE):
        reads[d].wait()
        writes[d].start()

        def add_edges(k, carry, d=d):
            s = d * CAP + k
            t = tile_ref[s]
            live = k < count_ref[d]
            c = t & (TC - 1)
            first = pl.multiple_of(k * TILE, TILE)

            at_bottom = t >= TC * (TR - 1)

            @pl.when(live & ((t < TC) | at_bottom))
            def _():
                side = jnp.where(at_bottom, 1, 0)
                at = pl.multiple_of(first + side * (TILE - HALO), HALO)
                x = buf[d, pl.ds(at, HALO), :].astype(F32)
                edge[d, side, c] += splat_low(dose_ref[s], (HALO, TILE)) * x

            return carry

        lax.fori_loop(0, CAP, add_edges, 0)
        if d > 0:
            send_tail(d - 1)
    send_tail(N_TILE - 1)
    for c in writes:
        c.wait()


def source_kernel(me_ref, dose_ref, tile_ref, count_ref, groups, out, buf, part, total, sems):
    me = me_ref[0]
    copies = [pltpu.make_async_copy(groups.at[d], buf.at[d], sems.at[d]) for d in range(N_TILE)]
    for c in copies:
        c.start()
    for d in range(N_TILE):
        copies[d].wait()
        for k in range(CAP):
            x = buf[d, k * TILE : (k + 1) * TILE].astype(F32)
            part[d * CAP + k] = jnp.sum(x.reshape(TILE // 8, 8, TILE), axis=0)
    sums = jnp.sum(jnp.sum(part[...], axis=1), axis=1, keepdims=True) * (1.0 / (TILE * TILE))
    total[...] = jnp.broadcast_to(sums, (SLOTS, TILE))
    row = iota((8, TILE), 0)
    lane = iota((8, TILE), 1)
    target_row = row * TR + ((lane & 31) >> 2)
    column = lane >> 5

    def add_slot(s, acc):
        d = s >> 3
        t = tile_ref[s]
        dose = jnp.where((s & (CAP - 1)) < count_ref[d], dose_ref[s], 0.0)
        value = jnp.broadcast_to(total[pl.ds(s, 1), :], (8, TILE))
        gap = (target_row - (d * TR + (t >> 2))).astype(F32)
        across = jnp.exp(gap * gap * (-1.0 / (2.0 * BAND_SPREAD**2)))
        return acc + jnp.where(column == (t & (TC - 1)), across * (splat_low(dose, (8, TILE)) * value), 0.0)

    acc = lax.fori_loop(0, SLOTS, add_slot, jnp.zeros((8, TILE), F32), unroll=8)
    for i in range(8):
        low_bits = ((i >> 2) & 1) + (i & 2) + 4 * (i & 1)
        result = jnp.zeros((8, TILE), F32)
        for g in range(4):
            r = low_bits + 8 * (g >> 1) + 16 * (g & 1)
            gap = jnp.abs(me * TC + column - ((me ^ r) * TC + (lane & (TC - 1))))
            gap = jnp.minimum(gap, NXC - gap).astype(F32)
            x = acc * jnp.exp(gap * gap * (-1.0 / (2.0 * LOOP_SPREAD**2)))
            x = x + pltpu.roll(x, 64, 1)
            x = x + pltpu.roll(x, 32, 1)
            result = jnp.where(column == g, x, result)
        out[i] = result


def select_rows(first):
    r = iota((HALO, TILE), 0)
    c = iota((HALO, TILE), 1)
    return jnp.where(c == r + first, 1.0, 0.0).astype(BF16)


def dot_nt(a, b):
    return lax.dot_general(a, b, (((1,), (1,)), ((), ())), preferred_element_type=F32)


def tile_at(t):
    at_row = pl.ds(pl.multiple_of((t >> 2) * TILE, TILE), TILE)
    at_col = pl.ds(pl.multiple_of((t & (TC - 1)) * TILE, TILE), TILE)
    return at_row, at_col


def decode(got):
    rows = []
    for b in range(N_TILE):
        x = got[b, INFO:MESSAGE].astype(F32)
        rows.append(x[0:1] + x[1:2] + x[2:3])
    return jnp.concatenate(rows, 0)


def slot_copies(info, tiles, dose_s, tile_s, sems):
    return (
        pltpu.make_async_copy(info, dose_s, sems.at[0]),
        pltpu.make_async_copy(tiles, tile_s, sems.at[1]),
    )


def deposit_kernel(got, ext, left, right, info, tiles, acc, dose_s, tile_s, sems):
    values = decode(got)
    info[...] = values
    tiles[...] = values.astype(jnp.int32)
    to_slots = slot_copies(info, tiles, dose_s, tile_s, sems)
    for c in to_slots:
        c.start()
    acc[...] = jnp.zeros_like(acc)
    for side in range(2):
        at = slice(0, HALO) if side == 0 else slice(EXT_ROWS - HALO, EXT_ROWS)
        for c in range(TC):
            first = BODY + (side * TC + c) * HALO
            x = got[0, first : first + HALO].astype(F32)
            for b in range(1, N_TILE):
                x = x + got[b, first : first + HALO].astype(F32)
            ext[at, c * TILE : (c + 1) * TILE] = x.astype(BF16)
    for c in to_slots:
        c.wait()

    def add_group(b, carry):
        for k in range(CAP):
            dose = dose_s[b, k]

            x = got[b, k * TILE : (k + 1) * TILE].astype(F32)
            acc[tile_at(tile_s[b, CAP + k])] += splat_low(dose, (TILE, TILE)) * x

        return carry

    lax.fori_loop(0, N_TILE, add_group, 0)
    for j in range(N_ROW_BLOCKS):
        lo, hi = j * ROW_BLOCK, (j + 1) * ROW_BLOCK
        ext[HALO + lo : HALO + hi, :] = acc[lo:hi, :].astype(BF16)
    blank = jnp.zeros((HALO, STRIP - EXT_ROWS), BF16)
    for out, first, lane in ((left, 0, 0), (right, TILE - HALO, COLS - TILE)):
        strip = dot_nt(select_rows(first), ext[:, lane : lane + TILE]).astype(BF16)
        out[...] = jnp.concatenate([strip, blank], 1)


def first_of_run():
    return lax.rem(lax.axis_index("stripe"), RUN) == 0


def early_kernel(got, ext, info, tiles, table_hbm, left, _, *rest):
    left_out = rest[N_MIDDLE]
    left_out[...] = left[...]
    pl.when(first_of_run())(lambda: middle_kernel(got, ext, info, tiles, table_hbm, *rest[:N_MIDDLE], *rest[N_MIDDLE + 1 :]))


def late_kernel(got, ext, info, tiles, table_hbm, *rest):
    pl.when(~first_of_run())(lambda: middle_kernel(got, ext, info, tiles, table_hbm, *rest[N_MIDDLE:]))


def middle_kernel(
    got, ext, info, tiles, table_hbm,
    local, own_num, sums, slot_dose, slot_tile, small,
    table, passed, nums, part, dose_s, tile_s, slot_sems, sems,
):
    to_rows = pltpu.make_async_copy(table_hbm.at[pl.ds(ROWS_PASS, 2 * TILE)], table.at[pl.ds(ROWS_PASS, 2 * TILE)], sems.at[0])
    to_cols = pltpu.make_async_copy(table_hbm.at[pl.ds(0, STRIPS)], table.at[pl.ds(0, STRIPS)], sems.at[1])
    to_small = pltpu.make_async_copy(table_hbm.at[pl.ds(SIDE_LEFT, 4 * TILE)], small, sems.at[2])
    to_slots = slot_copies(info, tiles, dose_s, tile_s, slot_sems)
    for c in (to_rows, to_cols, to_small) + to_slots:
        c.start()
    for s in range(SLOTS):
        x = got[s // CAP, (s % CAP) * TILE : (s % CAP + 1) * TILE].astype(F32)
        part[s] = jnp.sum(x.reshape(TILE // 8, 8, TILE), axis=0)
    to_rows.wait()
    for i in range(TR):
        lo, hi = i * TILE, (i + 1) * TILE
        both = jnp.dot(
            table[ROWS_PASS : ROWS_PASS + 2 * TILE, 0:ROWS_WINDOW],
            ext[lo : lo + ROWS_WINDOW, :],
            preferred_element_type=F32,
        )
        passed[0, lo:hi] = both[0:TILE].astype(BF16)
        passed[1, lo:hi] = both[TILE:].astype(BF16)
    to_cols.wait()
    lanes = iota((ROW_BLOCK, TILE), 1)
    for j in range(N_ROW_BLOCKS):
        lo, hi = ROW_BLOCK * j, ROW_BLOCK * (j + 1)
        for half in range(COLS // COL_BLOCK):
            own = slice(half * COL_BLOCK, (half + 1) * COL_BLOCK)
            if half == 0:
                beside, keep, first = slice(COL_BLOCK, COL_BLOCK + TILE), lanes < HALO, SIDE_LEFT
            else:
                beside, keep, first = slice(COL_BLOCK - TILE, COL_BLOCK), lanes >= TILE - HALO, SIDE_RIGHT
            narrow = jnp.where(keep, passed[0, lo:hi, beside].astype(F32), 0.0)
            dilated = jnp.where(keep, passed[1, lo:hi, beside].astype(F32), 0.0)
            side = (narrow + pltpu.roll(dilated, HALO, 1)).astype(BF16)
            result = jnp.dot(passed[0, lo:hi, own], table[OWN_NARROW : OWN_NARROW + COL_BLOCK, :], preferred_element_type=F32)
            result += jnp.dot(passed[1, lo:hi, own], table[OWN_DILATED : OWN_DILATED + COL_BLOCK, :], preferred_element_type=F32)
            result += jnp.dot(side, table[first : first + TILE, :], preferred_element_type=F32)
            local[lo:hi, own] = result
    for c in to_slots:
        c.wait()

    def see_group(b, carry):
        for k in range(CAP):
            s = b * CAP + k
            dose = dose_s[b, k]
            slot_dose[pl.ds(s, 1), :] = jnp.full((1, TILE), dose, F32)
            slot_tile[pl.ds(s, 1), :] = jnp.full((1, TILE), tile_s[b, CAP + k], jnp.int32)

            x = got[b, k * TILE : (k + 1) * TILE].astype(F32)
            seen = local[tile_at(tile_s[b, CAP + k])] * x
            nums[s] = jnp.sum(seen.reshape(TILE // 8, 8, TILE), axis=0)

        return carry

    lax.fori_loop(0, N_TILE, see_group, 0)
    for out, parts in ((own_num, nums), (sums, part)):
        total = jnp.sum(jnp.sum(parts[...], axis=1), axis=1, keepdims=True)
        out[...] = jnp.broadcast_to(total, (SLOTS, TILE))
    to_small.wait()


def forward_kernel(
    back_got, before, after, back_own, local, own_num, sums, slot_dose, slot_tile, small, info, tiles, got,
    energy, new_dose, backscatter,
    windows, halo_left, halo_right, edge_left, edge_right, final, nums, dose_s, tile_s, slot_sems, out_sems,
):
    me = lax.axis_index("tile")
    to_slots = slot_copies(info, tiles, dose_s, tile_s, slot_sems)
    for c in to_slots:
        c.start()
    lane = iota((8, TILE), 1)
    row = iota((8, TILE), 0)
    own = (back_own[...] + back_got[...]) * (1.0 / back_norm())
    own = jnp.sum(jnp.where(iota((8, 32), 0) == me, own, 0.0), axis=0, keepdims=True)
    own = jnp.broadcast_to(own, (8, 32))
    small_row, small_lane = iota((8, 32), 0), iota((8, 32), 1)
    terms = []
    for c in range(TC):
        at = small_lane == small_row * TC + c
        term = jnp.sum(jnp.where(at, own, 0.0), axis=1, keepdims=True)
        terms.append(jnp.broadcast_to(term, (8, TILE)))
        backscatter[c : c + 1, :] = jnp.sum(jnp.where(lane == row, terms[c], 0.0), axis=0, keepdims=True)[:, 0:TR]
    for i in range(TR):
        at = slice(TILE * i, TILE * (i + 2))
        windows[HALO * i : HALO * (i + 1), :] = before[:, at]
        windows[HALO * (TR + i) : HALO * (TR + i + 1), :] = after[:, at]
    strips = jnp.dot(windows[...], small[STRIPS - SIDE_LEFT :, :], preferred_element_type=F32)
    blank = jnp.zeros((2 * HALO, TILE), F32)
    for side, (halo, edge) in enumerate(((halo_left, edge_left), (halo_right, edge_right))):
        for i in range(TR):
            both = strips[HALO * (side * TR + i) : HALO * (side * TR + i + 1), :]
            stacked = jnp.concatenate([blank, both[:, 0:TILE], both[:, TILE:], blank, blank], 0)
            halo[TILE * i : TILE * (i + 1), :] = stacked.T.astype(BF16)
        weights = small[side * TILE : (side + 1) * TILE, side * TILE : (side + 1) * TILE]
        edge[...] = jnp.dot(halo[...], weights, preferred_element_type=F32)
    out_copies = []
    for p in range(TR):
        rows = slice(p * TILE, (p + 1) * TILE)
        for c in range(TC):
            at = slice(c * TILE, (c + 1) * TILE)
            x = local[rows, at] + ETA_BACK * terms[c][p : p + 1]
            if c == 0:
                x = x + edge_left[rows, :]
            if c == TC - 1:
                x = x + edge_right[rows, :]
            final[rows, at] = x
        if p % 2 == 1:
            at = pl.ds((p - 1) * TILE, 2 * TILE)
            out_copies.append(pltpu.make_async_copy(final.at[at], energy.at[at], out_sems.at[p]))
            out_copies[-1].start()
    for c in to_slots:
        c.wait()

    def see_group(b, carry):
        for k in range(CAP):
            s = b * CAP + k
            t = tile_s[b, CAP + k]
            live = dose_s[b, k] > 0.0
            column = t & (TC - 1)
            rows = pl.ds(pl.multiple_of((t >> 2) * TILE, TILE), TILE)
            nums[s] = jnp.zeros((8, TILE), F32)

            @pl.when(live & (column == 0))
            def _(k=k, s=s, rows=rows):
                x = got[b, k * TILE : (k + 1) * TILE].astype(F32) * edge_left[rows, :]
                nums[s] = jnp.sum(x.reshape(TILE // 8, 8, TILE), axis=0)

            @pl.when(live & (column == TC - 1))
            def _(k=k, s=s, rows=rows):
                x = got[b, k * TILE : (k + 1) * TILE].astype(F32) * edge_right[rows, :]
                nums[s] = jnp.sum(x.reshape(TILE // 8, 8, TILE), axis=0)

        return carry

    lax.fori_loop(0, N_TILE, see_group, 0)
    at_tile = slot_tile[:, 0:32] == iota((SLOTS, 32), 1)
    back = jnp.sum(jnp.where(at_tile, jnp.broadcast_to(own[0:1], (SLOTS, 32)), 0.0), axis=1, keepdims=True)
    num = jnp.sum(jnp.sum(nums[...], axis=1), axis=1, keepdims=True)
    total = sums[...]
    exposure = (own_num[...] + (num + (ETA_BACK * back) * total)) / total
    dose = slot_dose[...]
    corrected = jnp.where(dose > 0.0, dose * TARGET_DOSE / exposure, 0.0)
    at_slot = iota((SLOTS, TILE), 0) == iota((SLOTS, TILE), 1)
    new_dose[...] = jnp.sum(jnp.where(at_slot, corrected, 0.0), axis=0, keepdims=True)[:, 0:SLOTS]
    for copy in out_copies:
        copy.wait()


def spec(space):
    return pl.BlockSpec(memory_space=space)


VMEM, SMEM, HBM = pltpu.VMEM, pltpu.SMEM, pltpu.HBM
PACK_PARAMS = pltpu.CompilerParams(vmem_limit_bytes=64 * 2**20)
PARAMS = pltpu.CompilerParams(vmem_limit_bytes=24 * 2**20)


def cost(us):
    return pl.CostEstimate(flops=int(us * 1e9), bytes_accessed=int(us * 3e6), transcendentals=0)


def array(shape, dtype):
    return jax.ShapeDtypeStruct(shape, dtype)


def on_device(shot_blocks, shot_dose, shot_tile, shot_count):
    me_stripe = lax.axis_index("stripe").astype(jnp.int32).reshape(1)
    table = jnp.asarray(tables())
    groups = shot_blocks.reshape(N_TILE, BODY, TILE)

    message = pl.pallas_call(
        pack_kernel,
        out_shape=array((N_TILE, MESSAGE, TILE), BF16),
        in_specs=[spec(HBM)] * 4,
        out_specs=spec(HBM),
        scratch_shapes=[
            pltpu.VMEM((N_TILE, BODY, TILE), BF16),
            pltpu.VMEM((N_TILE, 2, TC, HALO, TILE), F32),
            pltpu.VMEM((N_TILE, MESSAGE - BODY, TILE), BF16),
            pltpu.SMEM((SLOTS,), F32),
            pltpu.SMEM((SLOTS,), jnp.int32),
            pltpu.SMEM((N_TILE,), jnp.int32),
            pltpu.SemaphoreType.DMA((N_TILE,)),
            pltpu.SemaphoreType.DMA((2 * N_TILE,)),
            pltpu.SemaphoreType.DMA((3,)),
        ],
        compiler_params=PACK_PARAMS,
        cost_estimate=cost(3.5),
        name="pack",
    )(shot_dose, shot_tile, shot_count, groups)
    got = lax.all_to_all(message, "tile", split_axis=0, concat_axis=0, tiled=True)

    back = pl.pallas_call(
        source_kernel,
        out_shape=array((8, 8, TILE), F32),
        in_specs=[spec(SMEM)] * 4 + [spec(HBM)],
        out_specs=spec(VMEM),
        scratch_shapes=[
            pltpu.VMEM((N_TILE, BODY, TILE), BF16),
            pltpu.VMEM((SLOTS, 8, TILE), F32),
            pltpu.VMEM((SLOTS, TILE), F32),
            pltpu.SemaphoreType.DMA((N_TILE,)),
        ],
        compiler_params=PARAMS,
        cost_estimate=cost(3),
        name="source",
    )(me_stripe, shot_dose, shot_tile, shot_count, groups)

    for bit in (1, 2, 4):
        half = back.shape[0] // 2
        sent = lax.ppermute(back[half:], "stripe", [(i, i ^ bit) for i in range(N_STRIPE)])
        back = back[:half] + sent
    back = back.reshape(8, TILE)
    sent = lax.ppermute(back, "stripe", [(i, i ^ 8) for i in range(N_STRIPE)])
    back = back[:, 0:64] + sent[:, 64:128]

    def swapped(x, stripe_bit, tile_bit):
        pairs = [
            (a * N_TILE + b, (a ^ stripe_bit) * N_TILE + (b ^ tile_bit))
            for a in range(N_STRIPE)
            for b in range(N_TILE)
        ]
        return lax.ppermute(x, ("stripe", "tile"), pairs)

    back = back[:, 0:32] + swapped(back, 16, 0)[:, 32:64] + swapped(back, 0, 4)[:, 0:32] + swapped(back, 16, 4)[:, 32:64]
    back, got = lax.optimization_barrier((back, got))
    back = back + swapped(back, 0, 1)
    back_got = swapped(back, 0, 3)

    pattern, left, right, info, tiles = pl.pallas_call(
        deposit_kernel,
        out_shape=(
            array((EXT_ROWS, COLS), BF16),
            array((HALO, STRIP), BF16),
            array((HALO, STRIP), BF16),
            array((N_TILE, TILE), F32),
            array((N_TILE, TILE), jnp.int32),
        ),
        in_specs=[spec(VMEM)],
        out_specs=(spec(VMEM),) * 5,
        scratch_shapes=[
            pltpu.VMEM((ROWS, COLS), F32),
            pltpu.SMEM((N_TILE, TILE), F32),
            pltpu.SMEM((N_TILE, TILE), jnp.int32),
            pltpu.SemaphoreType.DMA((2,)),
        ],
        compiler_params=PARAMS,
        cost_estimate=cost(2.5),
        name="deposit",
    )(got)

    ring_up = [(i, (i + 1) % N_STRIPE) for i in range(N_STRIPE)]
    before = lax.ppermute(right, "stripe", ring_up)

    slots = array((SLOTS, TILE), F32)
    results = (
        array((ROWS, COLS), F32),
        slots,
        slots,
        slots,
        array((SLOTS, TILE), jnp.int32),
        array((ROWS_PASS - SIDE_LEFT, COL_BLOCK), BF16),
    )
    scratch = [
        pltpu.VMEM((TABLE_END, COL_BLOCK), BF16),
        pltpu.VMEM((2, ROWS, COLS), BF16),
        pltpu.VMEM((SLOTS, 8, TILE), F32),
        pltpu.VMEM((SLOTS, 8, TILE), F32),
        pltpu.SMEM((N_TILE, TILE), F32),
        pltpu.SMEM((N_TILE, TILE), jnp.int32),
        pltpu.SemaphoreType.DMA((2,)),
        pltpu.SemaphoreType.DMA((3,)),
    ]
    *early, left = pl.pallas_call(
        early_kernel,
        out_shape=results + (array((HALO, STRIP), BF16),),
        in_specs=[spec(VMEM)] * 4 + [spec(HBM)] + [spec(VMEM)] * 2,
        out_specs=(spec(VMEM),) * (N_MIDDLE + 1),
        scratch_shapes=scratch,
        compiler_params=PARAMS,
        cost_estimate=cost(4),
        name="early",
    )(got, pattern, info, tiles, table, left, back)
    after = lax.ppermute(left, "stripe", [(j, i) for i, j in ring_up])
    local, own_num, sums, slot_dose, slot_tile, small = pl.pallas_call(
        late_kernel,
        out_shape=results,
        in_specs=[spec(VMEM)] * 4 + [spec(HBM)] + [spec(VMEM)] * N_MIDDLE,
        out_specs=(spec(VMEM),) * N_MIDDLE,
        scratch_shapes=scratch,
        input_output_aliases={5 + n: n for n in range(N_MIDDLE)},
        compiler_params=PARAMS,
        cost_estimate=cost(0),
        name="late",
    )(got, pattern, info, tiles, table, *early)

    energy, new_dose, backscatter = pl.pallas_call(
        forward_kernel,
        out_shape=(
            array((ROWS, COLS), F32),
            array((1, SLOTS), F32),
            array((TC, TR), F32),
        ),
        in_specs=[spec(VMEM)] * 13,
        out_specs=(spec(HBM), spec(VMEM), spec(VMEM)),
        scratch_shapes=[
            pltpu.VMEM((TR * 2 * HALO, 2 * TILE), BF16),
            pltpu.VMEM((ROWS, TILE), BF16),
            pltpu.VMEM((ROWS, TILE), BF16),
            pltpu.VMEM((ROWS, TILE), F32),
            pltpu.VMEM((ROWS, TILE), F32),
            pltpu.VMEM((ROWS, COLS), F32),
            pltpu.VMEM((SLOTS, 8, TILE), F32),
            pltpu.SMEM((N_TILE, TILE), F32),
            pltpu.SMEM((N_TILE, TILE), jnp.int32),
            pltpu.SemaphoreType.DMA((2,)),
            pltpu.SemaphoreType.DMA((TR,)),
        ],
        compiler_params=PARAMS,
        cost_estimate=cost(3),
        name="forward",
    )(back_got, before, after, back, local, own_num, sums, slot_dose, slot_tile, small, info, tiles, got)
    return energy, backscatter.T, new_dose.reshape(SLOTS)


def solution(mesh):
    in_specs = (
        P(("stripe", "tile"), None, None),
        P(("stripe", "tile")),
        P(("stripe", "tile")),
        P(("stripe", "tile")),
    )
    out_specs = (P("tile", "stripe"), P("tile", "stripe"), P(("stripe", "tile")))
    return jax.shard_map(
        on_device, mesh=mesh, in_specs=in_specs, out_specs=out_specs, check_vma=False
    )
```

```python
import jax
import jax.numpy as jnp
import numpy as np
import ml_dtypes
from jax import lax
from jax.experimental import pallas as pl
from jax.experimental.pallas import tpu as pltpu
from jax.sharding import PartitionSpec as P

TILE = 128
TR = 8
TC = 4
HALO = 16
CAP = 8
N_STRIPE = 32
RUN = 16
N_TILE = 8
SLOTS = N_TILE * CAP
ROWS = TR * TILE
COLS = TC * TILE
ROW_BLOCK = 256
COL_BLOCK = 256
EXT_ROWS = ROWS + 2 * HALO
STRIP = ROWS + TILE
BODY = CAP * TILE
EDGE = 2 * TC * HALO
INFO = BODY + EDGE
MESSAGE = INFO + HALO
N_ROW_BLOCKS = ROWS // ROW_BLOCK

ETA_BACK = 0.7
DILATED_WEIGHT = 0.5
TARGET_DOSE = 1.0
NARROW_SIGMA = 2.0
DILATED_SIGMA = 4.0
NXC = N_STRIPE * TC
NYC = N_TILE * TR
LOOP_SPREAD = NXC / 2.0
BAND_SPREAD = NYC / 5.0

F32 = jnp.float32
BF16 = jnp.bfloat16


def taps():
    offset = np.arange(-HALO, HALO + 1).astype(np.float32)
    narrow = np.exp(-offset * offset / np.float32(2.0 * NARROW_SIGMA**2))
    dilated = np.exp(-offset * offset / np.float32(8.0 * DILATED_SIGMA**2))
    dilated = np.where(np.arange(-HALO, HALO + 1) % 2 == 0, dilated, np.float32(0))
    narrow = (narrow / narrow.sum(dtype=np.float32)).astype(ml_dtypes.bfloat16)
    dilated = (dilated / dilated.sum(dtype=np.float32)).astype(ml_dtypes.bfloat16)
    return narrow.astype(np.float32), dilated.astype(np.float32)


def by_offset(table, offset):
    inside = np.abs(offset) <= HALO
    return np.where(inside, table[np.clip(offset + HALO, 0, 2 * HALO)], np.float32(0))


OWN_NARROW, OWN_DILATED, SIDE_LEFT, SIDE_RIGHT, STRIPS, ROWS_PASS = 0, 256, 512, 640, 768, 1024
TABLE_END = 1280
N_MIDDLE = 6
TABLE_ROWS = 5120
ROWS_WINDOW = TILE + 2 * HALO


def tables():
    narrow, dilated = taps()
    half = np.float32(DILATED_WEIGHT)
    table = np.zeros((TABLE_ROWS, COL_BLOCK), np.float32)
    q = np.arange(COL_BLOCK)[None, :]
    own = np.arange(COL_BLOCK)[:, None] - q
    table[OWN_NARROW : OWN_NARROW + COL_BLOCK] = by_offset(narrow, own)
    table[OWN_DILATED : OWN_DILATED + COL_BLOCK] = half * by_offset(dilated, own)
    n = np.arange(HALO)[:, None]
    before, after = n - HALO - q, n + COL_BLOCK - q
    left, right = table[SIDE_LEFT : SIDE_LEFT + TILE], table[SIDE_RIGHT : SIDE_RIGHT + TILE]
    left[0:HALO] = by_offset(narrow, after)
    left[HALO : 2 * HALO] = half * by_offset(dilated, after)
    left[2 * HALO : 3 * HALO] = by_offset(narrow, before)
    left[3 * HALO : 4 * HALO] = half * by_offset(dilated, before)
    right[TILE - HALO : TILE] = by_offset(narrow, before)
    right[0:HALO] = half * by_offset(dilated, before)
    right[2 * HALO : 3 * HALO] = by_offset(narrow, after)
    right[3 * HALO : 4 * HALO] = half * by_offset(dilated, after)
    j = np.arange(2 * TILE)[:, None]
    y = np.arange(TILE)[None, :]
    table[STRIPS : STRIPS + 2 * TILE, 0:TILE] = by_offset(narrow, j - HALO - y)
    table[STRIPS : STRIPS + 2 * TILE, TILE:] = by_offset(dilated, j - HALO - y)
    y = np.arange(TILE)[:, None]
    j = np.arange(ROWS_WINDOW)[None, :]
    table[ROWS_PASS : ROWS_PASS + TILE, 0:ROWS_WINDOW] = by_offset(narrow, j - HALO - y)
    table[ROWS_PASS + TILE : ROWS_PASS + 2 * TILE, 0:ROWS_WINDOW] = by_offset(dilated, j - HALO - y)
    return table.astype(ml_dtypes.bfloat16)


def back_norm():
    m = np.arange(NXC)
    m = np.minimum(m, NXC - m).astype(np.float64)
    sx = np.exp(-m * m / (2.0 * LOOP_SPREAD**2)).sum()
    o = np.arange(-(NYC - 1), NYC).astype(np.float64)
    sy = np.exp(-o * o / (2.0 * BAND_SPREAD**2)).sum()
    return float(sx * sy)


def iota(shape, dim):
    return lax.broadcasted_iota(jnp.int32, shape, dim)


def splat_low(value, shape):
    return jnp.full(shape, value, F32).astype(BF16).astype(F32)


def pack_kernel(dose_hbm, tile_hbm, count_hbm, groups, out, buf, edge, tail, dose_ref, tile_ref, count_ref, in_sems, out_sems, slot_sems):
    reads, writes = [], []
    for d in range(N_TILE):
        reads.append(pltpu.make_async_copy(groups.at[d], buf.at[d], in_sems.at[d]))
        writes.append(pltpu.make_async_copy(buf.at[d], out.at[d, pl.ds(0, BODY)], out_sems.at[d]))
    scalars = []
    for n, (source, target) in enumerate(((dose_hbm, dose_ref), (tile_hbm, tile_ref), (count_hbm, count_ref))):
        scalars.append(pltpu.make_async_copy(source, target, slot_sems.at[n]))
    for c in reads[:1] + scalars + reads[1:]:
        c.start()
    edge[...] = jnp.zeros_like(edge)
    row = iota((8, TILE), 0)
    lane = iota((8, TILE), 1)
    for c in scalars:
        c.wait()

    def add_info(s, acc):
        d = s >> 3
        k = s & (CAP - 1)
        dose = jnp.where(k < count_ref[d], dose_ref[s], 0.0)
        tile = jnp.full((8, TILE), tile_ref[s], jnp.int32).astype(F32)
        acc = jnp.where((row == d) & (lane == k), dose, acc)
        return jnp.where((row == d) & (lane == k + CAP), tile, acc)

    info = lax.fori_loop(0, SLOTS, add_info, jnp.zeros((8, TILE), F32), unroll=8)
    high = info.astype(BF16).astype(F32)
    middle = (info - high).astype(BF16).astype(F32)
    lowest = info - high - middle
    row = iota((HALO, TILE), 0)
    for d in range(N_TILE):
        at = slice(d, d + 1)
        rows = jnp.where(row == 0, high[at], jnp.where(row == 1, middle[at], jnp.where(row == 2, lowest[at], 0.0)))
        tail[d, EDGE:] = rows.astype(BF16)
    half = EDGE // 2
    blank = jnp.zeros((half, TILE), BF16)

    def send_tail(d):
        above = edge[d - 1, 1].reshape(half, TILE).astype(BF16) if d > 0 else blank
        below = edge[d + 1, 0].reshape(half, TILE).astype(BF16) if d < N_TILE - 1 else blank
        tail[d, 0:half] = above
        tail[d, half:EDGE] = below
        writes.append(
            pltpu.make_async_copy(tail.at[d], out.at[d, pl.ds(BODY, MESSAGE - BODY)], out_sems.at[N_TILE + d])
        )
        writes[-1].start()

    for d in range(N_TILE):
        reads[d].wait()
        writes[d].start()

        def add_edges(k, carry, d=d):
            s = d * CAP + k
            t = tile_ref[s]
            live = k < count_ref[d]
            c = t & (TC - 1)
            first = pl.multiple_of(k * TILE, TILE)

            at_bottom = t >= TC * (TR - 1)

            @pl.when(live & ((t < TC) | at_bottom))
            def _():
                side = jnp.where(at_bottom, 1, 0)
                at = pl.multiple_of(first + side * (TILE - HALO), HALO)
                x = buf[d, pl.ds(at, HALO), :].astype(F32)
                edge[d, side, c] += splat_low(dose_ref[s], (HALO, TILE)) * x

            return carry

        lax.fori_loop(0, CAP, add_edges, 0)
        if d > 0:
            send_tail(d - 1)
    send_tail(N_TILE - 1)
    for c in writes:
        c.wait()


def source_kernel(me_ref, dose_ref, tile_ref, count_ref, groups, out, buf, part, total, sems):
    me = me_ref[0]
    copies = [pltpu.make_async_copy(groups.at[d], buf.at[d], sems.at[d]) for d in range(N_TILE)]
    for c in copies:
        c.start()
    for d in range(N_TILE):
        copies[d].wait()
        for k in range(CAP):
            x = buf[d, k * TILE : (k + 1) * TILE].astype(F32)
            part[d * CAP + k] = jnp.sum(x.reshape(TILE // 8, 8, TILE), axis=0)
    sums = jnp.sum(jnp.sum(part[...], axis=1), axis=1, keepdims=True) * (1.0 / (TILE * TILE))
    total[...] = jnp.broadcast_to(sums, (SLOTS, TILE))
    row = iota((8, TILE), 0)
    lane = iota((8, TILE), 1)
    target_row = row * TR + ((lane & 31) >> 2)
    column = lane >> 5

    def add_slot(s, acc):
        d = s >> 3
        t = tile_ref[s]
        dose = jnp.where((s & (CAP - 1)) < count_ref[d], dose_ref[s], 0.0)
        value = jnp.broadcast_to(total[pl.ds(s, 1), :], (8, TILE))
        gap = (target_row - (d * TR + (t >> 2))).astype(F32)
        across = jnp.exp(gap * gap * (-1.0 / (2.0 * BAND_SPREAD**2)))
        return acc + jnp.where(column == (t & (TC - 1)), across * (splat_low(dose, (8, TILE)) * value), 0.0)

    acc = lax.fori_loop(0, SLOTS, add_slot, jnp.zeros((8, TILE), F32), unroll=8)
    for i in range(8):
        low_bits = ((i >> 2) & 1) + (i & 2) + 4 * (i & 1)
        result = jnp.zeros((8, TILE), F32)
        for g in range(4):
            r = low_bits + 8 * (g >> 1) + 16 * (g & 1)
            gap = jnp.abs(me * TC + column - ((me ^ r) * TC + (lane & (TC - 1))))
            gap = jnp.minimum(gap, NXC - gap).astype(F32)
            x = acc * jnp.exp(gap * gap * (-1.0 / (2.0 * LOOP_SPREAD**2)))
            x = x + pltpu.roll(x, 64, 1)
            x = x + pltpu.roll(x, 32, 1)
            result = jnp.where(column == g, x, result)
        out[i] = result


def select_rows(first):
    r = iota((HALO, TILE), 0)
    c = iota((HALO, TILE), 1)
    return jnp.where(c == r + first, 1.0, 0.0).astype(BF16)


def dot_nt(a, b):
    return lax.dot_general(a, b, (((1,), (1,)), ((), ())), preferred_element_type=F32)


def tile_at(t):
    at_row = pl.ds(pl.multiple_of((t >> 2) * TILE, TILE), TILE)
    at_col = pl.ds(pl.multiple_of((t & (TC - 1)) * TILE, TILE), TILE)
    return at_row, at_col


def decode(got):
    rows = []
    for b in range(N_TILE):
        x = got[b, INFO:MESSAGE].astype(F32)
        rows.append(x[0:1] + x[1:2] + x[2:3])
    return jnp.concatenate(rows, 0)


def slot_copies(info, tiles, dose_s, tile_s, sems):
    return (
        pltpu.make_async_copy(info, dose_s, sems.at[0]),
        pltpu.make_async_copy(tiles, tile_s, sems.at[1]),
    )


def deposit_kernel(got, ext, left, right, info, tiles, acc, dose_s, tile_s, sems):
    values = decode(got)
    info[...] = values
    tiles[...] = values.astype(jnp.int32)
    to_slots = slot_copies(info, tiles, dose_s, tile_s, sems)
    for c in to_slots:
        c.start()
    acc[...] = jnp.zeros_like(acc)
    for side in range(2):
        at = slice(0, HALO) if side == 0 else slice(EXT_ROWS - HALO, EXT_ROWS)
        for c in range(TC):
            first = BODY + (side * TC + c) * HALO
            x = got[0, first : first + HALO].astype(F32)
            for b in range(1, N_TILE):
                x = x + got[b, first : first + HALO].astype(F32)
            ext[at, c * TILE : (c + 1) * TILE] = x.astype(BF16)
    for c in to_slots:
        c.wait()

    def add_group(b, carry):
        for k in range(CAP):
            dose = dose_s[b, k]

            x = got[b, k * TILE : (k + 1) * TILE].astype(F32)
            acc[tile_at(tile_s[b, CAP + k])] += splat_low(dose, (TILE, TILE)) * x

        return carry

    lax.fori_loop(0, N_TILE, add_group, 0)
    for j in range(N_ROW_BLOCKS):
        lo, hi = j * ROW_BLOCK, (j + 1) * ROW_BLOCK
        ext[HALO + lo : HALO + hi, :] = acc[lo:hi, :].astype(BF16)
    blank = jnp.zeros((HALO, STRIP - EXT_ROWS), BF16)
    for out, first, lane in ((left, 0, 0), (right, TILE - HALO, COLS - TILE)):
        strip = dot_nt(select_rows(first), ext[:, lane : lane + TILE]).astype(BF16)
        out[...] = jnp.concatenate([strip, blank], 1)


def first_of_run():
    return lax.rem(lax.axis_index("stripe"), RUN) < 2


def early_kernel(got, ext, info, tiles, table_hbm, left, _, *rest):
    left_out = rest[N_MIDDLE]
    left_out[...] = left[...]
    pl.when(first_of_run())(lambda: middle_kernel(got, ext, info, tiles, table_hbm, *rest[:N_MIDDLE], *rest[N_MIDDLE + 1 :]))


def late_kernel(got, ext, info, tiles, table_hbm, *rest):
    pl.when(~first_of_run())(lambda: middle_kernel(got, ext, info, tiles, table_hbm, *rest[N_MIDDLE:]))


def middle_kernel(
    got, ext, info, tiles, table_hbm,
    local, own_num, sums, slot_dose, slot_tile, small,
    table, passed, nums, part, dose_s, tile_s, slot_sems, sems,
):
    to_rows = pltpu.make_async_copy(table_hbm.at[pl.ds(ROWS_PASS, 2 * TILE)], table.at[pl.ds(ROWS_PASS, 2 * TILE)], sems.at[0])
    to_cols = pltpu.make_async_copy(table_hbm.at[pl.ds(0, STRIPS)], table.at[pl.ds(0, STRIPS)], sems.at[1])
    to_small = pltpu.make_async_copy(table_hbm.at[pl.ds(SIDE_LEFT, 4 * TILE)], small, sems.at[2])
    to_slots = slot_copies(info, tiles, dose_s, tile_s, slot_sems)
    for c in (to_rows, to_cols, to_small) + to_slots:
        c.start()
    for s in range(SLOTS):
        x = got[s // CAP, (s % CAP) * TILE : (s % CAP + 1) * TILE].astype(F32)
        part[s] = jnp.sum(x.reshape(TILE // 8, 8, TILE), axis=0)
    to_rows.wait()
    for i in range(TR):
        lo, hi = i * TILE, (i + 1) * TILE
        both = jnp.dot(
            table[ROWS_PASS : ROWS_PASS + 2 * TILE, 0:ROWS_WINDOW],
            ext[lo : lo + ROWS_WINDOW, :],
            preferred_element_type=F32,
        )
        passed[0, lo:hi] = both[0:TILE].astype(BF16)
        passed[1, lo:hi] = both[TILE:].astype(BF16)
    to_cols.wait()
    lanes = iota((ROW_BLOCK, TILE), 1)
    for j in range(N_ROW_BLOCKS):
        lo, hi = ROW_BLOCK * j, ROW_BLOCK * (j + 1)
        for half in range(COLS // COL_BLOCK):
            own = slice(half * COL_BLOCK, (half + 1) * COL_BLOCK)
            if half == 0:
                beside, keep, first = slice(COL_BLOCK, COL_BLOCK + TILE), lanes < HALO, SIDE_LEFT
            else:
                beside, keep, first = slice(COL_BLOCK - TILE, COL_BLOCK), lanes >= TILE - HALO, SIDE_RIGHT
            narrow = jnp.where(keep, passed[0, lo:hi, beside].astype(F32), 0.0)
            dilated = jnp.where(keep, passed[1, lo:hi, beside].astype(F32), 0.0)
            side = (narrow + pltpu.roll(dilated, HALO, 1)).astype(BF16)
            result = jnp.dot(passed[0, lo:hi, own], table[OWN_NARROW : OWN_NARROW + COL_BLOCK, :], preferred_element_type=F32)
            result += jnp.dot(passed[1, lo:hi, own], table[OWN_DILATED : OWN_DILATED + COL_BLOCK, :], preferred_element_type=F32)
            result += jnp.dot(side, table[first : first + TILE, :], preferred_element_type=F32)
            local[lo:hi, own] = result
    for c in to_slots:
        c.wait()

    def see_group(b, carry):
        for k in range(CAP):
            s = b * CAP + k
            dose = dose_s[b, k]
            slot_dose[pl.ds(s, 1), :] = jnp.full((1, TILE), dose, F32)
            slot_tile[pl.ds(s, 1), :] = jnp.full((1, TILE), tile_s[b, CAP + k], jnp.int32)

            x = got[b, k * TILE : (k + 1) * TILE].astype(F32)
            seen = local[tile_at(tile_s[b, CAP + k])] * x
            nums[s] = jnp.sum(seen.reshape(TILE // 8, 8, TILE), axis=0)

        return carry

    lax.fori_loop(0, N_TILE, see_group, 0)
    for out, parts in ((own_num, nums), (sums, part)):
        total = jnp.sum(jnp.sum(parts[...], axis=1), axis=1, keepdims=True)
        out[...] = jnp.broadcast_to(total, (SLOTS, TILE))
    to_small.wait()


def forward_kernel(
    back_got, before, after, back_own, local, own_num, sums, slot_dose, slot_tile, small, info, tiles, got,
    energy, new_dose, backscatter,
    windows, halo_left, halo_right, edge_left, edge_right, final, nums, dose_s, tile_s, slot_sems, out_sems,
):
    me = lax.axis_index("tile")
    to_slots = slot_copies(info, tiles, dose_s, tile_s, slot_sems)
    for c in to_slots:
        c.start()
    lane = iota((8, TILE), 1)
    row = iota((8, TILE), 0)
    own = (back_own[...] + back_got[...]) * (1.0 / back_norm())
    own = jnp.sum(jnp.where(iota((8, 32), 0) == me, own, 0.0), axis=0, keepdims=True)
    own = jnp.broadcast_to(own, (8, 32))
    small_row, small_lane = iota((8, 32), 0), iota((8, 32), 1)
    terms = []
    for c in range(TC):
        at = small_lane == small_row * TC + c
        term = jnp.sum(jnp.where(at, own, 0.0), axis=1, keepdims=True)
        terms.append(jnp.broadcast_to(term, (8, TILE)))
        backscatter[c : c + 1, :] = jnp.sum(jnp.where(lane == row, terms[c], 0.0), axis=0, keepdims=True)[:, 0:TR]
    for i in range(TR):
        at = slice(TILE * i, TILE * (i + 2))
        windows[HALO * i : HALO * (i + 1), :] = before[:, at]
        windows[HALO * (TR + i) : HALO * (TR + i + 1), :] = after[:, at]
    strips = jnp.dot(windows[...], small[STRIPS - SIDE_LEFT :, :], preferred_element_type=F32)
    blank = jnp.zeros((2 * HALO, TILE), F32)
    for side, (halo, edge) in enumerate(((halo_left, edge_left), (halo_right, edge_right))):
        for i in range(TR):
            both = strips[HALO * (side * TR + i) : HALO * (side * TR + i + 1), :]
            stacked = jnp.concatenate([blank, both[:, 0:TILE], both[:, TILE:], blank, blank], 0)
            halo[TILE * i : TILE * (i + 1), :] = stacked.T.astype(BF16)
        weights = small[side * TILE : (side + 1) * TILE, side * TILE : (side + 1) * TILE]
        edge[...] = jnp.dot(halo[...], weights, preferred_element_type=F32)
    out_copies = []
    for p in range(TR):
        rows = slice(p * TILE, (p + 1) * TILE)
        for c in range(TC):
            at = slice(c * TILE, (c + 1) * TILE)
            x = local[rows, at] + ETA_BACK * terms[c][p : p + 1]
            if c == 0:
                x = x + edge_left[rows, :]
            if c == TC - 1:
                x = x + edge_right[rows, :]
            final[rows, at] = x
        if p % 2 == 1:
            at = pl.ds((p - 1) * TILE, 2 * TILE)
            out_copies.append(pltpu.make_async_copy(final.at[at], energy.at[at], out_sems.at[p]))
            out_copies[-1].start()
    for c in to_slots:
        c.wait()

    def see_group(b, carry):
        for k in range(CAP):
            s = b * CAP + k
            t = tile_s[b, CAP + k]
            live = dose_s[b, k] > 0.0
            column = t & (TC - 1)
            rows = pl.ds(pl.multiple_of((t >> 2) * TILE, TILE), TILE)
            nums[s] = jnp.zeros((8, TILE), F32)

            @pl.when(live & (column == 0))
            def _(k=k, s=s, rows=rows):
                x = got[b, k * TILE : (k + 1) * TILE].astype(F32) * edge_left[rows, :]
                nums[s] = jnp.sum(x.reshape(TILE // 8, 8, TILE), axis=0)

            @pl.when(live & (column == TC - 1))
            def _(k=k, s=s, rows=rows):
                x = got[b, k * TILE : (k + 1) * TILE].astype(F32) * edge_right[rows, :]
                nums[s] = jnp.sum(x.reshape(TILE // 8, 8, TILE), axis=0)

        return carry

    lax.fori_loop(0, N_TILE, see_group, 0)
    at_tile = slot_tile[:, 0:32] == iota((SLOTS, 32), 1)
    back = jnp.sum(jnp.where(at_tile, jnp.broadcast_to(own[0:1], (SLOTS, 32)), 0.0), axis=1, keepdims=True)
    num = jnp.sum(jnp.sum(nums[...], axis=1), axis=1, keepdims=True)
    total = sums[...]
    exposure = (own_num[...] + (num + (ETA_BACK * back) * total)) / total
    dose = slot_dose[...]
    corrected = jnp.where(dose > 0.0, dose * TARGET_DOSE / exposure, 0.0)
    at_slot = iota((SLOTS, TILE), 0) == iota((SLOTS, TILE), 1)
    new_dose[...] = jnp.sum(jnp.where(at_slot, corrected, 0.0), axis=0, keepdims=True)[:, 0:SLOTS]
    for copy in out_copies:
        copy.wait()


def spec(space):
    return pl.BlockSpec(memory_space=space)


VMEM, SMEM, HBM = pltpu.VMEM, pltpu.SMEM, pltpu.HBM
PACK_PARAMS = pltpu.CompilerParams(vmem_limit_bytes=64 * 2**20)
PARAMS = pltpu.CompilerParams(vmem_limit_bytes=24 * 2**20)


def cost(us):
    return pl.CostEstimate(flops=int(us * 1e9), bytes_accessed=int(us * 3e6), transcendentals=0)


def array(shape, dtype):
    return jax.ShapeDtypeStruct(shape, dtype)


def on_device(shot_blocks, shot_dose, shot_tile, shot_count):
    me_stripe = lax.axis_index("stripe").astype(jnp.int32).reshape(1)
    table = jnp.asarray(tables())
    groups = shot_blocks.reshape(N_TILE, BODY, TILE)

    message = pl.pallas_call(
        pack_kernel,
        out_shape=array((N_TILE, MESSAGE, TILE), BF16),
        in_specs=[spec(HBM)] * 4,
        out_specs=spec(HBM),
        scratch_shapes=[
            pltpu.VMEM((N_TILE, BODY, TILE), BF16),
            pltpu.VMEM((N_TILE, 2, TC, HALO, TILE), F32),
            pltpu.VMEM((N_TILE, MESSAGE - BODY, TILE), BF16),
            pltpu.SMEM((SLOTS,), F32),
            pltpu.SMEM((SLOTS,), jnp.int32),
            pltpu.SMEM((N_TILE,), jnp.int32),
            pltpu.SemaphoreType.DMA((N_TILE,)),
            pltpu.SemaphoreType.DMA((2 * N_TILE,)),
            pltpu.SemaphoreType.DMA((3,)),
        ],
        compiler_params=PACK_PARAMS,
        cost_estimate=cost(3.5),
        name="pack",
    )(shot_dose, shot_tile, shot_count, groups)
    got = lax.all_to_all(message, "tile", split_axis=0, concat_axis=0, tiled=True)

    back = pl.pallas_call(
        source_kernel,
        out_shape=array((8, 8, TILE), F32),
        in_specs=[spec(SMEM)] * 4 + [spec(HBM)],
        out_specs=spec(VMEM),
        scratch_shapes=[
            pltpu.VMEM((N_TILE, BODY, TILE), BF16),
            pltpu.VMEM((SLOTS, 8, TILE), F32),
            pltpu.VMEM((SLOTS, TILE), F32),
            pltpu.SemaphoreType.DMA((N_TILE,)),
        ],
        compiler_params=PARAMS,
        cost_estimate=cost(3),
        name="source",
    )(me_stripe, shot_dose, shot_tile, shot_count, groups)

    for bit in (1, 2, 4):
        half = back.shape[0] // 2
        sent = lax.ppermute(back[half:], "stripe", [(i, i ^ bit) for i in range(N_STRIPE)])
        back = back[:half] + sent
    back = back.reshape(8, TILE)
    sent = lax.ppermute(back, "stripe", [(i, i ^ 8) for i in range(N_STRIPE)])
    back = back[:, 0:64] + sent[:, 64:128]

    def swapped(x, stripe_bit, tile_bit):
        pairs = [
            (a * N_TILE + b, (a ^ stripe_bit) * N_TILE + (b ^ tile_bit))
            for a in range(N_STRIPE)
            for b in range(N_TILE)
        ]
        return lax.ppermute(x, ("stripe", "tile"), pairs)

    back = back[:, 0:32] + swapped(back, 16, 0)[:, 32:64] + swapped(back, 0, 4)[:, 0:32] + swapped(back, 16, 4)[:, 32:64]
    back, got = lax.optimization_barrier((back, got))
    back = back + swapped(back, 0, 1)
    back_got = swapped(back, 0, 3)

    pattern, left, right, info, tiles = pl.pallas_call(
        deposit_kernel,
        out_shape=(
            array((EXT_ROWS, COLS), BF16),
            array((HALO, STRIP), BF16),
            array((HALO, STRIP), BF16),
            array((N_TILE, TILE), F32),
            array((N_TILE, TILE), jnp.int32),
        ),
        in_specs=[spec(VMEM)],
        out_specs=(spec(VMEM),) * 5,
        scratch_shapes=[
            pltpu.VMEM((ROWS, COLS), F32),
            pltpu.SMEM((N_TILE, TILE), F32),
            pltpu.SMEM((N_TILE, TILE), jnp.int32),
            pltpu.SemaphoreType.DMA((2,)),
        ],
        compiler_params=PARAMS,
        cost_estimate=cost(2.5),
        name="deposit",
    )(got)

    ring_up = [(i, (i + 1) % N_STRIPE) for i in range(N_STRIPE)]
    before = lax.ppermute(right, "stripe", ring_up)

    slots = array((SLOTS, TILE), F32)
    results = (
        array((ROWS, COLS), F32),
        slots,
        slots,
        slots,
        array((SLOTS, TILE), jnp.int32),
        array((ROWS_PASS - SIDE_LEFT, COL_BLOCK), BF16),
    )
    scratch = [
        pltpu.VMEM((TABLE_END, COL_BLOCK), BF16),
        pltpu.VMEM((2, ROWS, COLS), BF16),
        pltpu.VMEM((SLOTS, 8, TILE), F32),
        pltpu.VMEM((SLOTS, 8, TILE), F32),
        pltpu.SMEM((N_TILE, TILE), F32),
        pltpu.SMEM((N_TILE, TILE), jnp.int32),
        pltpu.SemaphoreType.DMA((2,)),
        pltpu.SemaphoreType.DMA((3,)),
    ]
    *early, left = pl.pallas_call(
        early_kernel,
        out_shape=results + (array((HALO, STRIP), BF16),),
        in_specs=[spec(VMEM)] * 4 + [spec(HBM)] + [spec(VMEM)] * 2,
        out_specs=(spec(VMEM),) * (N_MIDDLE + 1),
        scratch_shapes=scratch,
        compiler_params=PARAMS,
        cost_estimate=cost(4),
        name="early",
    )(got, pattern, info, tiles, table, left, back)
    after = lax.ppermute(left, "stripe", [(j, i) for i, j in ring_up])
    local, own_num, sums, slot_dose, slot_tile, small = pl.pallas_call(
        late_kernel,
        out_shape=results,
        in_specs=[spec(VMEM)] * 4 + [spec(HBM)] + [spec(VMEM)] * N_MIDDLE,
        out_specs=(spec(VMEM),) * N_MIDDLE,
        scratch_shapes=scratch,
        input_output_aliases={5 + n: n for n in range(N_MIDDLE)},
        compiler_params=PARAMS,
        cost_estimate=cost(0),
        name="late",
    )(got, pattern, info, tiles, table, *early)

    energy, new_dose, backscatter = pl.pallas_call(
        forward_kernel,
        out_shape=(
            array((ROWS, COLS), F32),
            array((1, SLOTS), F32),
            array((TC, TR), F32),
        ),
        in_specs=[spec(VMEM)] * 13,
        out_specs=(spec(HBM), spec(VMEM), spec(VMEM)),
        scratch_shapes=[
            pltpu.VMEM((TR * 2 * HALO, 2 * TILE), BF16),
            pltpu.VMEM((ROWS, TILE), BF16),
            pltpu.VMEM((ROWS, TILE), BF16),
            pltpu.VMEM((ROWS, TILE), F32),
            pltpu.VMEM((ROWS, TILE), F32),
            pltpu.VMEM((ROWS, COLS), F32),
            pltpu.VMEM((SLOTS, 8, TILE), F32),
            pltpu.SMEM((N_TILE, TILE), F32),
            pltpu.SMEM((N_TILE, TILE), jnp.int32),
            pltpu.SemaphoreType.DMA((2,)),
            pltpu.SemaphoreType.DMA((TR,)),
        ],
        compiler_params=PARAMS,
        cost_estimate=cost(3),
        name="forward",
    )(back_got, before, after, back, local, own_num, sums, slot_dose, slot_tile, small, info, tiles, got)
    return energy, backscatter.T, new_dose.reshape(SLOTS)


def solution(mesh):
    in_specs = (
        P(("stripe", "tile"), None, None),
        P(("stripe", "tile")),
        P(("stripe", "tile")),
        P(("stripe", "tile")),
    )
    out_specs = (P("tile", "stripe"), P("tile", "stripe"), P(("stripe", "tile")))
    return jax.shard_map(
        on_device, mesh=mesh, in_specs=in_specs, out_specs=out_specs, check_vma=False
    )
```

```python
import jax
import jax.numpy as jnp
import numpy as np
import ml_dtypes
from jax import lax
from jax.experimental import pallas as pl
from jax.experimental.pallas import tpu as pltpu
from jax.sharding import PartitionSpec as P

TILE = 128
TR = 8
TC = 4
HALO = 16
CAP = 8
N_STRIPE = 32
RUN = 16
N_TILE = 8
SLOTS = N_TILE * CAP
ROWS = TR * TILE
COLS = TC * TILE
ROW_BLOCK = 256
COL_BLOCK = 256
EXT_ROWS = ROWS + 2 * HALO
STRIP = ROWS + TILE
BODY = CAP * TILE
EDGE = 2 * TC * HALO
INFO = BODY + EDGE
MESSAGE = INFO + HALO
N_ROW_BLOCKS = ROWS // ROW_BLOCK

ETA_BACK = 0.7
DILATED_WEIGHT = 0.5
TARGET_DOSE = 1.0
NARROW_SIGMA = 2.0
DILATED_SIGMA = 4.0
NXC = N_STRIPE * TC
NYC = N_TILE * TR
LOOP_SPREAD = NXC / 2.0
BAND_SPREAD = NYC / 5.0

F32 = jnp.float32
BF16 = jnp.bfloat16


def taps():
    offset = np.arange(-HALO, HALO + 1).astype(np.float32)
    narrow = np.exp(-offset * offset / np.float32(2.0 * NARROW_SIGMA**2))
    dilated = np.exp(-offset * offset / np.float32(8.0 * DILATED_SIGMA**2))
    dilated = np.where(np.arange(-HALO, HALO + 1) % 2 == 0, dilated, np.float32(0))
    narrow = (narrow / narrow.sum(dtype=np.float32)).astype(ml_dtypes.bfloat16)
    dilated = (dilated / dilated.sum(dtype=np.float32)).astype(ml_dtypes.bfloat16)
    return narrow.astype(np.float32), dilated.astype(np.float32)


def by_offset(table, offset):
    inside = np.abs(offset) <= HALO
    return np.where(inside, table[np.clip(offset + HALO, 0, 2 * HALO)], np.float32(0))


OWN_NARROW, OWN_DILATED, SIDE_LEFT, SIDE_RIGHT, STRIPS, ROWS_PASS = 0, 256, 512, 640, 768, 1024
N_MIDDLE = 5
TABLE_ROWS = 1280
ROWS_WINDOW = TILE + 2 * HALO


def tables():
    narrow, dilated = taps()
    half = np.float32(DILATED_WEIGHT)
    table = np.zeros((TABLE_ROWS, COL_BLOCK), np.float32)
    q = np.arange(COL_BLOCK)[None, :]
    own = np.arange(COL_BLOCK)[:, None] - q
    table[OWN_NARROW : OWN_NARROW + COL_BLOCK] = by_offset(narrow, own)
    table[OWN_DILATED : OWN_DILATED + COL_BLOCK] = half * by_offset(dilated, own)
    n = np.arange(HALO)[:, None]
    before, after = n - HALO - q, n + COL_BLOCK - q
    left, right = table[SIDE_LEFT : SIDE_LEFT + TILE], table[SIDE_RIGHT : SIDE_RIGHT + TILE]
    left[0:HALO] = by_offset(narrow, after)
    left[HALO : 2 * HALO] = half * by_offset(dilated, after)
    left[2 * HALO : 3 * HALO] = by_offset(narrow, before)
    left[3 * HALO : 4 * HALO] = half * by_offset(dilated, before)
    right[TILE - HALO : TILE] = by_offset(narrow, before)
    right[0:HALO] = half * by_offset(dilated, before)
    right[2 * HALO : 3 * HALO] = by_offset(narrow, after)
    right[3 * HALO : 4 * HALO] = half * by_offset(dilated, after)
    j = np.arange(2 * TILE)[:, None]
    y = np.arange(TILE)[None, :]
    table[STRIPS : STRIPS + 2 * TILE, 0:TILE] = by_offset(narrow, j - HALO - y)
    table[STRIPS : STRIPS + 2 * TILE, TILE:] = by_offset(dilated, j - HALO - y)
    y = np.arange(TILE)[:, None]
    j = np.arange(ROWS_WINDOW)[None, :]
    table[ROWS_PASS : ROWS_PASS + TILE, 0:ROWS_WINDOW] = by_offset(narrow, j - HALO - y)
    table[ROWS_PASS + TILE : ROWS_PASS + 2 * TILE, 0:ROWS_WINDOW] = by_offset(dilated, j - HALO - y)
    return table.astype(ml_dtypes.bfloat16)


def back_norm():
    m = np.arange(NXC)
    m = np.minimum(m, NXC - m).astype(np.float64)
    sx = np.exp(-m * m / (2.0 * LOOP_SPREAD**2)).sum()
    o = np.arange(-(NYC - 1), NYC).astype(np.float64)
    sy = np.exp(-o * o / (2.0 * BAND_SPREAD**2)).sum()
    return float(sx * sy)


def iota(shape, dim):
    return lax.broadcasted_iota(jnp.int32, shape, dim)


def splat_low(value, shape):
    return jnp.full(shape, value, F32).astype(BF16).astype(F32)


def pack_kernel(dose_hbm, tile_hbm, count_hbm, groups, out, buf, edge, tail, dose_ref, tile_ref, count_ref, in_sems, out_sems, slot_sems):
    reads, writes = [], []
    for d in range(N_TILE):
        reads.append(pltpu.make_async_copy(groups.at[d], buf.at[d], in_sems.at[d]))
        writes.append(pltpu.make_async_copy(buf.at[d], out.at[d, pl.ds(0, BODY)], out_sems.at[d]))
    scalars = []
    for n, (source, target) in enumerate(((dose_hbm, dose_ref), (tile_hbm, tile_ref), (count_hbm, count_ref))):
        scalars.append(pltpu.make_async_copy(source, target, slot_sems.at[n]))
    for c in reads[:1] + scalars + reads[1:]:
        c.start()
    edge[...] = jnp.zeros_like(edge)
    row = iota((8, TILE), 0)
    lane = iota((8, TILE), 1)
    for c in scalars:
        c.wait()

    def add_info(s, acc):
        d = s >> 3
        k = s & (CAP - 1)
        dose = jnp.where(k < count_ref[d], dose_ref[s], 0.0)
        tile = jnp.full((8, TILE), tile_ref[s], jnp.int32).astype(F32)
        acc = jnp.where((row == d) & (lane == k), dose, acc)
        return jnp.where((row == d) & (lane == k + CAP), tile, acc)

    info = lax.fori_loop(0, SLOTS, add_info, jnp.zeros((8, TILE), F32), unroll=8)
    high = info.astype(BF16).astype(F32)
    middle = (info - high).astype(BF16).astype(F32)
    lowest = info - high - middle
    row = iota((HALO, TILE), 0)
    for d in range(N_TILE):
        at = slice(d, d + 1)
        rows = jnp.where(row == 0, high[at], jnp.where(row == 1, middle[at], jnp.where(row == 2, lowest[at], 0.0)))
        tail[d, EDGE:] = rows.astype(BF16)
    half = EDGE // 2
    blank = jnp.zeros((half, TILE), BF16)

    def send_tail(d):
        above = edge[d - 1, 1].reshape(half, TILE).astype(BF16) if d > 0 else blank
        below = edge[d + 1, 0].reshape(half, TILE).astype(BF16) if d < N_TILE - 1 else blank
        tail[d, 0:half] = above
        tail[d, half:EDGE] = below
        writes.append(
            pltpu.make_async_copy(tail.at[d], out.at[d, pl.ds(BODY, MESSAGE - BODY)], out_sems.at[N_TILE + d])
        )
        writes[-1].start()

    for d in range(N_TILE):
        reads[d].wait()
        writes[d].start()

        def add_edges(k, carry, d=d):
            s = d * CAP + k
            t = tile_ref[s]
            live = k < count_ref[d]
            c = t & (TC - 1)
            first = pl.multiple_of(k * TILE, TILE)

            at_bottom = t >= TC * (TR - 1)

            @pl.when(live & ((t < TC) | at_bottom))
            def _():
                side = jnp.where(at_bottom, 1, 0)
                at = pl.multiple_of(first + side * (TILE - HALO), HALO)
                x = buf[d, pl.ds(at, HALO), :].astype(F32)
                edge[d, side, c] += splat_low(dose_ref[s], (HALO, TILE)) * x

            return carry

        lax.fori_loop(0, CAP, add_edges, 0)
        if d > 0:
            send_tail(d - 1)
    send_tail(N_TILE - 1)
    for c in writes:
        c.wait()


def source_kernel(me_ref, dose_ref, tile_ref, count_ref, groups, out, buf, part, total, sems):
    me = me_ref[0]
    copies = [pltpu.make_async_copy(groups.at[d], buf.at[d], sems.at[d]) for d in range(N_TILE)]
    for c in copies:
        c.start()
    for d in range(N_TILE):
        copies[d].wait()
        for k in range(CAP):
            x = buf[d, k * TILE : (k + 1) * TILE].astype(F32)
            part[d * CAP + k] = jnp.sum(x.reshape(TILE // 8, 8, TILE), axis=0)
    sums = jnp.sum(jnp.sum(part[...], axis=1), axis=1, keepdims=True) * (1.0 / (TILE * TILE))
    total[...] = jnp.broadcast_to(sums, (SLOTS, TILE))
    row = iota((8, TILE), 0)
    lane = iota((8, TILE), 1)
    target_row = row * TR + ((lane & 31) >> 2)
    column = lane >> 5

    def add_slot(s, acc):
        d = s >> 3
        t = tile_ref[s]
        dose = jnp.where((s & (CAP - 1)) < count_ref[d], dose_ref[s], 0.0)
        value = jnp.broadcast_to(total[pl.ds(s, 1), :], (8, TILE))
        gap = (target_row - (d * TR + (t >> 2))).astype(F32)
        across = jnp.exp(gap * gap * (-1.0 / (2.0 * BAND_SPREAD**2)))
        return acc + jnp.where(column == (t & (TC - 1)), across * (splat_low(dose, (8, TILE)) * value), 0.0)

    acc = lax.fori_loop(0, SLOTS, add_slot, jnp.zeros((8, TILE), F32), unroll=8)
    for i in range(8):
        low_bits = ((i >> 2) & 1) + (i & 2) + 4 * (i & 1)
        result = jnp.zeros((8, TILE), F32)
        for g in range(4):
            r = low_bits + 8 * (g >> 1) + 16 * (g & 1)
            gap = jnp.abs(me * TC + column - ((me ^ r) * TC + (lane & (TC - 1))))
            gap = jnp.minimum(gap, NXC - gap).astype(F32)
            x = acc * jnp.exp(gap * gap * (-1.0 / (2.0 * LOOP_SPREAD**2)))
            x = x + pltpu.roll(x, 64, 1)
            x = x + pltpu.roll(x, 32, 1)
            result = jnp.where(column == g, x, result)
        out[i] = result


def select_rows(first):
    r = iota((HALO, TILE), 0)
    c = iota((HALO, TILE), 1)
    return jnp.where(c == r + first, 1.0, 0.0).astype(BF16)


def dot_nt(a, b):
    return lax.dot_general(a, b, (((1,), (1,)), ((), ())), preferred_element_type=F32)


def tile_at(t):
    at_row = pl.ds(pl.multiple_of((t >> 2) * TILE, TILE), TILE)
    at_col = pl.ds(pl.multiple_of((t & (TC - 1)) * TILE, TILE), TILE)
    return at_row, at_col


def decode(got):
    rows = []
    for b in range(N_TILE):
        x = got[b, INFO:MESSAGE].astype(F32)
        rows.append(x[0:1] + x[1:2] + x[2:3])
    return jnp.concatenate(rows, 0)


def slot_copies(info, tiles, dose_s, tile_s, sems):
    return (
        pltpu.make_async_copy(info, dose_s, sems.at[0]),
        pltpu.make_async_copy(tiles, tile_s, sems.at[1]),
    )


def deposit_kernel(got, ext, left, right, info, tiles, acc, dose_s, tile_s, sems):
    values = decode(got)
    info[...] = values
    tiles[...] = values.astype(jnp.int32)
    to_slots = slot_copies(info, tiles, dose_s, tile_s, sems)
    for c in to_slots:
        c.start()
    acc[...] = jnp.zeros_like(acc)
    for side in range(2):
        at = slice(0, HALO) if side == 0 else slice(EXT_ROWS - HALO, EXT_ROWS)
        for c in range(TC):
            first = BODY + (side * TC + c) * HALO
            x = got[0, first : first + HALO].astype(F32)
            for b in range(1, N_TILE):
                x = x + got[b, first : first + HALO].astype(F32)
            ext[at, c * TILE : (c + 1) * TILE] = x.astype(BF16)
    for c in to_slots:
        c.wait()

    def add_group(b, carry):
        for k in range(CAP):
            dose = dose_s[b, k]

            x = got[b, k * TILE : (k + 1) * TILE].astype(F32)
            acc[tile_at(tile_s[b, CAP + k])] += splat_low(dose, (TILE, TILE)) * x

        return carry

    lax.fori_loop(0, N_TILE, add_group, 0)
    for j in range(N_ROW_BLOCKS):
        lo, hi = j * ROW_BLOCK, (j + 1) * ROW_BLOCK
        ext[HALO + lo : HALO + hi, :] = acc[lo:hi, :].astype(BF16)
    blank = jnp.zeros((HALO, STRIP - EXT_ROWS), BF16)
    for out, first, lane in ((left, 0, 0), (right, TILE - HALO, COLS - TILE)):
        strip = dot_nt(select_rows(first), ext[:, lane : lane + TILE]).astype(BF16)
        out[...] = jnp.concatenate([strip, blank], 1)


def first_of_run():
    return lax.rem(lax.axis_index("stripe"), RUN) == 0


def early_kernel(got, ext, info, tiles, table, left, _, *rest):
    left_out = rest[N_MIDDLE]
    left_out[...] = left[...]
    pl.when(first_of_run())(lambda: middle_kernel(got, ext, info, tiles, table, *rest[:N_MIDDLE], *rest[N_MIDDLE + 1 :]))


def late_kernel(got, ext, info, tiles, table, *rest):
    pl.when(~first_of_run())(lambda: middle_kernel(got, ext, info, tiles, table, *rest[N_MIDDLE:]))


def middle_kernel(
    got, ext, info, tiles, table,
    local, own_num, sums, slot_dose, slot_tile,
    passed, nums, part, dose_s, tile_s, slot_sems,
):
    to_slots = slot_copies(info, tiles, dose_s, tile_s, slot_sems)
    for c in to_slots:
        c.start()
    for i in range(TR):
        lo, hi = i * TILE, (i + 1) * TILE
        both = jnp.dot(
            table[ROWS_PASS : ROWS_PASS + 2 * TILE, 0:ROWS_WINDOW],
            ext[lo : lo + ROWS_WINDOW, :],
            preferred_element_type=F32,
        )
        passed[0, lo:hi] = both[0:TILE].astype(BF16)
        passed[1, lo:hi] = both[TILE:].astype(BF16)
    lanes = iota((ROW_BLOCK, TILE), 1)
    for j in range(N_ROW_BLOCKS):
        lo, hi = ROW_BLOCK * j, ROW_BLOCK * (j + 1)
        for half in range(COLS // COL_BLOCK):
            own = slice(half * COL_BLOCK, (half + 1) * COL_BLOCK)
            if half == 0:
                beside, keep, first = slice(COL_BLOCK, COL_BLOCK + TILE), lanes < HALO, SIDE_LEFT
            else:
                beside, keep, first = slice(COL_BLOCK - TILE, COL_BLOCK), lanes >= TILE - HALO, SIDE_RIGHT
            narrow = jnp.where(keep, passed[0, lo:hi, beside].astype(F32), 0.0)
            dilated = jnp.where(keep, passed[1, lo:hi, beside].astype(F32), 0.0)
            side = (narrow + pltpu.roll(dilated, HALO, 1)).astype(BF16)
            result = jnp.dot(passed[0, lo:hi, own], table[OWN_NARROW : OWN_NARROW + COL_BLOCK, :], preferred_element_type=F32)
            result += jnp.dot(passed[1, lo:hi, own], table[OWN_DILATED : OWN_DILATED + COL_BLOCK, :], preferred_element_type=F32)
            result += jnp.dot(side, table[first : first + TILE, :], preferred_element_type=F32)
            local[lo:hi, own] = result
    for c in to_slots:
        c.wait()

    def see_group(b, carry):
        for k in range(CAP):
            s = b * CAP + k
            dose = dose_s[b, k]
            slot_dose[pl.ds(s, 1), :] = jnp.full((1, TILE), dose, F32)
            slot_tile[pl.ds(s, 1), :] = jnp.full((1, TILE), tile_s[b, CAP + k], jnp.int32)

            x = got[b, k * TILE : (k + 1) * TILE].astype(F32)
            seen = local[tile_at(tile_s[b, CAP + k])] * x
            nums[s] = jnp.sum(seen.reshape(TILE // 8, 8, TILE), axis=0)
            part[s] = jnp.sum(x.reshape(TILE // 8, 8, TILE), axis=0)

        return carry

    lax.fori_loop(0, N_TILE, see_group, 0)
    for out, parts in ((own_num, nums), (sums, part)):
        total = jnp.sum(jnp.sum(parts[...], axis=1), axis=1, keepdims=True)
        out[...] = jnp.broadcast_to(total, (SLOTS, TILE))


def forward_kernel(
    back_got, before, after, back_own, local, own_num, sums, slot_dose, slot_tile, table, info, tiles, got,
    energy, new_dose, backscatter,
    windows, halo_left, halo_right, edge_left, edge_right, final, nums, dose_s, tile_s, slot_sems, out_sems,
):
    me = lax.axis_index("tile")
    to_slots = slot_copies(info, tiles, dose_s, tile_s, slot_sems)
    for c in to_slots:
        c.start()
    lane = iota((8, TILE), 1)
    row = iota((8, TILE), 0)
    own = (back_own[...] + back_got[...]) * (1.0 / back_norm())
    own = jnp.sum(jnp.where(iota((8, 32), 0) == me, own, 0.0), axis=0, keepdims=True)
    own = jnp.broadcast_to(own, (8, 32))
    small_row, small_lane = iota((8, 32), 0), iota((8, 32), 1)
    terms = []
    for c in range(TC):
        at = small_lane == small_row * TC + c
        term = jnp.sum(jnp.where(at, own, 0.0), axis=1, keepdims=True)
        terms.append(jnp.broadcast_to(term, (8, TILE)))
        backscatter[c : c + 1, :] = jnp.sum(jnp.where(lane == row, terms[c], 0.0), axis=0, keepdims=True)[:, 0:TR]
    for i in range(TR):
        at = slice(TILE * i, TILE * (i + 2))
        windows[HALO * i : HALO * (i + 1), :] = before[:, at]
        windows[HALO * (TR + i) : HALO * (TR + i + 1), :] = after[:, at]
    strips = jnp.dot(windows[...], table[STRIPS : STRIPS + 2 * TILE, :], preferred_element_type=F32)
    blank = jnp.zeros((2 * HALO, TILE), F32)
    for side, (halo, edge) in enumerate(((halo_left, edge_left), (halo_right, edge_right))):
        for i in range(TR):
            both = strips[HALO * (side * TR + i) : HALO * (side * TR + i + 1), :]
            stacked = jnp.concatenate([blank, both[:, 0:TILE], both[:, TILE:], blank, blank], 0)
            halo[TILE * i : TILE * (i + 1), :] = stacked.T.astype(BF16)
        first = SIDE_LEFT + side * TILE
        weights = table[first : first + TILE, side * TILE : (side + 1) * TILE]
        edge[...] = jnp.dot(halo[...], weights, preferred_element_type=F32)
    out_copies = []
    for p in range(TR):
        rows = slice(p * TILE, (p + 1) * TILE)
        for c in range(TC):
            at = slice(c * TILE, (c + 1) * TILE)
            x = local[rows, at] + ETA_BACK * terms[c][p : p + 1]
            if c == 0:
                x = x + edge_left[rows, :]
            if c == TC - 1:
                x = x + edge_right[rows, :]
            final[rows, at] = x
        if p % 2 == 1:
            at = pl.ds((p - 1) * TILE, 2 * TILE)
            out_copies.append(pltpu.make_async_copy(final.at[at], energy.at[at], out_sems.at[p]))
            out_copies[-1].start()
    for c in to_slots:
        c.wait()

    def see_group(b, carry):
        for k in range(CAP):
            s = b * CAP + k
            t = tile_s[b, CAP + k]
            live = dose_s[b, k] > 0.0
            column = t & (TC - 1)
            rows = pl.ds(pl.multiple_of((t >> 2) * TILE, TILE), TILE)
            nums[s] = jnp.zeros((8, TILE), F32)

            @pl.when(live & (column == 0))
            def _(k=k, s=s, rows=rows):
                x = got[b, k * TILE : (k + 1) * TILE].astype(F32) * edge_left[rows, :]
                nums[s] = jnp.sum(x.reshape(TILE // 8, 8, TILE), axis=0)

            @pl.when(live & (column == TC - 1))
            def _(k=k, s=s, rows=rows):
                x = got[b, k * TILE : (k + 1) * TILE].astype(F32) * edge_right[rows, :]
                nums[s] = jnp.sum(x.reshape(TILE // 8, 8, TILE), axis=0)

        return carry

    lax.fori_loop(0, N_TILE, see_group, 0)
    at_tile = slot_tile[:, 0:32] == iota((SLOTS, 32), 1)
    back = jnp.sum(jnp.where(at_tile, jnp.broadcast_to(own[0:1], (SLOTS, 32)), 0.0), axis=1, keepdims=True)
    num = jnp.sum(jnp.sum(nums[...], axis=1), axis=1, keepdims=True)
    total = sums[...]
    exposure = (own_num[...] + (num + (ETA_BACK * back) * total)) / total
    dose = slot_dose[...]
    corrected = jnp.where(dose > 0.0, dose * TARGET_DOSE / exposure, 0.0)
    at_slot = iota((SLOTS, TILE), 0) == iota((SLOTS, TILE), 1)
    new_dose[...] = jnp.sum(jnp.where(at_slot, corrected, 0.0), axis=0, keepdims=True)[:, 0:SLOTS]
    for copy in out_copies:
        copy.wait()


def spec(space):
    return pl.BlockSpec(memory_space=space)


VMEM, SMEM, HBM = pltpu.VMEM, pltpu.SMEM, pltpu.HBM
PACK_PARAMS = pltpu.CompilerParams(vmem_limit_bytes=64 * 2**20)
PARAMS = pltpu.CompilerParams(vmem_limit_bytes=24 * 2**20)


def cost(us):
    return pl.CostEstimate(flops=int(us * 1e9), bytes_accessed=int(us * 3e6), transcendentals=0)


def array(shape, dtype):
    return jax.ShapeDtypeStruct(shape, dtype)


def on_device(shot_blocks, shot_dose, shot_tile, shot_count):
    me_stripe = lax.axis_index("stripe").astype(jnp.int32).reshape(1)
    table = jnp.asarray(tables())
    groups = shot_blocks.reshape(N_TILE, BODY, TILE)

    message = pl.pallas_call(
        pack_kernel,
        out_shape=array((N_TILE, MESSAGE, TILE), BF16),
        in_specs=[spec(HBM)] * 4,
        out_specs=spec(HBM),
        scratch_shapes=[
            pltpu.VMEM((N_TILE, BODY, TILE), BF16),
            pltpu.VMEM((N_TILE, 2, TC, HALO, TILE), F32),
            pltpu.VMEM((N_TILE, MESSAGE - BODY, TILE), BF16),
            pltpu.SMEM((SLOTS,), F32),
            pltpu.SMEM((SLOTS,), jnp.int32),
            pltpu.SMEM((N_TILE,), jnp.int32),
            pltpu.SemaphoreType.DMA((N_TILE,)),
            pltpu.SemaphoreType.DMA((2 * N_TILE,)),
            pltpu.SemaphoreType.DMA((3,)),
        ],
        compiler_params=PACK_PARAMS,
        cost_estimate=cost(3.5),
        name="pack",
    )(shot_dose, shot_tile, shot_count, groups)
    got = lax.all_to_all(message, "tile", split_axis=0, concat_axis=0, tiled=True)

    back = pl.pallas_call(
        source_kernel,
        out_shape=array((8, 8, TILE), F32),
        in_specs=[spec(SMEM)] * 4 + [spec(HBM)],
        out_specs=spec(VMEM),
        scratch_shapes=[
            pltpu.VMEM((N_TILE, BODY, TILE), BF16),
            pltpu.VMEM((SLOTS, 8, TILE), F32),
            pltpu.VMEM((SLOTS, TILE), F32),
            pltpu.SemaphoreType.DMA((N_TILE,)),
        ],
        compiler_params=PARAMS,
        cost_estimate=cost(3),
        name="source",
    )(me_stripe, shot_dose, shot_tile, shot_count, groups)

    for bit in (1, 2, 4):
        half = back.shape[0] // 2
        sent = lax.ppermute(back[half:], "stripe", [(i, i ^ bit) for i in range(N_STRIPE)])
        back = back[:half] + sent
    back = back.reshape(8, TILE)
    sent = lax.ppermute(back, "stripe", [(i, i ^ 8) for i in range(N_STRIPE)])
    back = back[:, 0:64] + sent[:, 64:128]

    def swapped(x, stripe_bit, tile_bit):
        pairs = [
            (a * N_TILE + b, (a ^ stripe_bit) * N_TILE + (b ^ tile_bit))
            for a in range(N_STRIPE)
            for b in range(N_TILE)
        ]
        return lax.ppermute(x, ("stripe", "tile"), pairs)

    back = back[:, 0:32] + swapped(back, 16, 0)[:, 32:64] + swapped(back, 0, 4)[:, 0:32] + swapped(back, 16, 4)[:, 32:64]
    back, got = lax.optimization_barrier((back, got))
    back = back + swapped(back, 0, 1)
    back_got = swapped(back, 0, 3)

    pattern, left, right, info, tiles = pl.pallas_call(
        deposit_kernel,
        out_shape=(
            array((EXT_ROWS, COLS), BF16),
            array((HALO, STRIP), BF16),
            array((HALO, STRIP), BF16),
            array((N_TILE, TILE), F32),
            array((N_TILE, TILE), jnp.int32),
        ),
        in_specs=[spec(VMEM)],
        out_specs=(spec(VMEM),) * 5,
        scratch_shapes=[
            pltpu.VMEM((ROWS, COLS), F32),
            pltpu.SMEM((N_TILE, TILE), F32),
            pltpu.SMEM((N_TILE, TILE), jnp.int32),
            pltpu.SemaphoreType.DMA((2,)),
        ],
        compiler_params=PARAMS,
        cost_estimate=cost(2.5),
        name="deposit",
    )(got)

    ring_up = [(i, (i + 1) % N_STRIPE) for i in range(N_STRIPE)]
    before = lax.ppermute(right, "stripe", ring_up)

    slots = array((SLOTS, TILE), F32)
    results = (
        array((ROWS, COLS), F32),
        slots,
        slots,
        slots,
        array((SLOTS, TILE), jnp.int32),
    )
    scratch = [
        pltpu.VMEM((2, ROWS, COLS), BF16),
        pltpu.VMEM((SLOTS, 8, TILE), F32),
        pltpu.VMEM((SLOTS, 8, TILE), F32),
        pltpu.SMEM((N_TILE, TILE), F32),
        pltpu.SMEM((N_TILE, TILE), jnp.int32),
        pltpu.SemaphoreType.DMA((2,)),
    ]
    *early, left = pl.pallas_call(
        early_kernel,
        out_shape=results + (array((HALO, STRIP), BF16),),
        in_specs=[spec(VMEM)] * 7,
        out_specs=(spec(VMEM),) * (N_MIDDLE + 1),
        scratch_shapes=scratch,
        compiler_params=PARAMS,
        cost_estimate=cost(4),
        name="early",
    )(got, pattern, info, tiles, table, left, back)
    after = lax.ppermute(left, "stripe", [(j, i) for i, j in ring_up])
    local, own_num, sums, slot_dose, slot_tile = pl.pallas_call(
        late_kernel,
        out_shape=results,
        in_specs=[spec(VMEM)] * (5 + N_MIDDLE),
        out_specs=(spec(VMEM),) * N_MIDDLE,
        scratch_shapes=scratch,
        input_output_aliases={5 + n: n for n in range(N_MIDDLE)},
        compiler_params=PARAMS,
        cost_estimate=cost(0),
        name="late",
    )(got, pattern, info, tiles, table, *early)

    energy, new_dose, backscatter = pl.pallas_call(
        forward_kernel,
        out_shape=(
            array((ROWS, COLS), F32),
            array((1, SLOTS), F32),
            array((TC, TR), F32),
        ),
        in_specs=[spec(VMEM)] * 13,
        out_specs=(spec(HBM), spec(VMEM), spec(VMEM)),
        scratch_shapes=[
            pltpu.VMEM((TR * 2 * HALO, 2 * TILE), BF16),
            pltpu.VMEM((ROWS, TILE), BF16),
            pltpu.VMEM((ROWS, TILE), BF16),
            pltpu.VMEM((ROWS, TILE), F32),
            pltpu.VMEM((ROWS, TILE), F32),
            pltpu.VMEM((ROWS, COLS), F32),
            pltpu.VMEM((SLOTS, 8, TILE), F32),
            pltpu.SMEM((N_TILE, TILE), F32),
            pltpu.SMEM((N_TILE, TILE), jnp.int32),
            pltpu.SemaphoreType.DMA((2,)),
            pltpu.SemaphoreType.DMA((TR,)),
        ],
        compiler_params=PARAMS,
        cost_estimate=cost(3),
        name="forward",
    )(back_got, before, after, back, local, own_num, sums, slot_dose, slot_tile, table, info, tiles, got)
    return energy, backscatter.T, new_dose.reshape(SLOTS)


def solution(mesh):
    in_specs = (
        P(("stripe", "tile"), None, None),
        P(("stripe", "tile")),
        P(("stripe", "tile")),
        P(("stripe", "tile")),
    )
    out_specs = (P("tile", "stripe"), P("tile", "stripe"), P(("stripe", "tile")))
    return jax.shard_map(
        on_device, mesh=mesh, in_specs=in_specs, out_specs=out_specs, check_vma=False
    )
```

```python
import jax
import jax.numpy as jnp
import numpy as np
import ml_dtypes
from jax import lax
from jax.experimental import pallas as pl
from jax.experimental.pallas import tpu as pltpu
from jax.sharding import PartitionSpec as P

TILE = 128
TR = 8
TC = 4
HALO = 16
CAP = 8
N_STRIPE = 32
RUN = 16
N_TILE = 8
SLOTS = N_TILE * CAP
ROWS = TR * TILE
COLS = TC * TILE
ROW_BLOCK = 256
COL_BLOCK = 256
EXT_ROWS = ROWS + 2 * HALO
STRIP = ROWS + TILE
BODY = CAP * TILE
EDGE = 2 * TC * HALO
INFO = BODY + EDGE
MESSAGE = INFO + HALO
N_ROW_BLOCKS = ROWS // ROW_BLOCK

ETA_BACK = 0.7
DILATED_WEIGHT = 0.5
TARGET_DOSE = 1.0
NARROW_SIGMA = 2.0
DILATED_SIGMA = 4.0
NXC = N_STRIPE * TC
NYC = N_TILE * TR
LOOP_SPREAD = NXC / 2.0
BAND_SPREAD = NYC / 5.0

F32 = jnp.float32
BF16 = jnp.bfloat16


def taps():
    offset = np.arange(-HALO, HALO + 1).astype(np.float32)
    narrow = np.exp(-offset * offset / np.float32(2.0 * NARROW_SIGMA**2))
    dilated = np.exp(-offset * offset / np.float32(8.0 * DILATED_SIGMA**2))
    dilated = np.where(np.arange(-HALO, HALO + 1) % 2 == 0, dilated, np.float32(0))
    narrow = (narrow / narrow.sum(dtype=np.float32)).astype(ml_dtypes.bfloat16)
    dilated = (dilated / dilated.sum(dtype=np.float32)).astype(ml_dtypes.bfloat16)
    return narrow.astype(np.float32), dilated.astype(np.float32)


def by_offset(table, offset):
    inside = np.abs(offset) <= HALO
    return np.where(inside, table[np.clip(offset + HALO, 0, 2 * HALO)], np.float32(0))


OWN_NARROW, OWN_DILATED, SIDE_LEFT, SIDE_RIGHT, STRIPS, ROWS_PASS = 0, 256, 512, 640, 768, 1024
N_MIDDLE = 5
TABLE_ROWS = 1280
ROWS_WINDOW = TILE + 2 * HALO


def tables():
    narrow, dilated = taps()
    half = np.float32(DILATED_WEIGHT)
    table = np.zeros((TABLE_ROWS, COL_BLOCK), np.float32)
    q = np.arange(COL_BLOCK)[None, :]
    own = np.arange(COL_BLOCK)[:, None] - q
    table[OWN_NARROW : OWN_NARROW + COL_BLOCK] = by_offset(narrow, own)
    table[OWN_DILATED : OWN_DILATED + COL_BLOCK] = half * by_offset(dilated, own)
    n = np.arange(HALO)[:, None]
    before, after = n - HALO - q, n + COL_BLOCK - q
    left, right = table[SIDE_LEFT : SIDE_LEFT + TILE], table[SIDE_RIGHT : SIDE_RIGHT + TILE]
    left[0:HALO] = by_offset(narrow, after)
    left[HALO : 2 * HALO] = half * by_offset(dilated, after)
    left[2 * HALO : 3 * HALO] = by_offset(narrow, before)
    left[3 * HALO : 4 * HALO] = half * by_offset(dilated, before)
    right[TILE - HALO : TILE] = by_offset(narrow, before)
    right[0:HALO] = half * by_offset(dilated, before)
    right[2 * HALO : 3 * HALO] = by_offset(narrow, after)
    right[3 * HALO : 4 * HALO] = half * by_offset(dilated, after)
    j = np.arange(2 * TILE)[:, None]
    y = np.arange(TILE)[None, :]
    table[STRIPS : STRIPS + 2 * TILE, 0:TILE] = by_offset(narrow, j - HALO - y)
    table[STRIPS : STRIPS + 2 * TILE, TILE:] = by_offset(dilated, j - HALO - y)
    y = np.arange(TILE)[:, None]
    j = np.arange(ROWS_WINDOW)[None, :]
    table[ROWS_PASS : ROWS_PASS + TILE, 0:ROWS_WINDOW] = by_offset(narrow, j - HALO - y)
    table[ROWS_PASS + TILE : ROWS_PASS + 2 * TILE, 0:ROWS_WINDOW] = by_offset(dilated, j - HALO - y)
    return table.astype(ml_dtypes.bfloat16)


def back_norm():
    m = np.arange(NXC)
    m = np.minimum(m, NXC - m).astype(np.float64)
    sx = np.exp(-m * m / (2.0 * LOOP_SPREAD**2)).sum()
    o = np.arange(-(NYC - 1), NYC).astype(np.float64)
    sy = np.exp(-o * o / (2.0 * BAND_SPREAD**2)).sum()
    return float(sx * sy)


def iota(shape, dim):
    return lax.broadcasted_iota(jnp.int32, shape, dim)


def splat_low(value, shape):
    return jnp.full(shape, value, F32).astype(BF16).astype(F32)


def pack_kernel(dose_hbm, tile_hbm, count_hbm, groups, out, buf, edge, tail, dose_ref, tile_ref, count_ref, in_sems, out_sems, slot_sems):
    reads, writes = [], []
    for d in range(N_TILE):
        reads.append(pltpu.make_async_copy(groups.at[d], buf.at[d], in_sems.at[d]))
        writes.append(pltpu.make_async_copy(buf.at[d], out.at[d, pl.ds(0, BODY)], out_sems.at[d]))
    scalars = []
    for n, (source, target) in enumerate(((dose_hbm, dose_ref), (tile_hbm, tile_ref), (count_hbm, count_ref))):
        scalars.append(pltpu.make_async_copy(source, target, slot_sems.at[n]))
    for c in reads[:1] + scalars + reads[1:]:
        c.start()
    edge[...] = jnp.zeros_like(edge)
    row = iota((8, TILE), 0)
    lane = iota((8, TILE), 1)
    for c in scalars:
        c.wait()

    def add_info(s, acc):
        d = s >> 3
        k = s & (CAP - 1)
        dose = jnp.where(k < count_ref[d], dose_ref[s], 0.0)
        tile = jnp.full((8, TILE), tile_ref[s], jnp.int32).astype(F32)
        acc = jnp.where((row == d) & (lane == k), dose, acc)
        return jnp.where((row == d) & (lane == k + CAP), tile, acc)

    info = lax.fori_loop(0, SLOTS, add_info, jnp.zeros((8, TILE), F32), unroll=8)
    high = info.astype(BF16).astype(F32)
    middle = (info - high).astype(BF16).astype(F32)
    lowest = info - high - middle
    row = iota((HALO, TILE), 0)
    for d in range(N_TILE):
        at = slice(d, d + 1)
        rows = jnp.where(row == 0, high[at], jnp.where(row == 1, middle[at], jnp.where(row == 2, lowest[at], 0.0)))
        tail[d, EDGE:] = rows.astype(BF16)
    half = EDGE // 2
    blank = jnp.zeros((half, TILE), BF16)

    def send_tail(d):
        above = edge[d - 1, 1].reshape(half, TILE).astype(BF16) if d > 0 else blank
        below = edge[d + 1, 0].reshape(half, TILE).astype(BF16) if d < N_TILE - 1 else blank
        tail[d, 0:half] = above
        tail[d, half:EDGE] = below
        writes.append(
            pltpu.make_async_copy(tail.at[d], out.at[d, pl.ds(BODY, MESSAGE - BODY)], out_sems.at[N_TILE + d])
        )
        writes[-1].start()

    for d in range(N_TILE):
        reads[d].wait()
        writes[d].start()

        def add_edges(k, carry, d=d):
            s = d * CAP + k
            t = tile_ref[s]
            live = k < count_ref[d]
            c = t & (TC - 1)
            first = pl.multiple_of(k * TILE, TILE)

            at_bottom = t >= TC * (TR - 1)

            @pl.when(live & ((t < TC) | at_bottom))
            def _():
                side = jnp.where(at_bottom, 1, 0)
                at = pl.multiple_of(first + side * (TILE - HALO), HALO)
                x = buf[d, pl.ds(at, HALO), :].astype(F32)
                edge[d, side, c] += splat_low(dose_ref[s], (HALO, TILE)) * x

            return carry

        lax.fori_loop(0, CAP, add_edges, 0, unroll=True)
        if d > 0:
            send_tail(d - 1)
    send_tail(N_TILE - 1)
    for c in writes:
        c.wait()


def source_kernel(me_ref, dose_ref, tile_ref, count_ref, groups, out, buf, part, total, sems):
    me = me_ref[0]
    copies = [pltpu.make_async_copy(groups.at[d], buf.at[d], sems.at[d]) for d in range(N_TILE)]
    for c in copies:
        c.start()
    for d in range(N_TILE):
        copies[d].wait()
        for k in range(CAP):
            x = buf[d, k * TILE : (k + 1) * TILE].astype(F32)
            part[d * CAP + k] = jnp.sum(x.reshape(TILE // 8, 8, TILE), axis=0)
    sums = jnp.sum(jnp.sum(part[...], axis=1), axis=1, keepdims=True) * (1.0 / (TILE * TILE))
    total[...] = jnp.broadcast_to(sums, (SLOTS, TILE))
    row = iota((8, TILE), 0)
    lane = iota((8, TILE), 1)
    target_row = row * TR + ((lane & 31) >> 2)
    column = lane >> 5

    def add_slot(s, acc):
        d = s >> 3
        t = tile_ref[s]
        dose = jnp.where((s & (CAP - 1)) < count_ref[d], dose_ref[s], 0.0)
        value = jnp.broadcast_to(total[pl.ds(s, 1), :], (8, TILE))
        gap = (target_row - (d * TR + (t >> 2))).astype(F32)
        across = jnp.exp(gap * gap * (-1.0 / (2.0 * BAND_SPREAD**2)))
        return acc + jnp.where(column == (t & (TC - 1)), across * (splat_low(dose, (8, TILE)) * value), 0.0)

    acc = lax.fori_loop(0, SLOTS, add_slot, jnp.zeros((8, TILE), F32), unroll=8)
    for i in range(8):
        low_bits = ((i >> 2) & 1) + (i & 2) + 4 * (i & 1)
        result = jnp.zeros((8, TILE), F32)
        for g in range(4):
            r = low_bits + 8 * (g >> 1) + 16 * (g & 1)
            gap = jnp.abs(me * TC + column - ((me ^ r) * TC + (lane & (TC - 1))))
            gap = jnp.minimum(gap, NXC - gap).astype(F32)
            x = acc * jnp.exp(gap * gap * (-1.0 / (2.0 * LOOP_SPREAD**2)))
            x = x + pltpu.roll(x, 64, 1)
            x = x + pltpu.roll(x, 32, 1)
            result = jnp.where(column == g, x, result)
        out[i] = result


def select_rows(first):
    r = iota((HALO, TILE), 0)
    c = iota((HALO, TILE), 1)
    return jnp.where(c == r + first, 1.0, 0.0).astype(BF16)


def dot_nt(a, b):
    return lax.dot_general(a, b, (((1,), (1,)), ((), ())), preferred_element_type=F32)


def tile_at(t):
    at_row = pl.ds(pl.multiple_of((t >> 2) * TILE, TILE), TILE)
    at_col = pl.ds(pl.multiple_of((t & (TC - 1)) * TILE, TILE), TILE)
    return at_row, at_col


def decode(got):
    rows = []
    for b in range(N_TILE):
        x = got[b, INFO:MESSAGE].astype(F32)
        rows.append(x[0:1] + x[1:2] + x[2:3])
    return jnp.concatenate(rows, 0)


def slot_copies(info, tiles, dose_s, tile_s, sems):
    return (
        pltpu.make_async_copy(info, dose_s, sems.at[0]),
        pltpu.make_async_copy(tiles, tile_s, sems.at[1]),
    )


def deposit_kernel(got, ext, left, right, info, tiles, acc, dose_s, tile_s, sems):
    values = decode(got)
    info[...] = values
    tiles[...] = values.astype(jnp.int32)
    to_slots = slot_copies(info, tiles, dose_s, tile_s, sems)
    for c in to_slots:
        c.start()
    acc[...] = jnp.zeros_like(acc)
    for side in range(2):
        at = slice(0, HALO) if side == 0 else slice(EXT_ROWS - HALO, EXT_ROWS)
        for c in range(TC):
            first = BODY + (side * TC + c) * HALO
            x = got[0, first : first + HALO].astype(F32)
            for b in range(1, N_TILE):
                x = x + got[b, first : first + HALO].astype(F32)
            ext[at, c * TILE : (c + 1) * TILE] = x.astype(BF16)
    for c in to_slots:
        c.wait()

    def add_group(b, carry):
        for k in range(CAP):
            dose = dose_s[b, k]

            x = got[b, k * TILE : (k + 1) * TILE].astype(F32)
            acc[tile_at(tile_s[b, CAP + k])] += splat_low(dose, (TILE, TILE)) * x

        return carry

    lax.fori_loop(0, N_TILE, add_group, 0)
    for j in range(N_ROW_BLOCKS):
        lo, hi = j * ROW_BLOCK, (j + 1) * ROW_BLOCK
        ext[HALO + lo : HALO + hi, :] = acc[lo:hi, :].astype(BF16)
    blank = jnp.zeros((HALO, STRIP - EXT_ROWS), BF16)
    for out, first, lane in ((left, 0, 0), (right, TILE - HALO, COLS - TILE)):
        strip = dot_nt(select_rows(first), ext[:, lane : lane + TILE]).astype(BF16)
        out[...] = jnp.concatenate([strip, blank], 1)


def first_of_run():
    return lax.rem(lax.axis_index("stripe"), RUN) == 0


def early_kernel(got, ext, info, tiles, table, left, _, *rest):
    left_out = rest[N_MIDDLE]
    left_out[...] = left[...]
    pl.when(first_of_run())(lambda: middle_kernel(got, ext, info, tiles, table, *rest[:N_MIDDLE], *rest[N_MIDDLE + 1 :]))


def late_kernel(got, ext, info, tiles, table, *rest):
    pl.when(~first_of_run())(lambda: middle_kernel(got, ext, info, tiles, table, *rest[N_MIDDLE:]))


def middle_kernel(
    got, ext, info, tiles, table,
    local, own_num, sums, slot_dose, slot_tile,
    passed, nums, part, dose_s, tile_s, slot_sems,
):
    to_slots = slot_copies(info, tiles, dose_s, tile_s, slot_sems)
    for c in to_slots:
        c.start()
    for i in range(TR):
        lo, hi = i * TILE, (i + 1) * TILE
        both = jnp.dot(
            table[ROWS_PASS : ROWS_PASS + 2 * TILE, 0:ROWS_WINDOW],
            ext[lo : lo + ROWS_WINDOW, :],
            preferred_element_type=F32,
        )
        passed[0, lo:hi] = both[0:TILE].astype(BF16)
        passed[1, lo:hi] = both[TILE:].astype(BF16)
    lanes = iota((ROW_BLOCK, TILE), 1)
    for j in range(N_ROW_BLOCKS):
        lo, hi = ROW_BLOCK * j, ROW_BLOCK * (j + 1)
        for half in range(COLS // COL_BLOCK):
            own = slice(half * COL_BLOCK, (half + 1) * COL_BLOCK)
            if half == 0:
                beside, keep, first = slice(COL_BLOCK, COL_BLOCK + TILE), lanes < HALO, SIDE_LEFT
            else:
                beside, keep, first = slice(COL_BLOCK - TILE, COL_BLOCK), lanes >= TILE - HALO, SIDE_RIGHT
            narrow = jnp.where(keep, passed[0, lo:hi, beside].astype(F32), 0.0)
            dilated = jnp.where(keep, passed[1, lo:hi, beside].astype(F32), 0.0)
            side = (narrow + pltpu.roll(dilated, HALO, 1)).astype(BF16)
            result = jnp.dot(passed[0, lo:hi, own], table[OWN_NARROW : OWN_NARROW + COL_BLOCK, :], preferred_element_type=F32)
            result += jnp.dot(passed[1, lo:hi, own], table[OWN_DILATED : OWN_DILATED + COL_BLOCK, :], preferred_element_type=F32)
            result += jnp.dot(side, table[first : first + TILE, :], preferred_element_type=F32)
            local[lo:hi, own] = result
    for c in to_slots:
        c.wait()

    def see_group(b, carry):
        for k in range(CAP):
            s = b * CAP + k
            dose = dose_s[b, k]
            slot_dose[pl.ds(s, 1), :] = jnp.full((1, TILE), dose, F32)
            slot_tile[pl.ds(s, 1), :] = jnp.full((1, TILE), tile_s[b, CAP + k], jnp.int32)

            x = got[b, k * TILE : (k + 1) * TILE].astype(F32)
            seen = local[tile_at(tile_s[b, CAP + k])] * x
            nums[s] = jnp.sum(seen.reshape(TILE // 8, 8, TILE), axis=0)
            part[s] = jnp.sum(x.reshape(TILE // 8, 8, TILE), axis=0)

        return carry

    lax.fori_loop(0, N_TILE, see_group, 0)
    for out, parts in ((own_num, nums), (sums, part)):
        total = jnp.sum(jnp.sum(parts[...], axis=1), axis=1, keepdims=True)
        out[...] = jnp.broadcast_to(total, (SLOTS, TILE))


def forward_kernel(
    back_got, before, after, back_own, local, own_num, sums, slot_dose, slot_tile, table, info, tiles, got,
    energy, new_dose, backscatter,
    windows, halo_left, halo_right, edges, final, nums, dose_s, tile_s, slot_sems, out_sems,
):
    me = lax.axis_index("tile")
    to_slots = slot_copies(info, tiles, dose_s, tile_s, slot_sems)
    for c in to_slots:
        c.start()
    lane = iota((8, TILE), 1)
    row = iota((8, TILE), 0)
    own = (back_own[...] + back_got[...]) * (1.0 / back_norm())
    own = jnp.sum(jnp.where(iota((8, 32), 0) == me, own, 0.0), axis=0, keepdims=True)
    own = jnp.broadcast_to(own, (8, 32))
    small_row, small_lane = iota((8, 32), 0), iota((8, 32), 1)
    terms = []
    for c in range(TC):
        at = small_lane == small_row * TC + c
        term = jnp.sum(jnp.where(at, own, 0.0), axis=1, keepdims=True)
        terms.append(jnp.broadcast_to(term, (8, TILE)))
        backscatter[c : c + 1, :] = jnp.sum(jnp.where(lane == row, terms[c], 0.0), axis=0, keepdims=True)[:, 0:TR]
    for i in range(TR):
        at = slice(TILE * i, TILE * (i + 2))
        windows[HALO * i : HALO * (i + 1), :] = before[:, at]
        windows[HALO * (TR + i) : HALO * (TR + i + 1), :] = after[:, at]
    strips = jnp.dot(windows[...], table[STRIPS : STRIPS + 2 * TILE, :], preferred_element_type=F32)
    blank = jnp.zeros((2 * HALO, TILE), F32)
    for side, halo in enumerate((halo_left, halo_right)):
        for i in range(TR):
            both = strips[HALO * (side * TR + i) : HALO * (side * TR + i + 1), :]
            stacked = jnp.concatenate([blank, both[:, 0:TILE], both[:, TILE:], blank, blank], 0)
            halo[TILE * i : TILE * (i + 1), :] = stacked.T.astype(BF16)
        first = SIDE_LEFT + side * TILE
        weights = table[first : first + TILE, side * TILE : (side + 1) * TILE]
        edges[side] = jnp.dot(halo[...], weights, preferred_element_type=F32)
    out_copies = []
    for p in range(TR):
        rows = slice(p * TILE, (p + 1) * TILE)
        for c in range(TC):
            at = slice(c * TILE, (c + 1) * TILE)
            x = local[rows, at] + ETA_BACK * terms[c][p : p + 1]
            if c == 0:
                x = x + edges[0, rows, :]
            if c == TC - 1:
                x = x + edges[1, rows, :]
            final[rows, at] = x
        if p % 2 == 1:
            at = pl.ds((p - 1) * TILE, 2 * TILE)
            out_copies.append(pltpu.make_async_copy(final.at[at], energy.at[at], out_sems.at[p]))
            out_copies[-1].start()
    for c in to_slots:
        c.wait()

    def see_group(b, carry):
        for k in range(CAP):
            s = b * CAP + k
            t = tile_s[b, CAP + k]
            live = dose_s[b, k] > 0.0
            column = t & (TC - 1)
            rows = pl.ds(pl.multiple_of((t >> 2) * TILE, TILE), TILE)
            nums[s] = jnp.zeros((8, TILE), F32)

            @pl.when(live & ((column == 0) | (column == TC - 1)))
            def _(k=k, s=s, rows=rows, side=column >> 1):
                x = got[b, k * TILE : (k + 1) * TILE].astype(F32) * edges[side, rows, :]
                nums[s] = jnp.sum(x.reshape(TILE // 8, 8, TILE), axis=0)

        return carry

    lax.fori_loop(0, N_TILE, see_group, 0)
    at_tile = slot_tile[:, 0:32] == iota((SLOTS, 32), 1)
    back = jnp.sum(jnp.where(at_tile, jnp.broadcast_to(own[0:1], (SLOTS, 32)), 0.0), axis=1, keepdims=True)
    num = jnp.sum(jnp.sum(nums[...], axis=1), axis=1, keepdims=True)
    total = sums[...]
    exposure = (own_num[...] + (num + (ETA_BACK * back) * total)) / total
    dose = slot_dose[...]
    corrected = jnp.where(dose > 0.0, dose * TARGET_DOSE / exposure, 0.0)
    at_slot = iota((SLOTS, TILE), 0) == iota((SLOTS, TILE), 1)
    new_dose[...] = jnp.sum(jnp.where(at_slot, corrected, 0.0), axis=0, keepdims=True)[:, 0:SLOTS]
    for copy in out_copies:
        copy.wait()


def spec(space):
    return pl.BlockSpec(memory_space=space)


VMEM, SMEM, HBM = pltpu.VMEM, pltpu.SMEM, pltpu.HBM
PACK_PARAMS = pltpu.CompilerParams(vmem_limit_bytes=64 * 2**20)
PARAMS = pltpu.CompilerParams(vmem_limit_bytes=24 * 2**20)


def cost(us):
    return pl.CostEstimate(flops=int(us * 1e9), bytes_accessed=int(us * 3e6), transcendentals=0)


def array(shape, dtype):
    return jax.ShapeDtypeStruct(shape, dtype)


def on_device(shot_blocks, shot_dose, shot_tile, shot_count):
    me_stripe = lax.axis_index("stripe").astype(jnp.int32).reshape(1)
    table = jnp.asarray(tables())
    groups = shot_blocks.reshape(N_TILE, BODY, TILE)

    message = pl.pallas_call(
        pack_kernel,
        out_shape=array((N_TILE, MESSAGE, TILE), BF16),
        in_specs=[spec(HBM)] * 4,
        out_specs=spec(HBM),
        scratch_shapes=[
            pltpu.VMEM((N_TILE, BODY, TILE), BF16),
            pltpu.VMEM((N_TILE, 2, TC, HALO, TILE), F32),
            pltpu.VMEM((N_TILE, MESSAGE - BODY, TILE), BF16),
            pltpu.SMEM((SLOTS,), F32),
            pltpu.SMEM((SLOTS,), jnp.int32),
            pltpu.SMEM((N_TILE,), jnp.int32),
            pltpu.SemaphoreType.DMA((N_TILE,)),
            pltpu.SemaphoreType.DMA((2 * N_TILE,)),
            pltpu.SemaphoreType.DMA((3,)),
        ],
        compiler_params=PACK_PARAMS,
        cost_estimate=cost(3.5),
        name="pack",
    )(shot_dose, shot_tile, shot_count, groups)
    got = lax.all_to_all(message, "tile", split_axis=0, concat_axis=0, tiled=True)

    back = pl.pallas_call(
        source_kernel,
        out_shape=array((8, 8, TILE), F32),
        in_specs=[spec(SMEM)] * 4 + [spec(HBM)],
        out_specs=spec(VMEM),
        scratch_shapes=[
            pltpu.VMEM((N_TILE, BODY, TILE), BF16),
            pltpu.VMEM((SLOTS, 8, TILE), F32),
            pltpu.VMEM((SLOTS, TILE), F32),
            pltpu.SemaphoreType.DMA((N_TILE,)),
        ],
        compiler_params=PARAMS,
        cost_estimate=cost(3),
        name="source",
    )(me_stripe, shot_dose, shot_tile, shot_count, groups)

    for bit in (1, 2, 4):
        half = back.shape[0] // 2
        sent = lax.ppermute(back[half:], "stripe", [(i, i ^ bit) for i in range(N_STRIPE)])
        back = back[:half] + sent
    back = back.reshape(8, TILE)
    sent = lax.ppermute(back, "stripe", [(i, i ^ 8) for i in range(N_STRIPE)])
    back = back[:, 0:64] + sent[:, 64:128]

    def swapped(x, stripe_bit, tile_bit):
        pairs = [
            (a * N_TILE + b, (a ^ stripe_bit) * N_TILE + (b ^ tile_bit))
            for a in range(N_STRIPE)
            for b in range(N_TILE)
        ]
        return lax.ppermute(x, ("stripe", "tile"), pairs)

    back = back[:, 0:32] + swapped(back, 16, 0)[:, 32:64] + swapped(back, 0, 4)[:, 0:32] + swapped(back, 16, 4)[:, 32:64]
    back, got = lax.optimization_barrier((back, got))
    back = back + swapped(back, 0, 1)
    back_got = swapped(back, 0, 3)

    pattern, left, right, info, tiles = pl.pallas_call(
        deposit_kernel,
        out_shape=(
            array((EXT_ROWS, COLS), BF16),
            array((HALO, STRIP), BF16),
            array((HALO, STRIP), BF16),
            array((N_TILE, TILE), F32),
            array((N_TILE, TILE), jnp.int32),
        ),
        in_specs=[spec(VMEM)],
        out_specs=(spec(VMEM),) * 5,
        scratch_shapes=[
            pltpu.VMEM((ROWS, COLS), F32),
            pltpu.SMEM((N_TILE, TILE), F32),
            pltpu.SMEM((N_TILE, TILE), jnp.int32),
            pltpu.SemaphoreType.DMA((2,)),
        ],
        compiler_params=PARAMS,
        cost_estimate=cost(2.5),
        name="deposit",
    )(got)

    ring_up = [(i, (i + 1) % N_STRIPE) for i in range(N_STRIPE)]
    before = lax.ppermute(right, "stripe", ring_up)

    slots = array((SLOTS, TILE), F32)
    results = (
        array((ROWS, COLS), F32),
        slots,
        slots,
        slots,
        array((SLOTS, TILE), jnp.int32),
    )
    scratch = [
        pltpu.VMEM((2, ROWS, COLS), BF16),
        pltpu.VMEM((SLOTS, 8, TILE), F32),
        pltpu.VMEM((SLOTS, 8, TILE), F32),
        pltpu.SMEM((N_TILE, TILE), F32),
        pltpu.SMEM((N_TILE, TILE), jnp.int32),
        pltpu.SemaphoreType.DMA((2,)),
    ]
    *early, left = pl.pallas_call(
        early_kernel,
        out_shape=results + (array((HALO, STRIP), BF16),),
        in_specs=[spec(VMEM)] * 7,
        out_specs=(spec(VMEM),) * (N_MIDDLE + 1),
        scratch_shapes=scratch,
        compiler_params=PARAMS,
        cost_estimate=cost(4),
        name="early",
    )(got, pattern, info, tiles, table, left, back)
    after = lax.ppermute(left, "stripe", [(j, i) for i, j in ring_up])
    local, own_num, sums, slot_dose, slot_tile = pl.pallas_call(
        late_kernel,
        out_shape=results,
        in_specs=[spec(VMEM)] * (5 + N_MIDDLE),
        out_specs=(spec(VMEM),) * N_MIDDLE,
        scratch_shapes=scratch,
        input_output_aliases={5 + n: n for n in range(N_MIDDLE)},
        compiler_params=PARAMS,
        cost_estimate=cost(0),
        name="late",
    )(got, pattern, info, tiles, table, *early)

    energy, new_dose, backscatter = pl.pallas_call(
        forward_kernel,
        out_shape=(
            array((ROWS, COLS), F32),
            array((1, SLOTS), F32),
            array((TC, TR), F32),
        ),
        in_specs=[spec(VMEM)] * 13,
        out_specs=(spec(HBM), spec(VMEM), spec(VMEM)),
        scratch_shapes=[
            pltpu.VMEM((TR * 2 * HALO, 2 * TILE), BF16),
            pltpu.VMEM((ROWS, TILE), BF16),
            pltpu.VMEM((ROWS, TILE), BF16),
            pltpu.VMEM((2, ROWS, TILE), F32),
            pltpu.VMEM((ROWS, COLS), F32),
            pltpu.VMEM((SLOTS, 8, TILE), F32),
            pltpu.SMEM((N_TILE, TILE), F32),
            pltpu.SMEM((N_TILE, TILE), jnp.int32),
            pltpu.SemaphoreType.DMA((2,)),
            pltpu.SemaphoreType.DMA((TR,)),
        ],
        compiler_params=PARAMS,
        cost_estimate=cost(3),
        name="forward",
    )(back_got, before, after, back, local, own_num, sums, slot_dose, slot_tile, table, info, tiles, got)
    return energy, backscatter.T, new_dose.reshape(SLOTS)


def solution(mesh):
    in_specs = (
        P(("stripe", "tile"), None, None),
        P(("stripe", "tile")),
        P(("stripe", "tile")),
        P(("stripe", "tile")),
    )
    out_specs = (P("tile", "stripe"), P("tile", "stripe"), P(("stripe", "tile")))
    return jax.shard_map(
        on_device, mesh=mesh, in_specs=in_specs, out_specs=out_specs, check_vma=False
    )
```
